32 devices in a mesh: tm: 4 (over z), lon: 8 (over y, x, core).
Axes of the slice: x: 2, y: 2, z: 4, core: 2. Of those that a mesh axis runs over, the one named last changes fastest.
Arguments:
- noise: bfloat16 [2, 256, 1024, 512], P(None, 'tm', 'lon'), may hold values from -6 to 6
- observed: float32 [256, 256, 1024], P('tm', 'lon'), may hold values from -6 to 6
- mask: int32 [256, 256, 1024], P('tm', 'lon'), may hold values from 0 to 1, as said below
- lat_factor: bfloat16 [256, 256], replicated, as said below
- lon_factor: bfloat16 [1024, 1024], P('lon'), as said below
- spectrum: float32 [257], replicated, may hold values from 0.1 to 4
Outputs:
- posterior: float32 [2, 256, 256, 1024], P(None, 'tm', 'lon')
- residual_next: float32 [2, 256, 256, 1024], P(None, 'tm', 'lon')
The draws below stay inside these ranges and needn't reach their ends.
Inputs may be any that keep to these rules, and one draw needn't show every extreme that they name: `mask`: 1 where the cell is observed, 0 elsewhere. `lat_factor`: lower triangular with a positive diagonal. `lon_factor`: lower triangular with a positive diagonal.
All inputs are finite; a program needn't handle non-finite values.
Results may differ from the reference program's by a relative error of at most 0.0026.
Values may be sent and summed in bfloat16 or wider, within the bound.
No kernel may reach another device: no remote copies, remote signals or barrier semaphores. Data moves between devices by JAX's collectives and lax.ppermute only.
A program may use at most 192 MiB of HBM per device.

```python
import math
import jax
import jax.numpy as jnp
from jax import lax

LON = 1024
LAT = 256
HOURS = 256
EMBED = 512


def lower_factor(key, order):
    entries = jax.random.normal(jax.random.fold_in(key, 11), (order, order), jnp.float32)
    diagonal = jax.random.uniform(jax.random.fold_in(key, 12), (order,), jnp.float32, 0.5, 1.0)
    row_index = lax.broadcasted_iota(jnp.int32, (order, order), 0)
    col_index = lax.broadcasted_iota(jnp.int32, (order, order), 1)
    scaling = jnp.sqrt(0.5 / (row_index + 1).astype(jnp.float32))
    lower = jnp.where(col_index < row_index, entries * scaling, 0.0)
    return lower + jnp.where(col_index == row_index, diagonal[:, None], 0.0)


def draw_lat_factor(key, part):
    return lower_factor(key, LAT).astype(jnp.bfloat16)


def draw_lon_factor(key, part):
    return lower_factor(key, LON).astype(jnp.bfloat16)


def draw_mask(key, part):
    ticket = jax.random.randint(jax.random.fold_in(key, 21), (HOURS, LAT, LON), 0, 1000)
    hour_index = lax.broadcasted_iota(jnp.int32, (HOURS, LAT, LON), 0)
    lat_index = lax.broadcasted_iota(jnp.int32, (HOURS, LAT, LON), 1)
    limit = 200 + 350 * hour_index // (HOURS - 1) + 350 * lat_index // (LAT - 1)
    return jnp.where(ticket < limit, 1, 0).astype(jnp.int32)


def block_scale(own_key, dims, shards, least, high):
    level, own = 1.0, jax.random.fold_in(own_key, 6)
    for dim, parts in shards:
        draws = jnp.exp(jax.random.uniform(jax.random.fold_in(own, dim), (parts,), jnp.float32, least / len(shards), high / len(shards)))
        level = level * jnp.repeat(draws, dims[dim] // parts).reshape([-1 if axis == dim else 1 for axis in range(len(dims))])
    return level


def centred(rng, extent, deviation, most, pieces=(), kind=jnp.bfloat16):
    values = jax.random.normal(rng, extent, jnp.float32) * deviation
    if len(pieces) > 0:
        values = block_scale(rng, extent, pieces, -0.22, 0.18) * values
    return jnp.clip(values, min=-most, max=most).astype(kind)


def setup_inputs(seed: int = 0) -> dict:
    splits = jax.random.split(jax.random.key(seed), 7)
    noise = centred(splits[0], (2, LAT, LON, EMBED), 1.0, 6.0, ((1, 4), (2, 8)))
    observed = centred(splits[1], (HOURS, LAT, LON), 1.0, 6.0, ((0, 4), (1, 8)), jnp.float32)
    mask = draw_mask(jax.random.fold_in(splits[6], 71), 0)
    lat_factor = draw_lat_factor(jax.random.fold_in(splits[6], 71), 0)
    lon_factor = draw_lon_factor(jax.random.fold_in(splits[6], 71), 0)
    spectrum = jnp.clip(jnp.exp(jax.random.uniform(splits[5], (HOURS + 1,), jnp.float32, math.log(0.1), math.log(4.0))), 0.1, 4.0)
    return {"noise": noise, "observed": observed, "mask": mask, "lat_factor": lat_factor, "lon_factor": lon_factor, "spectrum": spectrum}


PRECISE = lax.Precision.HIGHEST
NOISE_VAR = 0.25

def reference(noise, observed, mask, lat_factor, lon_factor, spectrum):
    periods = 2 * HOURS
    powers = jnp.concatenate([spectrum, spectrum[1:-1][::-1]])
    amplitude = jnp.sqrt(powers / periods)
    row_index = lax.broadcasted_iota(jnp.int32, (HOURS, periods), 0)
    col_index = lax.broadcasted_iota(jnp.int32, (HOURS, periods), 1)
    phase = (row_index * col_index % periods).astype(jnp.float32) * (2.0 * jnp.pi / periods)
    table_cos = (jnp.cos(phase) * amplitude).astype(jnp.bfloat16)
    table_sin = (jnp.sin(phase) * amplitude).astype(jnp.bfloat16)

    def transform_row(noise_row):
        real_part = jnp.dot(noise_row[0], table_cos.T, preferred_element_type=jnp.float32) + jnp.dot(noise_row[1], table_sin.T, preferred_element_type=jnp.float32)
        imag_part = jnp.dot(noise_row[1], table_cos.T, preferred_element_type=jnp.float32) - jnp.dot(noise_row[0], table_sin.T, preferred_element_type=jnp.float32)
        return jnp.stack([real_part, imag_part])
    hourly = lax.map(transform_row, jnp.moveaxis(noise, 1, 0))
    hourly = jnp.transpose(hourly, (1, 3, 0, 2))
    lat_whole = lat_factor.astype(jnp.float32)
    lon_whole = lon_factor.astype(jnp.float32)
    prior_draw = jnp.einsum('ab,shbo->shao', lat_whole, hourly, precision=PRECISE)
    prior_draw = jnp.einsum('op,shap->shao', lon_whole, prior_draw, precision=PRECISE)
    observed_mask = mask.astype(jnp.float32)
    residual = observed_mask * (observed[None] - prior_draw)
    lat_kernel = jnp.dot(lat_whole, lat_whole.T, precision=PRECISE)
    lon_kernel = jnp.dot(lon_whole, lon_whole.T, precision=PRECISE)
    correlation = jnp.real(jnp.fft.ifft(powers))[:HOURS]
    hour_index = jnp.arange(HOURS)
    lag_table = jnp.abs(hour_index[:, None] - hour_index[None, :])
    hour_kernel = correlation[lag_table]
    applied = jnp.einsum('op,shap->shao', lon_kernel, residual, precision=PRECISE)
    applied = jnp.einsum('ab,shbo->shao', lat_kernel, applied, precision=PRECISE)
    applied = jnp.einsum('hk,skao->shao', hour_kernel, applied, precision=PRECISE)
    operated = observed_mask * applied + NOISE_VAR * residual
    norm_sq = lax.optimization_barrier(jnp.sum(residual * residual, axis=(1, 2, 3)))
    bending = lax.optimization_barrier(jnp.sum(residual * operated, axis=(1, 2, 3)))
    step_size = (norm_sq / bending)[:, None, None, None]
    return (prior_draw + step_size * applied, residual - step_size * operated)
```

```python
import functools
import jax
import jax.numpy as jnp
from jax import lax
from jax.experimental import pallas as pl
from jax.experimental.pallas import tpu as pltpu
from jax.sharding import PartitionSpec as P

F32, BF16, I16, I32 = jnp.float32, jnp.bfloat16, jnp.int16, jnp.int32
EXACT, HIGH = lax.Precision.HIGHEST, lax.Precision.HIGH
NOISE_VAR = 0.25
SPECTRUM_MAX = 4.0
HOURLY_MAX = 400.0
STEPS = 1024.0
LEAST = -18.0
CODE_MAX = 2.0**13.5
GROUP = 16
VMEM = 52 * 1024 * 1024


def angle_tables(row_count, col_count, period):
    row_index = lax.broadcasted_iota(I32, (row_count, col_count), 0)
    col_index = lax.broadcasted_iota(I32, (row_count, col_count), 1)
    phase = (row_index * col_index % period).astype(F32) * (2.0 * jnp.pi / period)
    return (jnp.cos(phase), jnp.sin(phase))


def encode(x):
    size = jnp.maximum(jnp.abs(x), 2.0**LEAST)
    code = (jnp.log(size) * (STEPS / 0.6931471805599453) + (0.5 - STEPS * LEAST)).astype(I32)
    return jnp.where(x < 0, -code, code).astype(I16)


def decode(code):
    wide = code.astype(I32)
    size = jnp.exp2(jnp.abs(wide).astype(F32) * (1.0 / STEPS) + LEAST)
    size = jnp.where(wide == 0, 0.0, size)
    return jnp.where(wide < 0, -size, size)


def dot(a, b):
    return jnp.dot(a, b, preferred_element_type=F32)


def dot_rows(a, b):
    return lax.dot_general(a, b, (((1,), (1,)), ((), ())), preferred_element_type=F32)


def two_part_dot(a, b):
    top = a.astype(BF16)
    rest = (a - top.astype(F32)).astype(BF16)
    return dot(top, b) + dot(rest, b)


def fold(x):
    rows, cols = x.shape
    x = jnp.sum(x.reshape(rows // 8, 8, cols), axis=0)
    total = x[:, :128]
    for start in range(128, cols, 128):
        total = total + x[:, start : start + 128]
    return total


def call(body, name, grid, out_shape, in_specs, out_specs, flops, moved, scratch=(), aliases={}):
    return pl.pallas_call(
        body,
        name=name,
        grid=(grid,),
        out_shape=out_shape,
        in_specs=in_specs,
        out_specs=out_specs,
        scratch_shapes=list(scratch),
        input_output_aliases=aliases,
        compiler_params=pltpu.CompilerParams(vmem_limit_bytes=VMEM),
        cost_estimate=pl.CostEstimate(flops=flops, bytes_accessed=moved, transcendentals=0),
    )


def whole_spec(shape):
    return pl.BlockSpec(shape, lambda i: (0,) * len(shape))


SCALARS = pl.BlockSpec(memory_space=pltpu.SMEM)


def struct(shape, kind):
    return jax.ShapeDtypeStruct(shape, kind)


class Kernels:
    def __init__(self, zs, qs, hour_local, lat_local, lat_rows, lon_local):
        self.zs, self.qs = zs, qs
        self.hl, self.al, self.lr, self.ol = hour_local, lat_local, lat_rows, lon_local
        self.hours, self.lats, self.lons = zs * hour_local, zs * lat_local, qs * lon_local
        self.cells = hour_local * lat_rows * self.lons

    def parts_specs(self):
        return [pl.BlockSpec((GROUP, self.lr, self.ol), lambda i: (i, 0, 0))] * self.qs

    def parts_shape(self, kind):
        return [struct((self.hl, self.lr, self.ol), kind)] * self.qs

    def grid_spec(self):
        return pl.BlockSpec((GROUP, self.lr, self.lons), lambda i: (i, 0, 0))

    def hourly(self, noise, tables):
        zs, hl, al, ol, hours = self.zs, self.hl, self.al, self.ol, self.hours
        periods = noise.shape[3]

        def body(noise_ref, table_ref, out_ref, turned):
            for start in range(0, GROUP, 4):
                part = noise_ref[:, start : start + 4].reshape(2, 4 * ol, periods)
                total = dot_rows(table_ref[0], part[0]) + dot_rows(table_ref[1], part[1])
                for k in range(4):
                    turned[pl.ds(start + k, hours, stride=GROUP), :] = total[:, k * ol : (k + 1) * ol]
            out_ref[...] = turned[...].reshape(zs, hl, GROUP, ol).astype(BF16)

        return call(
            body, "hourly", al // GROUP, struct((zs, hl, al, ol), BF16),
            [pl.BlockSpec((2, GROUP, ol, periods), lambda i: (0, i, 0, 0)), whole_spec(tables.shape)],
            pl.BlockSpec((zs, hl, GROUP, ol), lambda i: (0, 0, i, 0)),
            4 * hours * periods * al * ol, 2 * noise.size + 2 * hours * al * ol,
            [pltpu.VMEM((hours * GROUP, ol), F32)],
        )(noise, tables)

    def lat_up(self, g, lat, gain):
        zs, qs, hl, lr, ol, lats = self.zs, self.qs, self.hl, self.lr, self.ol, self.lats

        def body(gain_ref, g_ref, lat_ref, *outs):
            for start in range(0, GROUP, 4):
                part = [g_ref[:, start + k].reshape(lats, ol) for k in range(4)]
                total = dot(lat_ref[...], jnp.concatenate(part, axis=1))
                code = encode(total * gain_ref[0])
                for k in range(4):
                    for d in range(qs):
                        outs[d][start + k] = code[d * lr : (d + 1) * lr, k * ol : (k + 1) * ol]

        return call(
            body, "lat_up", hl // GROUP, self.parts_shape(I16),
            [SCALARS, pl.BlockSpec((zs, GROUP, self.al, ol), lambda i: (0, i, 0, 0)), whole_spec(lat.shape)],
            self.parts_specs(), 2 * self.cells * lats, 4 * self.cells,
        )(gain.reshape(1), g, lat)

    def residual(self, parts, back, lon_up, lon_down, observed, mask):
        qs, hl, lr, ol, lons = self.qs, self.hl, self.lr, self.ol, self.lons
        rows = GROUP * lr

        def body(back_ref, *refs):
            codes, (up_ref, down_ref, observed_ref, mask_ref), outs = refs[:qs], refs[qs : qs + 4], refs[qs + 4 :]
            prior_ref, norm_ref, sent = outs[0], outs[1], outs[2:]
            x = jnp.concatenate([decode(c[...].reshape(rows, ol)) for c in codes], axis=1)
            prior = two_part_dot(x, up_ref[...]) * back_ref[0]
            prior_ref[...] = prior.reshape(GROUP, lr, lons)
            seen = mask_ref[...].reshape(rows, lons).astype(F32)
            resid = seen * (observed_ref[...].reshape(rows, lons) - prior)

            @pl.when(pl.program_id(0) == 0)
            def _():
                norm_ref[...] = jnp.zeros_like(norm_ref)

            norm_ref[...] += fold(resid * resid)
            v = two_part_dot(resid, down_ref[...]).astype(BF16)
            for d in range(qs):
                sent[d][...] = v[:, d * ol : (d + 1) * ol].reshape(GROUP, lr, ol)

        out = call(
            body, "residual", hl // GROUP,
            [struct((hl, lr, lons), F32), struct((8, 128), F32)] + self.parts_shape(BF16),
            [SCALARS] + self.parts_specs() + [whole_spec(lon_up.shape)] * 2 + [self.grid_spec()] * 2,
            [self.grid_spec(), whole_spec((8, 128))] + self.parts_specs(),
            8 * self.cells * lons, 16 * self.cells,
        )(back.reshape(1), *parts, lon_up, lon_down, observed, mask)
        return out[0], jnp.sum(out[1]), out[2:]

    def lat_down(self, parts, lat_t):
        zs, qs, hl, al, lr, ol, lats = self.zs, self.qs, self.hl, self.al, self.lr, self.ol, self.lats

        def body(*refs):
            sent, (lat_ref, out_ref, turned) = refs[:qs], refs[qs:]
            for start in range(0, GROUP, 4):
                part = [jnp.concatenate([s[start + k] for s in sent], axis=0) for k in range(4)]
                total = dot(lat_ref[...], jnp.concatenate(part, axis=1))
                for k in range(4):
                    turned[pl.ds(start + k, lats, stride=GROUP), :] = total[:, k * ol : (k + 1) * ol]
            out_ref[...] = turned[...].reshape(zs, al, GROUP, ol).astype(BF16)

        return call(
            body, "lat_down", hl // GROUP, struct((zs, al, hl, ol), BF16),
            self.parts_specs() + [whole_spec(lat_t.shape)],
            pl.BlockSpec((zs, al, GROUP, ol), lambda i: (0, 0, i, 0)),
            2 * self.cells * lats, 4 * self.cells,
            [pltpu.VMEM((lats * GROUP, ol), F32)],
        )(*parts, lat_t)

    def over_hours(self, x, kern):
        zs, hl, al, ol, hours = self.zs, self.hl, self.al, self.ol, self.hours

        def body(x_ref, kern_ref, out_ref, bend_ref, turned):
            @pl.when(pl.program_id(0) == 0)
            def _():
                bend_ref[...] = jnp.zeros_like(bend_ref)

            for start in range(0, GROUP, 4):
                part = [x_ref[:, start + k].reshape(hours, ol) for k in range(4)]
                part = jnp.concatenate(part, axis=1)
                total = dot(kern_ref[0], part) + dot(kern_ref[1], part)
                bend_ref[...] += fold(total * part.astype(F32))
                for k in range(4):
                    turned[pl.ds(start + k, hours, stride=GROUP), :] = total[:, k * ol : (k + 1) * ol]
            out_ref[...] = turned[...].reshape(zs, hl, GROUP, ol).astype(BF16)

        out = call(
            body, "over_hours", al // GROUP, [struct((zs, hl, al, ol), BF16), struct((8, 128), F32)],
            [pl.BlockSpec((zs, GROUP, hl, ol), lambda i: (0, i, 0, 0)), whole_spec(kern.shape)],
            [pl.BlockSpec((zs, hl, GROUP, ol), lambda i: (0, 0, i, 0)), whole_spec((8, 128))],
            4 * self.cells * hours, 4 * self.cells,
            [pltpu.VMEM((hours * GROUP, ol), F32)],
        )(x, kern)
        return out[0], jnp.sum(out[1])

    def finish(self, s, parts, back, step, lon_up, prior, observed, mask, earlier):
        qs, hl, lr, ol, lons = self.qs, self.hl, self.lr, self.ol, self.lons
        rows = GROUP * lr

        def body(scalar_ref, *refs):
            codes, (up_ref, prior_ref, observed_ref, mask_ref) = refs[:qs], refs[qs : qs + 4]
            posterior_ref, next_ref = refs[-2:]
            x = jnp.concatenate([decode(c[...].reshape(rows, ol)) for c in codes], axis=1)
            scaled = two_part_dot(x, up_ref[...]) * scalar_ref[0]
            prior = prior_ref[...].reshape(rows, lons)
            seen = mask_ref[...].reshape(rows, lons).astype(F32)
            resid = seen * (observed_ref[...].reshape(rows, lons) - prior)
            shape = (1, GROUP, lr, lons)
            posterior_ref[...] = (prior + scaled).reshape(shape)
            next_ref[...] = (resid - seen * scaled - scalar_ref[1] * resid).reshape(shape)

        full = struct((2, hl, lr, lons), F32)
        out_spec = pl.BlockSpec((1, GROUP, lr, lons), lambda i: (s, i, 0, 0))
        count = 1 + qs + 4
        return call(
            body, "finish", hl // GROUP, [full, full],
            [SCALARS] + self.parts_specs() + [whole_spec(lon_up.shape)] + [self.grid_spec()] * 3
            + [pl.BlockSpec(memory_space=pl.ANY)] * len(earlier),
            [out_spec, out_spec], 4 * self.cells * lons, 22 * self.cells,
            aliases={count + i: i for i in range(len(earlier))},
        )(jnp.stack([back * step, NOISE_VAR * step]), *parts, lon_up, prior, observed, mask, *earlier)


class Plain(Kernels):
    def hourly(self, noise, tables):
        h = jnp.einsum("cyxk,cjk->jyx", noise, tables, preferred_element_type=F32)
        return h.reshape(self.zs, self.hl, self.al, self.ol).astype(BF16)

    def lat_up(self, g, lat, gain):
        split = lat.reshape(self.qs, self.lr, self.zs, self.al)
        x = jnp.einsum("qlzy,zhyx->qhlx", split, g, preferred_element_type=F32)
        code = encode(x * gain)
        return [code[d] for d in range(self.qs)]

    def up(self, parts, lon_up):
        x = jnp.concatenate([decode(c) for c in parts], axis=2)
        return jnp.einsum("hlx,xo->hlo", x, lon_up.astype(F32), precision=HIGH)

    def residual(self, parts, back, lon_up, lon_down, observed, mask):
        prior = self.up(parts, lon_up) * back
        resid = mask.astype(F32) * (observed - prior)
        v = jnp.einsum("hlo,op->hlp", resid, lon_down.astype(F32), precision=HIGH).astype(BF16)
        return prior, jnp.sum(resid * resid), jnp.split(v, self.qs, axis=2)

    def lat_down(self, parts, lat_t):
        split = lat_t.reshape(self.zs, self.al, self.qs, self.lr)
        x = jnp.einsum("zyql,qhlx->zyhx", split, jnp.stack(parts), preferred_element_type=F32)
        return x.astype(BF16)

    def over_hours(self, x, kern):
        split = kern.astype(F32).sum(0).reshape(self.zs, self.hl, self.zs, self.hl)
        x = x.astype(F32)
        y = jnp.einsum("ghzk,zykx->ghyx", split, x, precision=HIGH)
        return y.astype(BF16), jnp.einsum("ghyx,gyhx->", y, x)

    def finish(self, s, parts, back, step, lon_up, prior, observed, mask, earlier):
        scaled = self.up(parts, lon_up) * (back * step)
        seen = mask.astype(F32)
        resid = seen * (observed - prior)
        pair = (prior + scaled, resid - seen * scaled - NOISE_VAR * step * resid)
        if not earlier:
            return pair
        return tuple(jnp.stack([a, b]) for a, b in zip(earlier, pair))


def swap_tm(x):
    return lax.all_to_all(x, "tm", split_axis=0, concat_axis=0, tiled=True)


def swap_lon(parts):
    count = len(parts)
    return [parts[0]] + [
        lax.ppermute(parts[d], "lon", [(i, i ^ d) for i in range(count)]) for d in range(1, count)
    ]


def largest_norm(factor, axis):
    return jnp.sqrt(jnp.max(jnp.sum(jnp.square(factor.astype(F32)), axis=axis)))


def shards(noise, observed, mask, lat_factor, lon_factor, spectrum):
    _, lat_local, lon_local, periods = noise.shape
    hour_local, lat_rows, lon_count = observed.shape
    hours = periods // 2
    zs, qs = hours // hour_local, lon_count // lon_local
    lat_count = zs * lat_local
    fits = lon_local % 128 == 0 and lat_rows % 16 == 0
    fits = fits and lat_local % GROUP == 0 and hour_local % GROUP == 0
    stages = (Kernels if fits else Plain)(zs, qs, hour_local, lat_local, lat_rows, lon_local)

    powers = jnp.concatenate([spectrum, spectrum[1:-1][::-1]])
    amplitude = jnp.sqrt(powers / periods)
    cosine_tab, sine_tab = angle_tables(hours, periods, periods)
    table_cos = (cosine_tab * amplitude).astype(BF16)
    table_sin = (sine_tab * amplitude).astype(BF16)
    tables = (jnp.stack([table_cos, table_sin]), jnp.stack([-table_sin, table_cos]))

    def hour_kernel():
        scaled = powers / periods
        kern = jnp.dot(cosine_tab * scaled, cosine_tab.T, precision=EXACT) + jnp.dot(
            sine_tab * scaled, sine_tab.T, precision=EXACT
        )
        top = lax.reduce_precision(kern, 8, 7)
        return jnp.stack([top.astype(BF16), (kern - top).astype(BF16)])

    arrived = [swap_tm(stages.hourly(noise, table)) for table in tables]
    kern = hour_kernel()
    order = lax.axis_index("lon") ^ jnp.arange(qs)
    lon = lax.all_gather(lon_factor, "lon", axis=0, tiled=True).reshape(lon_count, qs, lon_local)
    lon_down = jnp.take(lon, order, axis=1).reshape(lon_count, lon_count)
    lon_up = lon_down.T
    lat = jnp.take(lat_factor.reshape(qs, lat_rows, lat_count), order, axis=0)
    lat = lat.reshape(lat_count, lat_count)
    lat_t = lat.T
    lat_row_norm = largest_norm(lat_factor, 1)
    lon_col_norm = largest_norm(lon_down, 0)
    lat_norm = jnp.sqrt(jnp.sum(jnp.square(lat_factor.astype(F32))))
    first_gain = CODE_MAX / jnp.maximum(lat_row_norm * (lat_count**0.5 * HOURLY_MAX), 1e-30)

    earlier = ()
    for s in range(2):
        parts = swap_lon(stages.lat_up(arrived[s], lat, first_gain))
        prior, norm_sq, parts = stages.residual(parts, 1.0 / first_gain, lon_up, lon_down, observed, mask)
        x = swap_tm(stages.lat_down(swap_lon(parts), lat_t))
        y, bending = stages.over_hours(x, kern)
        y = swap_tm(y)
        if s == 1:
            bending, _ = lax.optimization_barrier((bending, step))
        norm_sq, bending = lax.psum((norm_sq, bending), ("tm", "lon"))
        step = norm_sq / (bending + NOISE_VAR * norm_sq)
        bound = SPECTRUM_MAX * lat_row_norm * lat_norm * lon_col_norm * jnp.sqrt(norm_sq)
        gain = CODE_MAX / jnp.maximum(bound, 1e-30)
        parts = swap_lon(stages.lat_up(y, lat, gain))
        earlier = stages.finish(s, parts, 1.0 / gain, step, lon_up, prior, observed, mask, earlier)
    return tuple(earlier)


def solution(mesh):
    return jax.shard_map(
        shards,
        mesh=mesh,
        in_specs=(
            P(None, "tm", "lon", None),
            P("tm", "lon", None),
            P("tm", "lon", None),
            P(),
            P("lon", None),
            P(),
        ),
        out_specs=(P(None, "tm", "lon", None), P(None, "tm", "lon", None)),
        check_vma=False,
    )
```

```python
import functools
import jax
import jax.numpy as jnp
from jax import lax
from jax.experimental import pallas as pl
from jax.experimental.pallas import tpu as pltpu
from jax.sharding import PartitionSpec as P

F32, BF16, I16, I32 = jnp.float32, jnp.bfloat16, jnp.int16, jnp.int32
EXACT, HIGH = lax.Precision.HIGHEST, lax.Precision.HIGH
NOISE_VAR = 0.25
SPECTRUM_MAX = 4.0
HOURLY_MAX = 400.0
STEPS = 1024.0
LEAST = -18.0
CODE_MAX = 2.0**13.5
GROUP = 16
HALVES = 2
VMEM = 52 * 1024 * 1024


def encode(x):
    size = jnp.maximum(jnp.abs(x), 2.0**LEAST)
    code = (jnp.log(size) * (STEPS / 0.6931471805599453) + (0.5 - STEPS * LEAST)).astype(I32)
    return jnp.where(x < 0, -code, code).astype(I16)


def decode(code):
    wide = code.astype(I32)
    size = jnp.exp2(jnp.abs(wide).astype(F32) * (1.0 / STEPS) + LEAST)
    size = jnp.where(wide == 0, 0.0, size)
    return jnp.where(wide < 0, -size, size)


def dot(a, b):
    return jnp.dot(a, b, preferred_element_type=F32)


def dot_rows(a, b):
    return lax.dot_general(a, b, (((1,), (1,)), ((), ())), preferred_element_type=F32)


def two_part_dot(a, b):
    top = a.astype(BF16)
    rest = (a - top.astype(F32)).astype(BF16)
    both = dot(jnp.concatenate([top, rest], axis=0), b)
    return both[: a.shape[0]] + both[a.shape[0] :]


def fold(x):
    rows, cols = x.shape
    x = jnp.sum(x.reshape(rows // 8, 8, cols), axis=0)
    total = x[:, :128]
    for start in range(128, cols, 128):
        total = total + x[:, start : start + 128]
    return total


def whole_spec(shape):
    return pl.BlockSpec(shape, lambda i: (0,) * len(shape))


SCALARS = pl.BlockSpec(memory_space=pltpu.SMEM)
ANYWHERE = pl.BlockSpec(memory_space=pl.ANY)


def struct(shape, kind):
    return jax.ShapeDtypeStruct(shape, kind)


class Kernels:
    def __init__(self, zs, qs, hour_local, lat_local, lat_rows, lon_local):
        self.zs, self.qs = zs, qs
        self.al, self.lr, self.ol = lat_local, lat_rows, lon_local
        self.hl = hour_local
        self.hp = hour_local // HALVES
        self.hours, self.lats, self.lons = zs * hour_local, zs * lat_local, qs * lon_local
        self.cells = self.hp * lat_rows * self.lons
        self.token = None

    def call(self, body, name, grid, out_shape, in_specs, out_specs, flops, moved, scratch=(), aliases={}):
        tokens = [] if self.token is None else [self.token]

        def run(*args):
            def whole(*refs):
                refs = list(refs)
                del refs[len(args) : len(args) + len(tokens)]
                place = len(args) + len(out_shape)
                token_ref = refs.pop(place)
                token_ref[...] = jnp.zeros_like(token_ref)
                body(*refs)

            out = pl.pallas_call(
                whole,
                name=name,
                grid=(grid,),
                out_shape=list(out_shape) + [struct((8, 128), F32)],
                in_specs=list(in_specs) + [ANYWHERE] * len(tokens),
                out_specs=list(out_specs) + [whole_spec((8, 128))],
                scratch_shapes=list(scratch),
                input_output_aliases=aliases,
                compiler_params=pltpu.CompilerParams(vmem_limit_bytes=VMEM),
                cost_estimate=pl.CostEstimate(flops=flops, bytes_accessed=moved, transcendentals=0),
            )(*args, *tokens)
            self.token = out[-1]
            return out[:-1]

        return run

    def after(self, x):
        return pl.pallas_call(
            lambda x_ref, token_ref, out_ref: None,
            name="after",
            out_shape=struct(x.shape, x.dtype),
            in_specs=[ANYWHERE, ANYWHERE],
            out_specs=ANYWHERE,
            input_output_aliases={0: 0},
            compiler_params=pltpu.CompilerParams(vmem_limit_bytes=VMEM),
            cost_estimate=pl.CostEstimate(flops=0, bytes_accessed=0, transcendentals=0),
        )(x, self.token)

    def parts_specs(self, group):
        return [pl.BlockSpec((group, self.lr, self.ol), lambda i: (i, 0, 0))] * self.qs

    def parts_shape(self, kind):
        return [struct((self.hp, self.lr, self.ol), kind)] * self.qs

    def grid_spec(self, group, c=None):
        start = 0 if c is None else c * (self.hp // group)
        return pl.BlockSpec((group, self.lr, self.lons), lambda i: (i + start, 0, 0))

    def hourly(self, noise, tables):
        zs, hp, al, ol, hours = self.zs, self.hp, self.al, self.ol, self.hours
        periods = noise.shape[3]

        def body(noise_ref, table_ref, *refs):
            outs, turned = refs[:HALVES], refs[HALVES]
            for start in range(0, GROUP, 4):
                part = noise_ref[:, start : start + 4].reshape(2, 4 * ol, periods)
                total = dot_rows(table_ref[0], part[0]) + dot_rows(table_ref[1], part[1])
                for k in range(4):
                    turned[pl.ds(start + k, hours, stride=GROUP), :] = total[:, k * ol : (k + 1) * ol]
            value = turned[...].reshape(HALVES, zs, hp, GROUP, ol).astype(BF16)
            for c in range(HALVES):
                outs[c][...] = value[c]

        return self.call(
            body, "hourly", al // GROUP, [struct((zs, hp, al, ol), BF16)] * HALVES,
            [pl.BlockSpec((2, GROUP, ol, periods), lambda i: (0, i, 0, 0)), whole_spec(tables.shape)],
            [pl.BlockSpec((zs, hp, GROUP, ol), lambda i: (0, 0, i, 0))] * HALVES,
            4 * hours * periods * al * ol, 2 * noise.size + 2 * hours * al * ol,
            [pltpu.VMEM((hours * GROUP, ol), F32)],
        )(noise, tables)

    def lat_up(self, g, lat, gain):
        zs, qs, hp, lr, ol, lats = self.zs, self.qs, self.hp, self.lr, self.ol, self.lats
        group = 8

        def body(gain_ref, g_ref, lat_ref, *outs):
            for start in range(0, group, 4):
                part = [g_ref[:, start + k].reshape(lats, ol) for k in range(4)]
                total = dot(lat_ref[...], jnp.concatenate(part, axis=1))
                code = encode(total * gain_ref[0])
                for k in range(4):
                    for d in range(qs):
                        outs[d][start + k] = code[d * lr : (d + 1) * lr, k * ol : (k + 1) * ol]

        return self.call(
            body, "lat_up", hp // group, self.parts_shape(I16),
            [SCALARS, pl.BlockSpec((zs, group, self.al, ol), lambda i: (0, i, 0, 0)), whole_spec(lat.shape)],
            self.parts_specs(group), 2 * self.cells * self.lats, 4 * self.cells,
        )(gain.reshape(1), g, lat)

    def residual(self, c, codes, back, lon_up, lon_down, observed, mask):
        qs, hp, lr, ol, lons = self.qs, self.hp, self.lr, self.ol, self.lons
        group = 8
        rows = group * lr

        def body(back_ref, *refs):
            arrived, (up_ref, down_ref, observed_ref, mask_ref) = refs[:qs], refs[qs : qs + 4]
            prior_ref, norm_ref, outs = refs[qs + 4], refs[qs + 5], refs[qs + 6 :]
            x = jnp.concatenate([decode(a[...].reshape(rows, ol)) for a in arrived], axis=1)
            prior = two_part_dot(x, up_ref[...]) * back_ref[0]
            prior_ref[...] = prior.reshape(group, lr, lons)
            seen = mask_ref[...].reshape(rows, lons).astype(F32)
            resid = seen * (observed_ref[...].reshape(rows, lons) - prior)

            @pl.when(pl.program_id(0) == 0)
            def _():
                norm_ref[...] = jnp.zeros_like(norm_ref)

            norm_ref[...] += fold(resid * resid)
            v = two_part_dot(resid, down_ref[...]).astype(BF16)
            for d in range(qs):
                outs[d][...] = v[:, d * ol : (d + 1) * ol].reshape(group, lr, ol)

        out = self.call(
            body, "residual", hp // group,
            [struct((hp, lr, lons), F32), struct((8, 128), F32)] + self.parts_shape(BF16),
            [SCALARS] + self.parts_specs(group) + [whole_spec(lon_up.shape)] * 2 + [self.grid_spec(group, c)] * 2,
            [self.grid_spec(group), whole_spec((8, 128))] + self.parts_specs(group),
            8 * self.cells * lons, 16 * self.cells,
        )(back.reshape(1), *codes, lon_up, lon_down, observed, mask)
        return out[0], out[1], out[2:]

    def lat_down(self, v, lat_t):
        zs, qs, hp, al, lr, ol, lats = self.zs, self.qs, self.hp, self.al, self.lr, self.ol, self.lats

        def body(*refs):
            sent, (lat_ref, out_ref, turned) = refs[:qs], refs[qs:]
            for start in range(0, GROUP, 4):
                part = [jnp.concatenate([s[start + k] for s in sent], axis=0) for k in range(4)]
                total = dot(lat_ref[...], jnp.concatenate(part, axis=1))
                for k in range(4):
                    turned[pl.ds(start + k, lats, stride=GROUP), :] = total[:, k * ol : (k + 1) * ol]
            out_ref[...] = turned[...].reshape(zs, al, GROUP, ol).astype(BF16)

        return self.call(
            body, "lat_down", hp // GROUP, [struct((zs, al, hp, ol), BF16)],
            self.parts_specs(GROUP) + [whole_spec(lat_t.shape)],
            [pl.BlockSpec((zs, al, GROUP, ol), lambda i: (0, 0, i, 0))],
            2 * self.cells * lats, 4 * self.cells,
            [pltpu.VMEM((lats * GROUP, ol), F32)],
        )(*v, lat_t)[0]

    def over_hours(self, halves, kern):
        zs, hp, al, ol, hours = self.zs, self.hp, self.al, self.ol, self.hours

        def body(*refs):
            sent, kern_ref, outs = refs[:HALVES], refs[HALVES], refs[HALVES + 1 : 2 * HALVES + 1]
            bend_ref, turned = refs[2 * HALVES + 1 :]

            @pl.when(pl.program_id(0) == 0)
            def _():
                bend_ref[...] = jnp.zeros_like(bend_ref)

            for start in range(0, GROUP, 4):
                part = [
                    jnp.concatenate([x[:, start + k].reshape(zs * hp, ol) for x in sent], axis=0) for k in range(4)
                ]
                part = jnp.concatenate(part, axis=1)
                total = dot(kern_ref[0], part) + dot(kern_ref[1], part)
                bend_ref[...] += fold(total * part.astype(F32))
                for k in range(4):
                    turned[pl.ds(start + k, hours, stride=GROUP), :] = total[:, k * ol : (k + 1) * ol]
            value = turned[...].reshape(HALVES, zs, hp, GROUP, ol).astype(BF16)
            for c in range(HALVES):
                outs[c][...] = value[c]

        out = self.call(
            body, "over_hours", al // GROUP, [struct((zs, hp, al, ol), BF16)] * HALVES + [struct((8, 128), F32)],
            [pl.BlockSpec((zs, GROUP, hp, ol), lambda i: (0, i, 0, 0))] * HALVES + [whole_spec(kern.shape)],
            [pl.BlockSpec((zs, hp, GROUP, ol), lambda i: (0, 0, i, 0))] * HALVES + [whole_spec((8, 128))],
            8 * self.cells * hours, 8 * self.cells,
            [pltpu.VMEM((hours * GROUP, ol), F32)],
        )(*halves, kern)
        return out[:HALVES], out[-1]

    def finish(self, s, c, codes, back, step, lon_up, prior, observed, mask, earlier):
        qs, hp, lr, ol, lons = self.qs, self.hp, self.lr, self.ol, self.lons
        group = 8
        rows = group * lr

        def body(scalar_ref, *refs):
            arrived, (up_ref, prior_ref, observed_ref, mask_ref) = refs[:qs], refs[qs : qs + 4]
            posterior_ref, next_ref = refs[-2:]
            x = jnp.concatenate([decode(a[...].reshape(rows, ol)) for a in arrived], axis=1)
            scaled = two_part_dot(x, up_ref[...]) * scalar_ref[0]
            prior = prior_ref[...].reshape(rows, lons)
            seen = mask_ref[...].reshape(rows, lons).astype(F32)
            resid = seen * (observed_ref[...].reshape(rows, lons) - prior)
            shape = (1, group, lr, lons)
            posterior_ref[...] = (prior + scaled).reshape(shape)
            next_ref[...] = (resid - seen * scaled - scalar_ref[1] * resid).reshape(shape)

        full = struct((2, self.hl, lr, lons), F32)
        start = c * (hp // group)
        out_spec = pl.BlockSpec((1, group, lr, lons), lambda i: (s, i + start, 0, 0))
        count = 1 + qs + 4
        return self.call(
            body, "finish", hp // group, [full, full],
            [SCALARS] + self.parts_specs(group) + [whole_spec(lon_up.shape), self.grid_spec(group)]
            + [self.grid_spec(group, c)] * 2 + [ANYWHERE] * len(earlier),
            [out_spec, out_spec], 4 * self.cells * lons, 22 * self.cells,
            aliases={count + i: i for i in range(len(earlier))},
        )(jnp.stack([back * step, NOISE_VAR * step]), *codes, lon_up, prior, observed, mask, *earlier)

    def joined(self, earlier):
        return tuple(earlier)


class Plain(Kernels):
    def after(self, x):
        return x

    def hourly(self, noise, tables):
        h = jnp.einsum("cyxk,cjk->jyx", noise, tables, preferred_element_type=F32).astype(BF16)
        h = h.reshape(HALVES, self.zs, self.hp, self.al, self.ol)
        return [h[c] for c in range(HALVES)]

    def lat_up(self, g, lat, gain):
        split = lat.reshape(self.qs, self.lr, self.zs, self.al)
        x = encode(jnp.einsum("qlzy,zhyx->qhlx", split, g, preferred_element_type=F32) * gain)
        return [x[d] for d in range(self.qs)]

    def up(self, codes, lon_up):
        x = jnp.concatenate([decode(c) for c in codes], axis=2)
        return jnp.einsum("hlx,xo->hlo", x, lon_up.astype(F32), precision=HIGH)

    def half(self, x, c):
        return x[c * self.hp : (c + 1) * self.hp]

    def residual(self, c, codes, back, lon_up, lon_down, observed, mask):
        prior = self.up(codes, lon_up) * back
        resid = self.half(mask, c).astype(F32) * (self.half(observed, c) - prior)
        v = jnp.einsum("hlo,op->hlp", resid, lon_down.astype(F32), precision=HIGH).astype(BF16)
        return prior, jnp.sum(resid * resid), jnp.split(v, self.qs, axis=2)

    def lat_down(self, v, lat_t):
        split = lat_t.reshape(self.zs, self.al, self.qs, self.lr)
        x = jnp.einsum("zyql,qhlx->zyhx", split, jnp.stack(v), preferred_element_type=F32)
        return x.astype(BF16)

    def over_hours(self, halves, kern):
        x = jnp.concatenate([jnp.swapaxes(h, 0, 1).reshape(self.al, -1, self.ol) for h in halves], axis=1)
        x = x.astype(F32)
        y = jnp.einsum("gk,ykx->gyx", kern.astype(F32).sum(0), x, precision=HIGH)
        bend = jnp.einsum("gyx,ygx->", y, x)
        y = y.astype(BF16).reshape(HALVES, self.zs, self.hp, self.al, self.ol)
        return [y[c] for c in range(HALVES)], bend

    def finish(self, s, c, codes, back, step, lon_up, prior, observed, mask, earlier):
        scaled = self.up(codes, lon_up) * (back * step)
        seen = self.half(mask, c).astype(F32)
        resid = seen * (self.half(observed, c) - prior)
        return tuple(earlier) + ((prior + scaled, resid - seen * scaled - NOISE_VAR * step * resid),)

    def joined(self, earlier):
        whole = []
        for i in range(2):
            samples = [
                jnp.concatenate([pair[i] for pair in earlier[s * HALVES : (s + 1) * HALVES]])
                for s in range(2)
            ]
            whole.append(jnp.stack(samples))
        return tuple(whole)


def swap_tm(x):
    return lax.all_to_all(x, "tm", split_axis=0, concat_axis=0, tiled=True)


def swap_lon(parts):
    count = len(parts)
    return [parts[0]] + [
        lax.ppermute(parts[d], "lon", [(i, i ^ d) for i in range(count)]) for d in range(1, count)
    ]


def largest_norm(factor, axis):
    return jnp.sqrt(jnp.max(jnp.sum(jnp.square(factor.astype(F32)), axis=axis)))


def shards(noise, observed, mask, lat_factor, lon_factor, spectrum):
    _, lat_local, lon_local, periods = noise.shape
    hour_local, lat_rows, lon_count = observed.shape
    hours = periods // 2
    hour_part = hour_local // HALVES
    zs, qs = hours // hour_local, lon_count // lon_local
    lat_count = zs * lat_local
    fits = lon_local % 128 == 0 and lat_rows % 16 == 0
    fits = fits and lat_local % GROUP == 0 and hour_part % GROUP == 0
    stages = (Kernels if fits else Plain)(zs, qs, hour_local, lat_local, lat_rows, lon_local)
    order = lax.axis_index("lon") ^ jnp.arange(qs)

    powers = jnp.concatenate([spectrum, spectrum[1:-1][::-1]])
    amplitude = jnp.sqrt(powers / periods)
    clock = jnp.arange(HALVES)[:, None, None] * hour_part + jnp.arange(zs)[None, :, None] * hour_local
    clock = (clock + jnp.arange(hour_part)).reshape(hours, 1)
    phase = (clock * jnp.arange(periods) % periods).astype(F32) * (2.0 * jnp.pi / periods)
    cosine_tab, sine_tab = jnp.cos(phase), jnp.sin(phase)
    table_cos = (cosine_tab * amplitude).astype(BF16)
    table_sin = (sine_tab * amplitude).astype(BF16)
    tables = (jnp.stack([table_cos, table_sin]), jnp.stack([-table_sin, table_cos]))

    def hour_kernel():
        scaled = powers / periods
        kern = jnp.dot(cosine_tab * scaled, cosine_tab.T, precision=EXACT) + jnp.dot(
            sine_tab * scaled, sine_tab.T, precision=EXACT
        )
        top = lax.reduce_precision(kern, 8, 7)
        return jnp.stack([top.astype(BF16), (kern - top).astype(BF16)])

    lon = lax.all_gather(lon_factor, "lon", axis=0, tiled=True).reshape(lon_count, qs, lon_local)
    units = [(s, c) for s in range(2) for c in range(HALVES)]
    first, second, third, fourth = units
    wait = stages.after
    arrived, waves = {}, {}
    for s in range(2):
        for c, part in enumerate(stages.hourly(noise, tables[s])):
            waves[s, c] = part
    arrived[first] = swap_tm(waves[first])
    arrived[second] = swap_tm(wait(waves[second]))
    kern = hour_kernel()
    lon_down = jnp.take(lon, order, axis=1).reshape(lon_count, lon_count)
    lon_up = lon_down.T
    lat = jnp.take(lat_factor.reshape(qs, lat_rows, lat_count), order, axis=0)
    lat = lat.reshape(lat_count, lat_count)
    lat_t = lat.T
    lat_row_norm = largest_norm(lat_factor, 1)
    lon_col_norm = largest_norm(lon_down, 0)
    lat_norm = jnp.sqrt(jnp.sum(jnp.square(lat_factor.astype(F32))))
    first_gain = CODE_MAX / jnp.maximum(lat_row_norm * (lat_count**0.5 * HOURLY_MAX), 1e-30)
    codes, priors, norms, sent, down = {}, {}, {}, {}, {}

    def up(u):
        codes[u] = swap_lon(stages.lat_up(arrived[u], lat, first_gain))

    def middle(u):
        priors[u], norms[u], v = stages.residual(
            u[1], codes[u], 1.0 / first_gain, lon_up, lon_down, observed, mask
        )
        sent[u] = swap_lon(v)

    def lower(u):
        down[u] = stages.lat_down(sent[u], lat_t)

    up(first)
    middle(first)
    arrived[third] = swap_tm(wait(waves[third]))
    up(second)
    lower(first)
    middle(second)
    arrived[fourth] = swap_tm(wait(waves[fourth]))
    up(third)
    lower(second)
    down[first] = swap_tm(wait(down[first]))
    middle(third)
    up(fourth)
    lower(third)
    down[second] = swap_tm(wait(down[second]))
    middle(fourth)
    down[third] = swap_tm(wait(down[third]))
    lower(fourth)
    down[fourth] = swap_tm(down[fourth])

    sums = []
    for s in range(2):
        mine = [u for u in units if u[0] == s]
        sums.append(sum(jnp.sum(norms[u]) for u in mine))
        halves, bending = stages.over_hours([down[u] for u in mine], kern)
        sums.append(jnp.sum(bending))
        for u in mine:
            waves[u] = halves[u[1]]
    arrived[first] = swap_tm(waves[first])
    arrived[second] = swap_tm(wait(waves[second]))
    sums = lax.psum(jnp.stack(sums), ("tm", "lon"))
    gains, steps = [], []
    for s in range(2):
        norm_sq, bending = sums[2 * s], sums[2 * s + 1]
        bound = SPECTRUM_MAX * lat_row_norm * lat_norm * lon_col_norm * jnp.sqrt(norm_sq)
        gains.append(CODE_MAX / jnp.maximum(bound, 1e-30))
        steps.append(norm_sq / (bending + NOISE_VAR * norm_sq))
    earlier = ()
    for u in units:
        s, c = u
        codes = swap_lon(stages.lat_up(arrived[u], lat, gains[s]))
        later = {first: third, second: fourth}.get(u)
        earlier = stages.finish(s, c, codes, 1.0 / gains[s], steps[s], lon_up, priors[u], observed, mask, earlier)
        if later is not None:
            arrived[later] = swap_tm(wait(waves[later]))
    return stages.joined(earlier)


def solution(mesh):
    return jax.shard_map(
        shards,
        mesh=mesh,
        in_specs=(
            P(None, "tm", "lon", None),
            P("tm", "lon", None),
            P("tm", "lon", None),
            P(),
            P("lon", None),
            P(),
        ),
        out_specs=(P(None, "tm", "lon", None), P(None, "tm", "lon", None)),
        check_vma=False,
    )
```

```python
import functools
import jax
import jax.numpy as jnp
from jax import lax
from jax.experimental import pallas as pl
from jax.experimental.pallas import tpu as pltpu
from jax.sharding import PartitionSpec as P

F32, BF16, I16, I32 = jnp.float32, jnp.bfloat16, jnp.int16, jnp.int32
EXACT, HIGH = lax.Precision.HIGHEST, lax.Precision.HIGH
NOISE_VAR = 0.25
SPECTRUM_MAX = 4.0
HOURLY_MAX = 400.0
STEPS = 1024.0
LEAST = -18.0
CODE_MAX = 2.0**13.5
GROUP = 16
HALVES = 2
EASE = 4
VMEM = 52 * 1024 * 1024


def encode(x):
    size = jnp.maximum(jnp.abs(x), 2.0**LEAST)
    code = (jnp.log(size) * (STEPS / 0.6931471805599453) + (0.5 - STEPS * LEAST)).astype(I32)
    return jnp.where(x < 0, -code, code).astype(I16)


def decode(code):
    wide = code.astype(I32)
    size = jnp.exp2(jnp.abs(wide).astype(F32) * (1.0 / STEPS) + LEAST)
    size = jnp.where(wide == 0, 0.0, size)
    return jnp.where(wide < 0, -size, size)


def dot(a, b):
    return jnp.dot(a, b, preferred_element_type=F32)


def dot_rows(a, b):
    return lax.dot_general(a, b, (((1,), (1,)), ((), ())), preferred_element_type=F32)


def two_part_dot(a, b):
    top = a.astype(BF16)
    rest = (a - top.astype(F32)).astype(BF16)
    both = dot(jnp.concatenate([top, rest], axis=0), b)
    return both[: a.shape[0]] + both[a.shape[0] :]


def fold(x):
    rows, cols = x.shape
    x = jnp.sum(x.reshape(rows // 8, 8, cols), axis=0)
    total = x[:, :128]
    for start in range(128, cols, 128):
        total = total + x[:, start : start + 128]
    return total


def whole_spec(shape):
    return pl.BlockSpec(shape, lambda i: (0,) * len(shape))


SCALARS = pl.BlockSpec(memory_space=pltpu.SMEM)
ANYWHERE = pl.BlockSpec(memory_space=pl.ANY)


def struct(shape, kind):
    return jax.ShapeDtypeStruct(shape, kind)


class Kernels:
    def __init__(self, zs, qs, hour_local, lat_local, lat_rows, lon_local):
        self.zs, self.qs = zs, qs
        self.al, self.lr, self.ol = lat_local, lat_rows, lon_local
        self.hl = hour_local
        self.hp = hour_local // HALVES
        self.hours, self.lats, self.lons = zs * hour_local, zs * lat_local, qs * lon_local
        self.cells = self.hp * lat_rows * self.lons
        self.token = None

    def call(self, body, name, grid, out_shape, in_specs, out_specs, flops, moved, scratch=(), aliases={}):
        tokens = [] if self.token is None else [self.token]

        def run(*args):
            def whole(*refs):
                refs = list(refs)
                del refs[len(args) : len(args) + len(tokens)]
                place = len(args) + len(out_shape)
                token_ref = refs.pop(place)
                token_ref[...] = jnp.zeros_like(token_ref)
                body(*refs)

            out = pl.pallas_call(
                whole,
                name=name,
                grid=(grid,),
                out_shape=list(out_shape) + [struct((8, 128), F32)],
                in_specs=list(in_specs) + [ANYWHERE] * len(tokens),
                out_specs=list(out_specs) + [whole_spec((8, 128))],
                scratch_shapes=list(scratch),
                input_output_aliases=aliases,
                compiler_params=pltpu.CompilerParams(vmem_limit_bytes=VMEM),
                cost_estimate=pl.CostEstimate(flops=flops * EASE, bytes_accessed=moved * EASE, transcendentals=0),
            )(*args, *tokens)
            self.token = out[-1]
            return out[:-1]

        return run

    def after(self, x, token=None):
        return pl.pallas_call(
            lambda x_ref, token_ref, out_ref: None,
            name="after",
            out_shape=struct(x.shape, x.dtype),
            in_specs=[ANYWHERE, ANYWHERE],
            out_specs=ANYWHERE,
            input_output_aliases={0: 0},
            compiler_params=pltpu.CompilerParams(vmem_limit_bytes=VMEM),
            cost_estimate=pl.CostEstimate(flops=0, bytes_accessed=0, transcendentals=0),
        )(x, self.token if token is None else token)

    def parts_specs(self, group):
        return [pl.BlockSpec((group, self.lr, self.ol), lambda i: (i, 0, 0))] * self.qs

    def parts_shape(self, kind):
        return [struct((self.hp, self.lr, self.ol), kind)] * self.qs

    def grid_spec(self, group, c=None):
        start = 0 if c is None else c * (self.hp // group)
        return pl.BlockSpec((group, self.lr, self.lons), lambda i: (i + start, 0, 0))

    def hourly(self, noise, tables):
        zs, hp, al, ol, hours = self.zs, self.hp, self.al, self.ol, self.hours
        periods = noise.shape[3]

        def body(noise_ref, table_ref, *refs):
            outs, turned = refs[:HALVES], refs[HALVES]
            for start in range(0, GROUP, 4):
                part = noise_ref[:, start : start + 4].reshape(2, 4 * ol, periods)
                total = dot_rows(table_ref[0], part[0]) + dot_rows(table_ref[1], part[1])
                for k in range(4):
                    turned[pl.ds(start + k, hours, stride=GROUP), :] = total[:, k * ol : (k + 1) * ol]
            value = turned[...].reshape(HALVES, zs, hp, GROUP, ol).astype(BF16)
            for c in range(HALVES):
                outs[c][...] = value[c]

        return self.call(
            body, "hourly", al // GROUP, [struct((zs, hp, al, ol), BF16)] * HALVES,
            [pl.BlockSpec((2, GROUP, ol, periods), lambda i: (0, i, 0, 0)), whole_spec(tables.shape)],
            [pl.BlockSpec((zs, hp, GROUP, ol), lambda i: (0, 0, i, 0))] * HALVES,
            4 * hours * periods * al * ol, 2 * noise.size + 2 * hours * al * ol,
            [pltpu.VMEM((hours * GROUP, ol), F32)],
        )(noise, tables)

    def lat_up(self, g, lat, gain):
        zs, qs, hp, lr, ol, lats = self.zs, self.qs, self.hp, self.lr, self.ol, self.lats
        group = 8

        def body(gain_ref, g_ref, lat_ref, *outs):
            for start in range(0, group, 4):
                part = [g_ref[:, start + k].reshape(lats, ol) for k in range(4)]
                total = dot(lat_ref[...], jnp.concatenate(part, axis=1))
                code = encode(total * gain_ref[0])
                for k in range(4):
                    for d in range(qs):
                        outs[d][start + k] = code[d * lr : (d + 1) * lr, k * ol : (k + 1) * ol]

        return self.call(
            body, "lat_up", hp // group, self.parts_shape(I16),
            [SCALARS, pl.BlockSpec((zs, group, self.al, ol), lambda i: (0, i, 0, 0)), whole_spec(lat.shape)],
            self.parts_specs(group), 2 * self.cells * self.lats, 4 * self.cells,
        )(gain.reshape(1), g, lat)

    def residual(self, c, codes, back, lon_up, lon_down, observed, mask):
        qs, hp, lr, ol, lons = self.qs, self.hp, self.lr, self.ol, self.lons
        group = 8
        rows = group * lr

        def body(back_ref, *refs):
            arrived, (up_ref, down_ref, observed_ref, mask_ref) = refs[:qs], refs[qs : qs + 4]
            prior_ref, norm_ref, outs = refs[qs + 4], refs[qs + 5], refs[qs + 6 :]
            x = jnp.concatenate([decode(a[...].reshape(rows, ol)) for a in arrived], axis=1)
            prior = two_part_dot(x, up_ref[...]) * back_ref[0]
            prior_ref[...] = prior.reshape(group, lr, lons)
            seen = mask_ref[...].reshape(rows, lons).astype(F32)
            resid = seen * (observed_ref[...].reshape(rows, lons) - prior)

            @pl.when(pl.program_id(0) == 0)
            def _():
                norm_ref[...] = jnp.zeros_like(norm_ref)

            norm_ref[...] += fold(resid * resid)
            v = two_part_dot(resid, down_ref[...]).astype(BF16)
            for d in range(qs):
                outs[d][...] = v[:, d * ol : (d + 1) * ol].reshape(group, lr, ol)

        out = self.call(
            body, "residual", hp // group,
            [struct((hp, lr, lons), F32), struct((8, 128), F32)] + self.parts_shape(BF16),
            [SCALARS] + self.parts_specs(group) + [whole_spec(lon_up.shape)] * 2 + [self.grid_spec(group, c)] * 2,
            [self.grid_spec(group), whole_spec((8, 128))] + self.parts_specs(group),
            8 * self.cells * lons, 16 * self.cells,
        )(back.reshape(1), *codes, lon_up, lon_down, observed, mask)
        return out[0], out[1], out[2:]

    def lat_down(self, v, lat_t):
        zs, qs, hp, al, lr, ol, lats = self.zs, self.qs, self.hp, self.al, self.lr, self.ol, self.lats

        def body(*refs):
            sent, (lat_ref, out_ref, turned) = refs[:qs], refs[qs:]
            for start in range(0, GROUP, 4):
                part = [jnp.concatenate([s[start + k] for s in sent], axis=0) for k in range(4)]
                total = dot(lat_ref[...], jnp.concatenate(part, axis=1))
                for k in range(4):
                    turned[pl.ds(start + k, lats, stride=GROUP), :] = total[:, k * ol : (k + 1) * ol]
            out_ref[...] = turned[...].reshape(zs, al, GROUP, ol).astype(BF16)

        return self.call(
            body, "lat_down", hp // GROUP, [struct((zs, al, hp, ol), BF16)],
            self.parts_specs(GROUP) + [whole_spec(lat_t.shape)],
            [pl.BlockSpec((zs, al, GROUP, ol), lambda i: (0, 0, i, 0))],
            2 * self.cells * lats, 4 * self.cells,
            [pltpu.VMEM((lats * GROUP, ol), F32)],
        )(*v, lat_t)[0]

    def over_hours(self, halves, kern):
        zs, hp, al, ol, hours = self.zs, self.hp, self.al, self.ol, self.hours

        def body(*refs):
            sent, kern_ref, outs = refs[:HALVES], refs[HALVES], refs[HALVES + 1 : 2 * HALVES + 1]
            bend_ref, turned = refs[2 * HALVES + 1 :]

            @pl.when(pl.program_id(0) == 0)
            def _():
                bend_ref[...] = jnp.zeros_like(bend_ref)

            for start in range(0, GROUP, 4):
                part = [
                    jnp.concatenate([x[:, start + k].reshape(zs * hp, ol) for x in sent], axis=0) for k in range(4)
                ]
                part = jnp.concatenate(part, axis=1)
                total = dot(kern_ref[0], part) + dot(kern_ref[1], part)
                bend_ref[...] += fold(total * part.astype(F32))
                for k in range(4):
                    turned[pl.ds(start + k, hours, stride=GROUP), :] = total[:, k * ol : (k + 1) * ol]
            value = turned[...].reshape(HALVES, zs, hp, GROUP, ol).astype(BF16)
            for c in range(HALVES):
                outs[c][...] = value[c]

        out = self.call(
            body, "over_hours", al // GROUP, [struct((zs, hp, al, ol), BF16)] * HALVES + [struct((8, 128), F32)],
            [pl.BlockSpec((zs, GROUP, hp, ol), lambda i: (0, i, 0, 0))] * HALVES + [whole_spec(kern.shape)],
            [pl.BlockSpec((zs, hp, GROUP, ol), lambda i: (0, 0, i, 0))] * HALVES + [whole_spec((8, 128))],
            8 * self.cells * hours, 8 * self.cells,
            [pltpu.VMEM((hours * GROUP, ol), F32)],
        )(*halves, kern)
        return out[:HALVES], out[-1]

    def finish(self, s, c, codes, back, step, lon_up, prior, observed, mask, earlier):
        qs, hp, lr, ol, lons = self.qs, self.hp, self.lr, self.ol, self.lons
        group = 8
        rows = group * lr

        def body(scalar_ref, *refs):
            arrived, (up_ref, prior_ref, observed_ref, mask_ref) = refs[:qs], refs[qs : qs + 4]
            posterior_ref, next_ref = refs[-2:]
            x = jnp.concatenate([decode(a[...].reshape(rows, ol)) for a in arrived], axis=1)
            scaled = two_part_dot(x, up_ref[...]) * scalar_ref[0]
            prior = prior_ref[...].reshape(rows, lons)
            seen = mask_ref[...].reshape(rows, lons).astype(F32)
            resid = seen * (observed_ref[...].reshape(rows, lons) - prior)
            shape = (1, group, lr, lons)
            posterior_ref[...] = (prior + scaled).reshape(shape)
            next_ref[...] = (resid - seen * scaled - scalar_ref[1] * resid).reshape(shape)

        full = struct((2, self.hl, lr, lons), F32)
        start = c * (hp // group)
        out_spec = pl.BlockSpec((1, group, lr, lons), lambda i: (s, i + start, 0, 0))
        count = 1 + qs + 4
        return self.call(
            body, "finish", hp // group, [full, full],
            [SCALARS] + self.parts_specs(group) + [whole_spec(lon_up.shape), self.grid_spec(group)]
            + [self.grid_spec(group, c)] * 2 + [ANYWHERE] * len(earlier),
            [out_spec, out_spec], 4 * self.cells * lons, 22 * self.cells,
            aliases={count + i: i for i in range(len(earlier))},
        )(jnp.stack([back * step, NOISE_VAR * step]), *codes, lon_up, prior, observed, mask, *earlier)

    def joined(self, earlier):
        return tuple(earlier)


class Plain(Kernels):
    def after(self, x, token=None):
        return x

    def hourly(self, noise, tables):
        h = jnp.einsum("cyxk,cjk->jyx", noise, tables, preferred_element_type=F32).astype(BF16)
        h = h.reshape(HALVES, self.zs, self.hp, self.al, self.ol)
        return [h[c] for c in range(HALVES)]

    def lat_up(self, g, lat, gain):
        split = lat.reshape(self.qs, self.lr, self.zs, self.al)
        x = encode(jnp.einsum("qlzy,zhyx->qhlx", split, g, preferred_element_type=F32) * gain)
        return [x[d] for d in range(self.qs)]

    def up(self, codes, lon_up):
        x = jnp.concatenate([decode(c) for c in codes], axis=2)
        return jnp.einsum("hlx,xo->hlo", x, lon_up.astype(F32), precision=HIGH)

    def half(self, x, c):
        return x[c * self.hp : (c + 1) * self.hp]

    def residual(self, c, codes, back, lon_up, lon_down, observed, mask):
        prior = self.up(codes, lon_up) * back
        resid = self.half(mask, c).astype(F32) * (self.half(observed, c) - prior)
        v = jnp.einsum("hlo,op->hlp", resid, lon_down.astype(F32), precision=HIGH).astype(BF16)
        return prior, jnp.sum(resid * resid), jnp.split(v, self.qs, axis=2)

    def lat_down(self, v, lat_t):
        split = lat_t.reshape(self.zs, self.al, self.qs, self.lr)
        x = jnp.einsum("zyql,qhlx->zyhx", split, jnp.stack(v), preferred_element_type=F32)
        return x.astype(BF16)

    def over_hours(self, halves, kern):
        x = jnp.concatenate([jnp.swapaxes(h, 0, 1).reshape(self.al, -1, self.ol) for h in halves], axis=1)
        x = x.astype(F32)
        y = jnp.einsum("gk,ykx->gyx", kern.astype(F32).sum(0), x, precision=HIGH)
        bend = jnp.einsum("gyx,ygx->", y, x)
        y = y.astype(BF16).reshape(HALVES, self.zs, self.hp, self.al, self.ol)
        return [y[c] for c in range(HALVES)], bend

    def finish(self, s, c, codes, back, step, lon_up, prior, observed, mask, earlier):
        scaled = self.up(codes, lon_up) * (back * step)
        seen = self.half(mask, c).astype(F32)
        resid = seen * (self.half(observed, c) - prior)
        return tuple(earlier) + ((prior + scaled, resid - seen * scaled - NOISE_VAR * step * resid),)

    def joined(self, earlier):
        whole = []
        for i in range(2):
            samples = [
                jnp.concatenate([pair[i] for pair in earlier[s * HALVES : (s + 1) * HALVES]])
                for s in range(2)
            ]
            whole.append(jnp.stack(samples))
        return tuple(whole)


def swap_tm(x):
    return lax.all_to_all(x, "tm", split_axis=0, concat_axis=0, tiled=True)


def swap_lon(parts):
    count = len(parts)
    return [parts[0]] + [
        lax.ppermute(parts[d], "lon", [(i, i ^ d) for i in range(count)]) for d in range(1, count)
    ]


def add_over_tm(x, count):
    return sum([lax.ppermute(x, "tm", [(i, i ^ d) for i in range(count)]) for d in range(1, count)], x)


def add_over_lon(x, count):
    d = 1
    while d < count:
        x = x + lax.ppermute(x, "lon", [(i, i ^ d) for i in range(count)])
        d *= 2
    return x


def largest_norm(factor, axis):
    return jnp.sqrt(jnp.max(jnp.sum(jnp.square(factor.astype(F32)), axis=axis)))


def shards(noise, observed, mask, lat_factor, lon_factor, spectrum):
    _, lat_local, lon_local, periods = noise.shape
    hour_local, lat_rows, lon_count = observed.shape
    hours = periods // 2
    hour_part = hour_local // HALVES
    zs, qs = hours // hour_local, lon_count // lon_local
    lat_count = zs * lat_local
    fits = lon_local % 128 == 0 and lat_rows % 16 == 0
    fits = fits and lat_local % GROUP == 0 and hour_part % GROUP == 0
    stages = (Kernels if fits else Plain)(zs, qs, hour_local, lat_local, lat_rows, lon_local)
    order = lax.axis_index("lon") ^ jnp.arange(qs)

    powers = jnp.concatenate([spectrum, spectrum[1:-1][::-1]])
    amplitude = jnp.sqrt(powers / periods)
    clock = jnp.arange(HALVES)[:, None, None] * hour_part + jnp.arange(zs)[None, :, None] * hour_local
    clock = (clock + jnp.arange(hour_part)).reshape(hours, 1)
    phase = (clock * jnp.arange(periods) % periods).astype(F32) * (2.0 * jnp.pi / periods)
    cosine_tab, sine_tab = jnp.cos(phase), jnp.sin(phase)
    table_cos = (cosine_tab * amplitude).astype(BF16)
    table_sin = (sine_tab * amplitude).astype(BF16)
    tables = (jnp.stack([table_cos, table_sin]), jnp.stack([-table_sin, table_cos]))

    def hour_kernel():
        scaled = powers / periods
        kern = jnp.dot(cosine_tab * scaled, cosine_tab.T, precision=EXACT) + jnp.dot(
            sine_tab * scaled, sine_tab.T, precision=EXACT
        )
        top = lax.reduce_precision(kern, 8, 7)
        return jnp.stack([top.astype(BF16), (kern - top).astype(BF16)])

    lon = lax.all_gather(lon_factor, "lon", axis=0, tiled=True).reshape(lon_count, qs, lon_local)
    units = [(s, c) for s in range(2) for c in range(HALVES)]
    first, second, third, fourth = units
    wait = stages.after
    arrived, waves = {}, {}
    for s in range(2):
        for c, part in enumerate(stages.hourly(noise, tables[s])):
            waves[s, c] = part
    arrived[first] = swap_tm(waves[first])
    arrived[second] = swap_tm(wait(waves[second]))
    kern = hour_kernel()
    lon_down = jnp.take(lon, order, axis=1).reshape(lon_count, lon_count)
    lon_up = lon_down.T
    lat = jnp.take(lat_factor.reshape(qs, lat_rows, lat_count), order, axis=0)
    lat = lat.reshape(lat_count, lat_count)
    lat_t = lat.T
    lat_row_norm = largest_norm(lat_factor, 1)
    lon_col_norm = largest_norm(lon_down, 0)
    lat_norm = jnp.sqrt(jnp.sum(jnp.square(lat_factor.astype(F32))))
    first_gain = CODE_MAX / jnp.maximum(lat_row_norm * (lat_count**0.5 * HOURLY_MAX), 1e-30)
    codes, priors, norms, sent, down = {}, {}, {}, {}, {}

    def up(u):
        codes[u] = swap_lon(stages.lat_up(arrived[u], lat, first_gain))

    def middle(u):
        priors[u], norms[u], v = stages.residual(
            u[1], codes[u], 1.0 / first_gain, lon_up, lon_down, observed, mask
        )
        sent[u] = swap_lon(v)

    def lower(u):
        down[u] = stages.lat_down(sent[u], lat_t)

    up(first)
    middle(first)
    arrived[third] = swap_tm(wait(waves[third]))
    up(second)
    lower(first)
    arrived[fourth] = swap_tm(wait(waves[fourth]))
    middle(second)
    up(third)
    lower(second)
    down[first] = swap_tm(wait(down[first]))
    middle(third)
    up(fourth)
    lower(third)
    down[second] = swap_tm(wait(down[second]))
    middle(fourth)
    down[third] = swap_tm(wait(down[third]))
    lower(fourth)
    down[fourth] = swap_tm(down[fourth])

    sums = []
    for s in range(2):
        mine = [u for u in units if u[0] == s]
        sums.append(sum(jnp.sum(norms[u]) for u in mine))
        halves, bending = stages.over_hours([down[u] for u in mine], kern)
        sums.append(jnp.sum(bending))
        for u in mine:
            waves[u] = halves[u[1]]
    arrived[first] = swap_tm(waves[first])
    sums = add_over_tm(jnp.broadcast_to(jnp.stack(sums)[:, None], (4, 128)), zs)
    arrived[second] = swap_tm(wait(waves[second], sums))
    sums = add_over_lon(sums, qs)[:, 0]
    gains, steps = [], []
    for s in range(2):
        norm_sq, bending = sums[2 * s], sums[2 * s + 1]
        bound = SPECTRUM_MAX * lat_row_norm * lat_norm * lon_col_norm * jnp.sqrt(norm_sq)
        gains.append(CODE_MAX / jnp.maximum(bound, 1e-30))
        steps.append(norm_sq / (bending + NOISE_VAR * norm_sq))
    earlier = ()
    for u in units:
        s, c = u
        codes = swap_lon(stages.lat_up(arrived[u], lat, gains[s]))
        later = {first: third, second: fourth}.get(u)
        earlier = stages.finish(s, c, codes, 1.0 / gains[s], steps[s], lon_up, priors[u], observed, mask, earlier)
        if later is not None:
            arrived[later] = swap_tm(wait(waves[later]))
    return stages.joined(earlier)


def solution(mesh):
    return jax.shard_map(
        shards,
        mesh=mesh,
        in_specs=(
            P(None, "tm", "lon", None),
            P("tm", "lon", None),
            P("tm", "lon", None),
            P(),
            P("lon", None),
            P(),
        ),
        out_specs=(P(None, "tm", "lon", None), P(None, "tm", "lon", None)),
        check_vma=False,
    )
```

```python
import functools
import jax
import jax.numpy as jnp
from jax import lax
from jax.experimental import pallas as pl
from jax.experimental.pallas import tpu as pltpu
from jax.sharding import PartitionSpec as P

F32, BF16, I16, I32 = jnp.float32, jnp.bfloat16, jnp.int16, jnp.int32
EXACT, HIGH = lax.Precision.HIGHEST, lax.Precision.HIGH
NOISE_VAR = 0.25
SPECTRUM_MAX = 4.0
HOURLY_MAX = 400.0
STEPS = 1024.0
LEAST = -18.0
CODE_MAX = 2.0**13.5
GROUP = 16
HALVES = 2
EASE = 4
VMEM = 52 * 1024 * 1024


def encode(x):
    size = jnp.maximum(jnp.abs(x), 2.0**LEAST)
    code = (jnp.log(size) * (STEPS / 0.6931471805599453) + (0.5 - STEPS * LEAST)).astype(I32)
    return jnp.where(x < 0, -code, code).astype(I16)


def decode(code):
    wide = code.astype(I32)
    size = jnp.exp2(jnp.abs(wide).astype(F32) * (1.0 / STEPS) + LEAST)
    size = jnp.where(wide == 0, 0.0, size)
    return jnp.where(wide < 0, -size, size)


def dot(a, b):
    return jnp.dot(a, b, preferred_element_type=F32)


def dot_rows(a, b):
    return lax.dot_general(a, b, (((1,), (1,)), ((), ())), preferred_element_type=F32)


def two_part_dot(a, b):
    top = a.astype(BF16)
    rest = (a - top.astype(F32)).astype(BF16)
    both = dot(jnp.concatenate([top, rest], axis=0), b)
    return both[: a.shape[0]] + both[a.shape[0] :]


def fold(x):
    rows, cols = x.shape
    x = jnp.sum(x.reshape(rows // 8, 8, cols), axis=0)
    total = x[:, :128]
    for start in range(128, cols, 128):
        total = total + x[:, start : start + 128]
    return total


def whole_spec(shape):
    return pl.BlockSpec(shape, lambda i: (0,) * len(shape))


SCALARS = pl.BlockSpec(memory_space=pltpu.SMEM)
ANYWHERE = pl.BlockSpec(memory_space=pl.ANY)


def struct(shape, kind):
    return jax.ShapeDtypeStruct(shape, kind)


class Kernels:
    def __init__(self, zs, qs, hour_local, lat_local, lat_rows, lon_local):
        self.zs, self.qs = zs, qs
        self.al, self.lr, self.ol = lat_local, lat_rows, lon_local
        self.hl = hour_local
        self.hp = hour_local // HALVES
        self.hours, self.lats, self.lons = zs * hour_local, zs * lat_local, qs * lon_local
        self.cells = self.hp * lat_rows * self.lons
        self.token = None

    def call(self, body, name, grid, out_shape, in_specs, out_specs, flops, moved, scratch=(), aliases={}):
        tokens = [] if self.token is None else [self.token]

        def run(*args):
            def whole(*refs):
                refs = list(refs)
                del refs[len(args) : len(args) + len(tokens)]
                place = len(args) + len(out_shape)
                token_ref = refs.pop(place)
                token_ref[...] = jnp.zeros_like(token_ref)
                body(*refs)

            out = pl.pallas_call(
                whole,
                name=name,
                grid=(grid,),
                out_shape=list(out_shape) + [struct((8, 128), F32)],
                in_specs=list(in_specs) + [ANYWHERE] * len(tokens),
                out_specs=list(out_specs) + [whole_spec((8, 128))],
                scratch_shapes=list(scratch),
                input_output_aliases=aliases,
                compiler_params=pltpu.CompilerParams(vmem_limit_bytes=VMEM),
                cost_estimate=pl.CostEstimate(flops=flops * EASE, bytes_accessed=moved * EASE, transcendentals=0),
            )(*args, *tokens)
            self.token = out[-1]
            return out[:-1]

        return run

    def after(self, x, token=None):
        return pl.pallas_call(
            lambda x_ref, token_ref, out_ref: None,
            name="after",
            out_shape=struct(x.shape, x.dtype),
            in_specs=[ANYWHERE, ANYWHERE],
            out_specs=ANYWHERE,
            input_output_aliases={0: 0},
            compiler_params=pltpu.CompilerParams(vmem_limit_bytes=VMEM),
            cost_estimate=pl.CostEstimate(flops=0, bytes_accessed=0, transcendentals=0),
        )(x, self.token if token is None else token)

    def parts_specs(self, group):
        return [pl.BlockSpec((group, self.lr, self.ol), lambda i: (i, 0, 0))] * self.qs

    def parts_shape(self, kind):
        return [struct((self.hp, self.lr, self.ol), kind)] * self.qs

    def grid_spec(self, group, c=None):
        start = 0 if c is None else c * (self.hp // group)
        return pl.BlockSpec((group, self.lr, self.lons), lambda i: (i + start, 0, 0))

    def hourly(self, noise, tables):
        zs, hp, al, ol, hours = self.zs, self.hp, self.al, self.ol, self.hours
        periods = noise.shape[3]

        def body(noise_ref, table_ref, *refs):
            outs, turned = refs[:HALVES], refs[HALVES]
            for start in range(0, GROUP, 4):
                part = noise_ref[:, start : start + 4].reshape(2, 4 * ol, periods)
                total = dot_rows(table_ref[0], part[0]) + dot_rows(table_ref[1], part[1])
                for k in range(4):
                    turned[pl.ds(start + k, hours, stride=GROUP), :] = total[:, k * ol : (k + 1) * ol]
            value = turned[...].reshape(zs, HALVES, hp, GROUP, ol).astype(BF16)
            for c in range(HALVES):
                outs[c][...] = value[:, c]

        return self.call(
            body, "hourly", al // GROUP, [struct((zs, hp, al, ol), BF16)] * HALVES,
            [pl.BlockSpec((2, GROUP, ol, periods), lambda i: (0, i, 0, 0)), whole_spec(tables.shape)],
            [pl.BlockSpec((zs, hp, GROUP, ol), lambda i: (0, 0, i, 0))] * HALVES,
            4 * hours * periods * al * ol, 2 * noise.size + 2 * hours * al * ol,
            [pltpu.VMEM((hours * GROUP, ol), F32)],
        )(noise, tables)

    def lat_up(self, c, g, lat, gain):
        zs, qs, hp, lr, ol, lats = self.zs, self.qs, self.hp, self.lr, self.ol, self.lats
        group = 8
        offset = c * (hp // group) if g.shape[1] == self.hl else 0

        def body(gain_ref, g_ref, lat_ref, *outs):
            for start in range(0, group, 4):
                part = [g_ref[:, start + k].reshape(lats, ol) for k in range(4)]
                total = dot(lat_ref[...], jnp.concatenate(part, axis=1))
                code = encode(total * gain_ref[0])
                for k in range(4):
                    for d in range(qs):
                        outs[d][start + k] = code[d * lr : (d + 1) * lr, k * ol : (k + 1) * ol]

        return self.call(
            body, "lat_up", hp // group, self.parts_shape(I16),
            [SCALARS, pl.BlockSpec((zs, group, self.al, ol), lambda i: (0, i + offset, 0, 0)), whole_spec(lat.shape)],
            self.parts_specs(group), 2 * self.cells * self.lats, 4 * self.cells,
        )(gain.reshape(1), g, lat)

    def residual(self, c, codes, back, lon_up, lon_down, observed, mask):
        qs, hp, lr, ol, lons = self.qs, self.hp, self.lr, self.ol, self.lons
        group = 8
        rows = group * lr

        def body(back_ref, *refs):
            arrived, (up_ref, down_ref, observed_ref, mask_ref) = refs[:qs], refs[qs : qs + 4]
            prior_ref, norm_ref, outs = refs[qs + 4], refs[qs + 5], refs[qs + 6 :]
            x = jnp.concatenate([decode(a[...].reshape(rows, ol)) for a in arrived], axis=1)
            prior = two_part_dot(x, up_ref[...]) * back_ref[0]
            prior_ref[...] = prior.reshape(group, lr, lons)
            seen = mask_ref[...].reshape(rows, lons).astype(F32)
            resid = seen * (observed_ref[...].reshape(rows, lons) - prior)

            @pl.when(pl.program_id(0) == 0)
            def _():
                norm_ref[...] = jnp.zeros_like(norm_ref)

            norm_ref[...] += fold(resid * resid)
            v = two_part_dot(resid, down_ref[...]).astype(BF16)
            for d in range(qs):
                outs[d][...] = v[:, d * ol : (d + 1) * ol].reshape(group, lr, ol)

        out = self.call(
            body, "residual", hp // group,
            [struct((hp, lr, lons), F32), struct((8, 128), F32)] + self.parts_shape(BF16),
            [SCALARS] + self.parts_specs(group) + [whole_spec(lon_up.shape)] * 2 + [self.grid_spec(group, c)] * 2,
            [self.grid_spec(group), whole_spec((8, 128))] + self.parts_specs(group),
            8 * self.cells * lons, 16 * self.cells,
        )(back.reshape(1), *codes, lon_up, lon_down, observed, mask)
        return out[0], out[1], out[2:]

    def lat_down(self, c, v, lat_t, earlier):
        zs, qs, hp, al, lr, ol, lats = self.zs, self.qs, self.hp, self.al, self.lr, self.ol, self.lats

        offset = c * (hp // GROUP)

        def body(*refs):
            sent, lat_ref, (out_ref, turned) = refs[:qs], refs[qs], refs[-2:]
            for start in range(0, GROUP, 4):
                part = [jnp.concatenate([s[start + k] for s in sent], axis=0) for k in range(4)]
                total = dot(lat_ref[...], jnp.concatenate(part, axis=1))
                for k in range(4):
                    turned[pl.ds(start + k, lats, stride=GROUP), :] = total[:, k * ol : (k + 1) * ol]
            out_ref[...] = turned[...].reshape(zs, al, GROUP, ol).astype(BF16)

        return self.call(
            body, "lat_down", hp // GROUP, [struct((zs, al, self.hl, ol), BF16)],
            self.parts_specs(GROUP) + [whole_spec(lat_t.shape)] + [ANYWHERE] * len(earlier),
            [pl.BlockSpec((zs, al, GROUP, ol), lambda i: (0, 0, i + offset, 0))],
            2 * self.cells * lats, 4 * self.cells,
            [pltpu.VMEM((lats * GROUP, ol), F32)], {qs + 1: 0} if earlier else {},
        )(*v, lat_t, *earlier)

    def over_hours(self, x, kern, pieces):
        zs, hl, al, ol, hours = self.zs, self.hl, self.al, self.ol, self.hours
        hp = hl // pieces

        def body(x_ref, kern_ref, *refs):
            outs, (bend_ref, turned) = refs[:pieces], refs[pieces:]

            @pl.when(pl.program_id(0) == 0)
            def _():
                bend_ref[...] = jnp.zeros_like(bend_ref)

            for start in range(0, GROUP, 4):
                part = [x_ref[:, start + k].reshape(hours, ol) for k in range(4)]
                part = jnp.concatenate(part, axis=1)
                total = dot(kern_ref[0], part) + dot(kern_ref[1], part)
                bend_ref[...] += fold(total * part.astype(F32))
                for k in range(4):
                    turned[pl.ds(start + k, hours, stride=GROUP), :] = total[:, k * ol : (k + 1) * ol]
            value = turned[...].reshape(zs, pieces, hp, GROUP, ol).astype(BF16)
            for c in range(pieces):
                outs[c][...] = value[:, c]

        out = self.call(
            body, "over_hours", al // GROUP, [struct((zs, hp, al, ol), BF16)] * pieces + [struct((8, 128), F32)],
            [pl.BlockSpec((zs, GROUP, hl, ol), lambda i: (0, i, 0, 0)), whole_spec(kern.shape)],
            [pl.BlockSpec((zs, hp, GROUP, ol), lambda i: (0, 0, i, 0))] * pieces + [whole_spec((8, 128))],
            8 * self.cells * hours, 8 * self.cells,
            [pltpu.VMEM((hours * GROUP, ol), F32)],
        )(x, kern)
        return out[:pieces], out[-1]

    def finish(self, s, c, codes, back, step, lon_up, prior, observed, mask, earlier):
        qs, hp, lr, ol, lons = self.qs, self.hp, self.lr, self.ol, self.lons
        group = 8
        rows = group * lr

        def body(scalar_ref, *refs):
            arrived, (up_ref, prior_ref, observed_ref, mask_ref) = refs[:qs], refs[qs : qs + 4]
            posterior_ref, next_ref = refs[-2:]
            x = jnp.concatenate([decode(a[...].reshape(rows, ol)) for a in arrived], axis=1)
            scaled = two_part_dot(x, up_ref[...]) * scalar_ref[0]
            prior = prior_ref[...].reshape(rows, lons)
            seen = mask_ref[...].reshape(rows, lons).astype(F32)
            resid = seen * (observed_ref[...].reshape(rows, lons) - prior)
            shape = (1, group, lr, lons)
            posterior_ref[...] = (prior + scaled).reshape(shape)
            next_ref[...] = (resid - seen * scaled - scalar_ref[1] * resid).reshape(shape)

        full = struct((2, self.hl, lr, lons), F32)
        start = c * (hp // group)
        out_spec = pl.BlockSpec((1, group, lr, lons), lambda i: (s, i + start, 0, 0))
        count = 1 + qs + 4
        return self.call(
            body, "finish", hp // group, [full, full],
            [SCALARS] + self.parts_specs(group) + [whole_spec(lon_up.shape), self.grid_spec(group)]
            + [self.grid_spec(group, c)] * 2 + [ANYWHERE] * len(earlier),
            [out_spec, out_spec], 4 * self.cells * lons, 22 * self.cells,
            aliases={count + i: i for i in range(len(earlier))},
        )(jnp.stack([back * step, NOISE_VAR * step]), *codes, lon_up, prior, observed, mask, *earlier)

    def joined(self, earlier):
        return tuple(earlier)


class Plain(Kernels):
    def after(self, x, token=None):
        return x

    def hourly(self, noise, tables):
        h = jnp.einsum("cyxk,cjk->jyx", noise, tables, preferred_element_type=F32).astype(BF16)
        h = h.reshape(self.zs, HALVES, self.hp, self.al, self.ol)
        return [h[:, c] for c in range(HALVES)]

    def lat_up(self, c, g, lat, gain):
        if g.shape[1] == self.hl:
            g = g[:, c * self.hp : (c + 1) * self.hp]
        split = lat.reshape(self.qs, self.lr, self.zs, self.al)
        x = encode(jnp.einsum("qlzy,zhyx->qhlx", split, g, preferred_element_type=F32) * gain)
        return [x[d] for d in range(self.qs)]

    def up(self, codes, lon_up):
        x = jnp.concatenate([decode(c) for c in codes], axis=2)
        return jnp.einsum("hlx,xo->hlo", x, lon_up.astype(F32), precision=HIGH)

    def half(self, x, c):
        return x[c * self.hp : (c + 1) * self.hp]

    def residual(self, c, codes, back, lon_up, lon_down, observed, mask):
        prior = self.up(codes, lon_up) * back
        resid = self.half(mask, c).astype(F32) * (self.half(observed, c) - prior)
        v = jnp.einsum("hlo,op->hlp", resid, lon_down.astype(F32), precision=HIGH).astype(BF16)
        return prior, jnp.sum(resid * resid), jnp.split(v, self.qs, axis=2)

    def lat_down(self, c, v, lat_t, earlier):
        split = lat_t.reshape(self.zs, self.al, self.qs, self.lr)
        x = jnp.einsum("zyql,qhlx->zyhx", split, jnp.stack(v), preferred_element_type=F32)
        return (jnp.concatenate(list(earlier) + [x.astype(BF16)], axis=2),)

    def over_hours(self, x, kern, pieces):
        x = jnp.swapaxes(x, 0, 1).reshape(self.al, self.hours, self.ol).astype(F32)
        y = jnp.einsum("gk,ykx->gyx", kern.astype(F32).sum(0), x, precision=HIGH)
        bend = jnp.einsum("gyx,ygx->", y, x)
        y = y.astype(BF16).reshape(self.zs, pieces, self.hl // pieces, self.al, self.ol)
        return [y[:, c] for c in range(pieces)], bend

    def finish(self, s, c, codes, back, step, lon_up, prior, observed, mask, earlier):
        scaled = self.up(codes, lon_up) * (back * step)
        seen = self.half(mask, c).astype(F32)
        resid = seen * (self.half(observed, c) - prior)
        return tuple(earlier) + ((prior + scaled, resid - seen * scaled - NOISE_VAR * step * resid),)

    def joined(self, earlier):
        whole = []
        for i in range(2):
            samples = [
                jnp.concatenate([pair[i] for pair in earlier[s * HALVES : (s + 1) * HALVES]])
                for s in range(2)
            ]
            whole.append(jnp.stack(samples))
        return tuple(whole)


def swap_tm(x):
    return lax.all_to_all(x, "tm", split_axis=0, concat_axis=0, tiled=True)


def swap_lon(parts):
    count = len(parts)
    return [parts[0]] + [
        lax.ppermute(parts[d], "lon", [(i, i ^ d) for i in range(count)]) for d in range(1, count)
    ]


def add_over_tm(x, count):
    return sum([lax.ppermute(x, "tm", [(i, i ^ d) for i in range(count)]) for d in range(1, count)], x)


def add_over_lon(x, count):
    d = 1
    while d < count:
        x = x + lax.ppermute(x, "lon", [(i, i ^ d) for i in range(count)])
        d *= 2
    return x


def largest_norm(factor, axis):
    return jnp.sqrt(jnp.max(jnp.sum(jnp.square(factor.astype(F32)), axis=axis)))


def shards(noise, observed, mask, lat_factor, lon_factor, spectrum):
    _, lat_local, lon_local, periods = noise.shape
    hour_local, lat_rows, lon_count = observed.shape
    hours = periods // 2
    hour_part = hour_local // HALVES
    zs, qs = hours // hour_local, lon_count // lon_local
    lat_count = zs * lat_local
    fits = lon_local % 128 == 0 and lat_rows % 16 == 0
    fits = fits and lat_local % GROUP == 0 and hour_part % GROUP == 0
    stages = (Kernels if fits else Plain)(zs, qs, hour_local, lat_local, lat_rows, lon_local)
    order = lax.axis_index("lon") ^ jnp.arange(qs)

    powers = jnp.concatenate([spectrum, spectrum[1:-1][::-1]])
    amplitude = jnp.sqrt(powers / periods)
    clock = jnp.arange(hours)[:, None]
    phase = (clock * jnp.arange(periods) % periods).astype(F32) * (2.0 * jnp.pi / periods)
    cosine_tab, sine_tab = jnp.cos(phase), jnp.sin(phase)
    table_cos = (cosine_tab * amplitude).astype(BF16)
    table_sin = (sine_tab * amplitude).astype(BF16)
    tables = (jnp.stack([table_cos, table_sin]), jnp.stack([-table_sin, table_cos]))

    def hour_kernel():
        scaled = powers / periods
        kern = jnp.dot(cosine_tab * scaled, cosine_tab.T, precision=EXACT) + jnp.dot(
            sine_tab * scaled, sine_tab.T, precision=EXACT
        )
        top = lax.reduce_precision(kern, 8, 7)
        return jnp.stack([top.astype(BF16), (kern - top).astype(BF16)])

    lon = lax.all_gather(lon_factor, "lon", axis=0, tiled=True).reshape(lon_count, qs, lon_local)
    units = [(s, c) for s in range(2) for c in range(HALVES)]
    first, second, third, fourth = units
    wait = stages.after
    arrived, waves = {}, {}
    for s in range(2):
        for c, part in enumerate(stages.hourly(noise, tables[s])):
            waves[s, c] = part
    arrived[first] = swap_tm(waves[first])
    arrived[second] = swap_tm(wait(waves[second]))
    kern = hour_kernel()
    lon_down = jnp.take(lon, order, axis=1).reshape(lon_count, lon_count)
    lon_up = lon_down.T
    lat = jnp.take(lat_factor.reshape(qs, lat_rows, lat_count), order, axis=0)
    lat = lat.reshape(lat_count, lat_count)
    lat_t = lat.T
    lat_row_norm = largest_norm(lat_factor, 1)
    lon_col_norm = largest_norm(lon_down, 0)
    lat_norm = jnp.sqrt(jnp.sum(jnp.square(lat_factor.astype(F32))))
    first_gain = CODE_MAX / jnp.maximum(lat_row_norm * (lat_count**0.5 * HOURLY_MAX), 1e-30)
    codes, priors, norms, sent, down = {}, {}, {}, {}, {}

    def up(u):
        codes[u] = swap_lon(stages.lat_up(u[1], arrived[u], lat, first_gain))

    def middle(u):
        priors[u], norms[u], v = stages.residual(
            u[1], codes[u], 1.0 / first_gain, lon_up, lon_down, observed, mask
        )
        sent[u] = swap_lon(v)

    def lower(u):
        s, c = u
        down[s] = stages.lat_down(c, sent[u], lat_t, down.get(s, ()))

    up(first)
    middle(first)
    arrived[third] = swap_tm(wait(waves[third]))
    up(second)
    lower(first)
    arrived[fourth] = swap_tm(wait(waves[fourth]))
    middle(second)
    up(third)
    lower(second)
    down[0] = swap_tm(wait(down[0][0]))
    up(fourth)
    middle(third)
    lower(third)
    middle(fourth)
    lower(fourth)
    down[1] = swap_tm(down[1][0])

    sums = []
    for s in range(2):
        sums.append(sum(jnp.sum(norms[u]) for u in units if u[0] == s))
        pieces, bending = stages.over_hours(down[s], kern, 1 if s == 0 else HALVES)
        sums.append(jnp.sum(bending))
        if s == 0:
            arrived[first] = arrived[second] = swap_tm(pieces[0])
        else:
            waves[third], waves[fourth] = pieces
    sums = add_over_tm(jnp.broadcast_to(jnp.stack(sums)[:, None], (4, 128)), zs)
    arrived[third] = swap_tm(wait(waves[third], sums))
    sums = add_over_lon(sums, qs)[:, 0]
    gains, steps = [], []
    for s in range(2):
        norm_sq, bending = sums[2 * s], sums[2 * s + 1]
        bound = SPECTRUM_MAX * lat_row_norm * lat_norm * lon_col_norm * jnp.sqrt(norm_sq)
        gains.append(CODE_MAX / jnp.maximum(bound, 1e-30))
        steps.append(norm_sq / (bending + NOISE_VAR * norm_sq))
    earlier = ()

    def back(u):
        s, c = u
        codes[u] = swap_lon(stages.lat_up(c, arrived[u], lat, gains[s]))

    def end(u):
        s, c = u
        return stages.finish(
            s, c, codes[u], 1.0 / gains[s], steps[s], lon_up, priors[u], observed, mask, earlier
        )

    back(first)
    back(second)
    earlier = end(first)
    arrived[fourth] = swap_tm(wait(waves[fourth]))
    back(third)
    earlier = end(second)
    earlier = end(third)
    back(fourth)
    earlier = end(fourth)
    return stages.joined(earlier)


def solution(mesh):
    return jax.shard_map(
        shards,
        mesh=mesh,
        in_specs=(
            P(None, "tm", "lon", None),
            P("tm", "lon", None),
            P("tm", "lon", None),
            P(),
            P("lon", None),
            P(),
        ),
        out_specs=(P(None, "tm", "lon", None), P(None, "tm", "lon", None)),
        check_vma=False,
    )
```

```python
import functools
import jax
import jax.numpy as jnp
from jax import lax
from jax.experimental import pallas as pl
from jax.experimental.pallas import tpu as pltpu
from jax.sharding import PartitionSpec as P

F32, BF16, I16, I32 = jnp.float32, jnp.bfloat16, jnp.int16, jnp.int32
EXACT, HIGH = lax.Precision.HIGHEST, lax.Precision.HIGH
NOISE_VAR = 0.25
SPECTRUM_MAX = 4.0
HOURLY_MAX = 400.0
STEPS = 1024.0
LEAST = -18.0
CODE_MAX = 2.0**13.5
GROUP = 16
HALVES = 2
EASE = 4
BACK_EASE = 4
VMEM = 52 * 1024 * 1024


def encode(x):
    size = jnp.maximum(jnp.abs(x), 2.0**LEAST)
    code = (jnp.log(size) * (STEPS / 0.6931471805599453) + (0.5 - STEPS * LEAST)).astype(I32)
    return jnp.where(x < 0, -code, code).astype(I16)


def decode(code):
    wide = code.astype(I32)
    size = jnp.exp2(jnp.abs(wide).astype(F32) * (1.0 / STEPS) + LEAST)
    size = jnp.where(wide == 0, 0.0, size)
    return jnp.where(wide < 0, -size, size)


def dot(a, b):
    return jnp.dot(a, b, preferred_element_type=F32)


def dot_rows(a, b):
    return lax.dot_general(a, b, (((1,), (1,)), ((), ())), preferred_element_type=F32)


def two_part_dot(a, b):
    top = a.astype(BF16)
    rest = (a - top.astype(F32)).astype(BF16)
    both = dot(jnp.concatenate([top, rest], axis=0), b)
    return both[: a.shape[0]] + both[a.shape[0] :]


def fold(x):
    rows, cols = x.shape
    x = jnp.sum(x.reshape(rows // 8, 8, cols), axis=0)
    total = x[:, :128]
    for start in range(128, cols, 128):
        total = total + x[:, start : start + 128]
    return total


def whole_spec(shape):
    return pl.BlockSpec(shape, lambda i: (0,) * len(shape))


SCALARS = pl.BlockSpec(memory_space=pltpu.SMEM)
ANYWHERE = pl.BlockSpec(memory_space=pl.ANY)


def struct(shape, kind):
    return jax.ShapeDtypeStruct(shape, kind)


class Kernels:
    def __init__(self, zs, qs, hour_local, lat_local, lat_rows, lon_local):
        self.zs, self.qs = zs, qs
        self.al, self.lr, self.ol = lat_local, lat_rows, lon_local
        self.hl = hour_local
        self.hp = hour_local // HALVES
        self.hours, self.lats, self.lons = zs * hour_local, zs * lat_local, qs * lon_local
        self.cells = self.hp * lat_rows * self.lons
        self.token = None
        self.ease = EASE

    def call(self, body, name, grid, out_shape, in_specs, out_specs, flops, moved, scratch=(), aliases={}):
        tokens = [] if self.token is None else [self.token]

        def run(*args):
            def whole(*refs):
                refs = list(refs)
                del refs[len(args) : len(args) + len(tokens)]
                place = len(args) + len(out_shape)
                token_ref = refs.pop(place)
                token_ref[...] = jnp.zeros_like(token_ref)
                body(*refs)

            out = pl.pallas_call(
                whole,
                name=name,
                grid=(grid,),
                out_shape=list(out_shape) + [struct((8, 128), F32)],
                in_specs=list(in_specs) + [ANYWHERE] * len(tokens),
                out_specs=list(out_specs) + [whole_spec((8, 128))],
                scratch_shapes=list(scratch),
                input_output_aliases=aliases,
                compiler_params=pltpu.CompilerParams(vmem_limit_bytes=VMEM),
                cost_estimate=pl.CostEstimate(flops=flops * self.ease, bytes_accessed=moved * self.ease, transcendentals=0),
            )(*args, *tokens)
            self.token = out[-1]
            return out[:-1]

        return run

    def after(self, x, token=None):
        return pl.pallas_call(
            lambda x_ref, token_ref, out_ref: None,
            name="after",
            out_shape=struct(x.shape, x.dtype),
            in_specs=[ANYWHERE, ANYWHERE],
            out_specs=ANYWHERE,
            input_output_aliases={0: 0},
            compiler_params=pltpu.CompilerParams(vmem_limit_bytes=VMEM),
            cost_estimate=pl.CostEstimate(flops=0, bytes_accessed=0, transcendentals=0),
        )(x, self.token if token is None else token)

    def parts_specs(self, group):
        return [pl.BlockSpec((group, self.lr, self.ol), lambda i: (i, 0, 0))] * self.qs

    def parts_shape(self, kind, size=None):
        return [struct((size or self.hp, self.lr, self.ol), kind)] * self.qs

    def grid_spec(self, group, start=0):
        offset = start // group
        return pl.BlockSpec((group, self.lr, self.lons), lambda i: (i + offset, 0, 0))

    def hourly(self, noise, tables):
        zs, hp, al, ol, hours = self.zs, self.hp, self.al, self.ol, self.hours
        periods = noise.shape[3]

        def body(noise_ref, table_ref, *refs):
            outs, turned = refs[:HALVES], refs[HALVES]
            for start in range(0, GROUP, 4):
                part = noise_ref[:, start : start + 4].reshape(2, 4 * ol, periods)
                total = dot_rows(table_ref[0], part[0]) + dot_rows(table_ref[1], part[1])
                for k in range(4):
                    turned[pl.ds(start + k, hours, stride=GROUP), :] = total[:, k * ol : (k + 1) * ol]
            value = turned[...].reshape(zs, HALVES, hp, GROUP, ol).astype(BF16)
            for c in range(HALVES):
                outs[c][...] = value[:, c]

        return self.call(
            body, "hourly", al // GROUP, [struct((zs, hp, al, ol), BF16)] * HALVES,
            [pl.BlockSpec((2, GROUP, ol, periods), lambda i: (0, i, 0, 0)), whole_spec(tables.shape)],
            [pl.BlockSpec((zs, hp, GROUP, ol), lambda i: (0, 0, i, 0))] * HALVES,
            4 * hours * periods * al * ol, 2 * noise.size + 2 * hours * al * ol,
            [pltpu.VMEM((hours * GROUP, ol), F32)],
        )(noise, tables)

    def lat_up(self, start, size, g, lat, gain):
        zs, qs, lr, ol, lats = self.zs, self.qs, self.lr, self.ol, self.lats
        cells = size * lr * self.lons
        group = 8
        offset = start // group

        def body(gain_ref, g_ref, lat_ref, *outs):
            for h in range(0, group, 4):
                part = [g_ref[:, h + k].reshape(lats, ol) for k in range(4)]
                total = dot(lat_ref[...], jnp.concatenate(part, axis=1))
                code = encode(total * gain_ref[0])
                for k in range(4):
                    for d in range(qs):
                        outs[d][h + k] = code[d * lr : (d + 1) * lr, k * ol : (k + 1) * ol]

        return self.call(
            body, "lat_up", size // group, self.parts_shape(I16, size),
            [SCALARS, pl.BlockSpec((zs, group, self.al, ol), lambda i: (0, i + offset, 0, 0)), whole_spec(lat.shape)],
            self.parts_specs(group), 2 * cells * self.lats, 4 * cells,
        )(gain.reshape(1), g, lat)

    def residual(self, c, codes, back, lon_up, lon_down, observed, mask):
        qs, hp, lr, ol, lons = self.qs, self.hp, self.lr, self.ol, self.lons
        group = 8
        rows = group * lr

        def body(back_ref, *refs):
            arrived, (up_ref, down_ref, observed_ref, mask_ref) = refs[:qs], refs[qs : qs + 4]
            prior_ref, norm_ref, outs = refs[qs + 4], refs[qs + 5], refs[qs + 6 :]
            x = jnp.concatenate([decode(a[...].reshape(rows, ol)) for a in arrived], axis=1)
            prior = two_part_dot(x, up_ref[...]) * back_ref[0]
            prior_ref[...] = prior.reshape(group, lr, lons)
            seen = mask_ref[...].reshape(rows, lons).astype(F32)
            resid = seen * (observed_ref[...].reshape(rows, lons) - prior)

            @pl.when(pl.program_id(0) == 0)
            def _():
                norm_ref[...] = jnp.zeros_like(norm_ref)

            norm_ref[...] += fold(resid * resid)
            v = two_part_dot(resid, down_ref[...]).astype(BF16)
            for d in range(qs):
                outs[d][...] = v[:, d * ol : (d + 1) * ol].reshape(group, lr, ol)

        out = self.call(
            body, "residual", hp // group,
            [struct((hp, lr, lons), F32), struct((8, 128), F32)] + self.parts_shape(BF16),
            [SCALARS] + self.parts_specs(group) + [whole_spec(lon_up.shape)] * 2 + [self.grid_spec(group, c * hp)] * 2,
            [self.grid_spec(group), whole_spec((8, 128))] + self.parts_specs(group),
            8 * self.cells * lons, 16 * self.cells,
        )(back.reshape(1), *codes, lon_up, lon_down, observed, mask)
        return out[0], out[1], out[2:]

    def lat_down(self, c, v, lat_t, whole, earlier):
        zs, qs, hp, al, lr, ol, lats = self.zs, self.qs, self.hp, self.al, self.lr, self.ol, self.lats

        offset = c * (hp // GROUP) if whole else 0
        size = self.hl if whole else hp

        def body(*refs):
            sent, lat_ref, (out_ref, turned) = refs[:qs], refs[qs], refs[-2:]
            for start in range(0, GROUP, 4):
                part = [jnp.concatenate([s[start + k] for s in sent], axis=0) for k in range(4)]
                total = dot(lat_ref[...], jnp.concatenate(part, axis=1))
                for k in range(4):
                    turned[pl.ds(start + k, lats, stride=GROUP), :] = total[:, k * ol : (k + 1) * ol]
            out_ref[...] = turned[...].reshape(zs, al, GROUP, ol).astype(BF16)

        return self.call(
            body, "lat_down", hp // GROUP, [struct((zs, al, size, ol), BF16)],
            self.parts_specs(GROUP) + [whole_spec(lat_t.shape)] + [ANYWHERE] * len(earlier),
            [pl.BlockSpec((zs, al, GROUP, ol), lambda i: (0, 0, i + offset, 0))],
            2 * self.cells * lats, 4 * self.cells,
            [pltpu.VMEM((lats * GROUP, ol), F32)], {qs + 1: 0} if earlier else {},
        )(*v, lat_t, *earlier)

    def over_hours(self, xs, kern, pieces):
        zs, hl, al, ol, hours = self.zs, self.hl, self.al, self.ol, self.hours
        count = len(xs)

        def body(*refs):
            arrived, kern_ref, refs = refs[:count], refs[count], refs[count + 1 :]
            outs, (bend_ref, turned) = refs[: len(pieces)], refs[len(pieces) :]

            @pl.when(pl.program_id(0) == 0)
            def _():
                bend_ref[...] = jnp.zeros_like(bend_ref)

            for start in range(0, GROUP, 4):
                part = []
                for k in range(4):
                    rows = [x[z, start + k] for z in range(zs) for x in arrived]
                    part.append(jnp.concatenate(rows, axis=0))
                part = jnp.concatenate(part, axis=1)
                total = dot(kern_ref[0], part) + dot(kern_ref[1], part)
                bend_ref[...] += fold(total * part.astype(F32))
                for k in range(4):
                    turned[pl.ds(start + k, hours, stride=GROUP), :] = total[:, k * ol : (k + 1) * ol]
            value = turned[...].reshape(zs, hl, GROUP, ol).astype(BF16)
            for out_ref, (first, size) in zip(outs, pieces):
                out_ref[...] = value[:, first : first + size]

        out = self.call(
            body, "over_hours", al // GROUP, [struct((zs, size, al, ol), BF16) for _, size in pieces] + [struct((8, 128), F32)],
            [pl.BlockSpec((zs, GROUP, hl // count, ol), lambda i: (0, i, 0, 0))] * count + [whole_spec(kern.shape)],
            [pl.BlockSpec((zs, size, GROUP, ol), lambda i: (0, 0, i, 0)) for _, size in pieces]
            + [whole_spec((8, 128))],
            8 * self.cells * hours, 8 * self.cells,
            [pltpu.VMEM((hours * GROUP, ol), F32)],
        )(*xs, kern)
        return out[:-1], out[-1]

    def finish(self, s, first, size, codes, back, step, lon_up, prior, observed, mask, earlier):
        qs, hp, lr, ol, lons = self.qs, self.hp, self.lr, self.ol, self.lons
        cells = size * lr * lons
        group = 8
        rows = group * lr

        def body(scalar_ref, *refs):
            arrived, (up_ref, prior_ref, observed_ref, mask_ref) = refs[:qs], refs[qs : qs + 4]
            posterior_ref, next_ref = refs[-2:]
            x = jnp.concatenate([decode(a[...].reshape(rows, ol)) for a in arrived], axis=1)
            scaled = two_part_dot(x, up_ref[...]) * scalar_ref[0]
            prior = prior_ref[...].reshape(rows, lons)
            seen = mask_ref[...].reshape(rows, lons).astype(F32)
            resid = seen * (observed_ref[...].reshape(rows, lons) - prior)
            shape = (1, group, lr, lons)
            posterior_ref[...] = (prior + scaled).reshape(shape)
            next_ref[...] = (resid - seen * scaled - scalar_ref[1] * resid).reshape(shape)

        full = struct((2, self.hl, lr, lons), F32)
        offset = first // group
        out_spec = pl.BlockSpec((1, group, lr, lons), lambda i: (s, i + offset, 0, 0))
        count = 1 + qs + 4
        return self.call(
            body, "finish", size // group, [full, full],
            [SCALARS] + self.parts_specs(group) + [whole_spec(lon_up.shape), self.grid_spec(group, first % hp)]
            + [self.grid_spec(group, first)] * 2 + [ANYWHERE] * len(earlier),
            [out_spec, out_spec], 4 * cells * lons, 22 * cells,
            aliases={count + i: i for i in range(len(earlier))},
        )(jnp.stack([back * step, NOISE_VAR * step]), *codes, lon_up, prior, observed, mask, *earlier)

    def joined(self, earlier):
        return tuple(earlier)


class Plain(Kernels):
    def after(self, x, token=None):
        return x

    def hourly(self, noise, tables):
        h = jnp.einsum("cyxk,cjk->jyx", noise, tables, preferred_element_type=F32).astype(BF16)
        h = h.reshape(self.zs, HALVES, self.hp, self.al, self.ol)
        return [h[:, c] for c in range(HALVES)]

    def lat_up(self, start, size, g, lat, gain):
        g = g[:, start : start + size]
        split = lat.reshape(self.qs, self.lr, self.zs, self.al)
        x = encode(jnp.einsum("qlzy,zhyx->qhlx", split, g, preferred_element_type=F32) * gain)
        return [x[d] for d in range(self.qs)]

    def up(self, codes, lon_up):
        x = jnp.concatenate([decode(c) for c in codes], axis=2)
        return jnp.einsum("hlx,xo->hlo", x, lon_up.astype(F32), precision=HIGH)

    def residual(self, c, codes, back, lon_up, lon_down, observed, mask):
        prior = self.up(codes, lon_up) * back
        here = slice(c * self.hp, (c + 1) * self.hp)
        resid = mask[here].astype(F32) * (observed[here] - prior)
        v = jnp.einsum("hlo,op->hlp", resid, lon_down.astype(F32), precision=HIGH).astype(BF16)
        return prior, jnp.sum(resid * resid), jnp.split(v, self.qs, axis=2)

    def lat_down(self, c, v, lat_t, whole, earlier):
        split = lat_t.reshape(self.zs, self.al, self.qs, self.lr)
        x = jnp.einsum("zyql,qhlx->zyhx", split, jnp.stack(v), preferred_element_type=F32)
        return (jnp.concatenate(list(earlier) + [x.astype(BF16)], axis=2),)

    def over_hours(self, xs, kern, pieces):
        x = jnp.concatenate(xs, axis=2)
        x = jnp.swapaxes(x, 0, 1).reshape(self.al, self.hours, self.ol).astype(F32)
        y = jnp.einsum("gk,ykx->gyx", kern.astype(F32).sum(0), x, precision=HIGH)
        bend = jnp.einsum("gyx,ygx->", y, x)
        y = y.astype(BF16).reshape(self.zs, self.hl, self.al, self.ol)
        return [y[:, first : first + size] for first, size in pieces], bend

    def finish(self, s, first, size, codes, back, step, lon_up, prior, observed, mask, earlier):
        scaled = self.up(codes, lon_up) * (back * step)
        here = slice(first, first + size)
        prior = prior[first % self.hp : first % self.hp + size]
        seen = mask[here].astype(F32)
        resid = seen * (observed[here] - prior)
        return tuple(earlier) + ((s, prior + scaled, resid - seen * scaled - NOISE_VAR * step * resid),)

    def joined(self, earlier):
        samples = [[e[1:] for e in earlier if e[0] == s] for s in range(2)]
        return tuple(jnp.stack([jnp.concatenate([e[i] for e in part]) for part in samples]) for i in range(2))


def swap_tm(x):
    return lax.all_to_all(x, "tm", split_axis=0, concat_axis=0, tiled=True)


def swap_lon(parts):
    count = len(parts)
    return [parts[0]] + [
        lax.ppermute(parts[d], "lon", [(i, i ^ d) for i in range(count)]) for d in range(1, count)
    ]


def add_over_tm(x, count):
    return sum([lax.ppermute(x, "tm", [(i, i ^ d) for i in range(count)]) for d in range(1, count)], x)


def add_over_lon(x, count):
    d = 1
    while d < count:
        x = x + lax.ppermute(x, "lon", [(i, i ^ d) for i in range(count)])
        d *= 2
    return x


def largest_norm(factor, axis):
    return jnp.sqrt(jnp.max(jnp.sum(jnp.square(factor.astype(F32)), axis=axis)))


def shards(noise, observed, mask, lat_factor, lon_factor, spectrum):
    _, lat_local, lon_local, periods = noise.shape
    hour_local, lat_rows, lon_count = observed.shape
    hours = periods // 2
    hour_part = hour_local // HALVES
    zs, qs = hours // hour_local, lon_count // lon_local
    lat_count = zs * lat_local
    fits = lon_local % 128 == 0 and lat_rows % 16 == 0
    fits = fits and lat_local % GROUP == 0 and hour_part % GROUP == 0
    stages = (Kernels if fits else Plain)(zs, qs, hour_local, lat_local, lat_rows, lon_local)
    order = lax.axis_index("lon") ^ jnp.arange(qs)

    powers = jnp.concatenate([spectrum, spectrum[1:-1][::-1]])
    amplitude = jnp.sqrt(powers / periods)
    clock = jnp.arange(hours)[:, None]
    phase = (clock * jnp.arange(periods) % periods).astype(F32) * (2.0 * jnp.pi / periods)
    cosine_tab, sine_tab = jnp.cos(phase), jnp.sin(phase)
    table_cos = (cosine_tab * amplitude).astype(BF16)
    table_sin = (sine_tab * amplitude).astype(BF16)
    tables = (jnp.stack([table_cos, table_sin]), jnp.stack([-table_sin, table_cos]))

    def hour_kernel():
        scaled = powers / periods
        kern = jnp.dot(cosine_tab * scaled, cosine_tab.T, precision=EXACT) + jnp.dot(
            sine_tab * scaled, sine_tab.T, precision=EXACT
        )
        top = lax.reduce_precision(kern, 8, 7)
        return jnp.stack([top.astype(BF16), (kern - top).astype(BF16)])

    lon = lax.all_gather(lon_factor, "lon", axis=0, tiled=True).reshape(lon_count, qs, lon_local)
    units = [(s, c) for s in range(2) for c in range(HALVES)]
    first, second, third, fourth = units
    wait = stages.after
    arrived, waves = {}, {}
    for s in range(2):
        for c, part in enumerate(stages.hourly(noise, tables[s])):
            waves[s, c] = part
    arrived[first] = swap_tm(waves[first])
    arrived[second] = swap_tm(wait(waves[second]))
    kern = hour_kernel()
    lon_down = jnp.take(lon, order, axis=1).reshape(lon_count, lon_count)
    lon_up = lon_down.T
    lat = jnp.take(lat_factor.reshape(qs, lat_rows, lat_count), order, axis=0)
    lat = lat.reshape(lat_count, lat_count)
    lat_t = lat.T
    lat_row_norm = largest_norm(lat_factor, 1)
    lon_col_norm = largest_norm(lon_down, 0)
    lat_norm = jnp.sqrt(jnp.sum(jnp.square(lat_factor.astype(F32))))
    first_gain = CODE_MAX / jnp.maximum(lat_row_norm * (lat_count**0.5 * HOURLY_MAX), 1e-30)
    codes, priors, norms, sent, down = {}, {}, {}, {}, {}

    def up(u):
        codes[u] = swap_lon(stages.lat_up(0, hour_part, arrived[u], lat, first_gain))

    def middle(u):
        priors[u], norms[u], v = stages.residual(
            u[1], codes[u], 1.0 / first_gain, lon_up, lon_down, observed, mask
        )
        sent[u] = swap_lon(v)

    def lower(u):
        down[u] = stages.lat_down(u[1], sent[u], lat_t, u[0] == 0, down[first] if u == second else ())

    up(first)
    middle(first)
    arrived[third] = swap_tm(wait(waves[third]))
    up(second)
    lower(first)
    arrived[fourth] = swap_tm(wait(waves[fourth]))
    middle(second)
    up(third)
    lower(second)
    down[second] = swap_tm(wait(down[second][0]))
    up(fourth)
    middle(third)
    lower(third)
    middle(fourth)
    down[third] = swap_tm(wait(down[third][0]))
    early, bending = stages.over_hours([down[second]], kern, [(0, hour_part), (hour_part, hour_part)])
    sums = [sum(jnp.sum(norms[u]) for u in units if u[0] == s) for s in range(2)] + [jnp.sum(bending)]
    lower(fourth)
    down[fourth] = swap_tm(down[fourth][0])
    early = list(early)
    early[0] = swap_tm(early[0])

    quarter = hour_part // 2
    pieces = [(0, hour_part), (hour_part, quarter), (hour_part + quarter, hour_part - quarter)]
    late, bending = stages.over_hours([down[third], down[fourth]], kern, pieces)
    sums.append(jnp.sum(bending))
    sums = add_over_tm(jnp.broadcast_to(jnp.stack(sums)[:, None], (4, 128)), zs)
    late = list(late)
    early[1] = swap_tm(wait(early[1], sums))
    sums = add_over_lon(sums, qs)[:, 0]
    gains, steps = [], []
    for s in range(2):
        norm_sq, bending = sums[s], sums[2 + s]
        bound = SPECTRUM_MAX * lat_row_norm * lat_norm * lon_col_norm * jnp.sqrt(norm_sq)
        gains.append(CODE_MAX / jnp.maximum(bound, 1e-30))
        steps.append(norm_sq / (bending + NOISE_VAR * norm_sq))
    earlier = ()

    stages.ease = BACK_EASE

    def back(s, start, size, g):
        return swap_lon(stages.lat_up(start, size, g, lat, gains[s]))

    def end(s, start, size, codes):
        prior = priors[s, start // hour_part]
        return stages.finish(
            s, start, size, codes, 1.0 / gains[s], steps[s], lon_up, prior, observed, mask, earlier
        )

    codes = back(0, 0, hour_part, early[0])
    earlier = end(0, 0, hour_part, codes)
    late[0] = swap_tm(wait(late[0]))
    codes = back(0, 0, hour_part, early[1])
    earlier = end(0, hour_part, hour_part, codes)
    late[1] = swap_tm(wait(late[1]))
    codes = back(1, 0, hour_part, late[0])
    earlier = end(1, *pieces[0], codes)
    late[2] = swap_tm(wait(late[2]))
    codes = back(1, 0, pieces[1][1], late[1])
    earlier = end(1, *pieces[1], codes)
    codes = back(1, 0, pieces[2][1], late[2])
    earlier = end(1, *pieces[2], codes)
    return stages.joined(earlier)


def solution(mesh):
    return jax.shard_map(
        shards,
        mesh=mesh,
        in_specs=(
            P(None, "tm", "lon", None),
            P("tm", "lon", None),
            P("tm", "lon", None),
            P(),
            P("lon", None),
            P(),
        ),
        out_specs=(P(None, "tm", "lon", None), P(None, "tm", "lon", None)),
        check_vma=False,
    )
```

```python
import functools
import jax
import jax.numpy as jnp
from jax import lax
from jax.experimental import pallas as pl
from jax.experimental.pallas import tpu as pltpu
from jax.sharding import PartitionSpec as P

F32, BF16, I16, I32 = jnp.float32, jnp.bfloat16, jnp.int16, jnp.int32
EXACT, HIGH = lax.Precision.HIGHEST, lax.Precision.HIGH
NOISE_VAR = 0.25
SPECTRUM_MAX = 4.0
HOURLY_MAX = 400.0
STEPS = 1024.0
LEAST = -18.0
CODE_MAX = 2.0**13.5
GROUP = 16
HALVES = 2
VMEM = 52 * 1024 * 1024


def encode(x):
    size = jnp.maximum(jnp.abs(x), 2.0**LEAST)
    code = (jnp.log(size) * (STEPS / 0.6931471805599453) + (0.5 - STEPS * LEAST)).astype(I32)
    return jnp.where(x < 0, -code, code).astype(I16)


def decode(code):
    wide = code.astype(I32)
    size = jnp.exp2(jnp.abs(wide).astype(F32) * (1.0 / STEPS) + LEAST)
    size = jnp.where(wide == 0, 0.0, size)
    return jnp.where(wide < 0, -size, size)


def dot(a, b):
    return jnp.dot(a, b, preferred_element_type=F32)


def dot_rows(a, b):
    return lax.dot_general(a, b, (((1,), (1,)), ((), ())), preferred_element_type=F32)


def two_part_dot(a, b):
    top = a.astype(BF16)
    rest = (a - top.astype(F32)).astype(BF16)
    both = dot(jnp.concatenate([top, rest], axis=0), b)
    return both[: a.shape[0]] + both[a.shape[0] :]


def fold(x):
    rows, cols = x.shape
    x = jnp.sum(x.reshape(rows // 8, 8, cols), axis=0)
    total = x[:, :128]
    for start in range(128, cols, 128):
        total = total + x[:, start : start + 128]
    return total


def whole_spec(shape):
    return pl.BlockSpec(shape, lambda i: (0,) * len(shape))


SCALARS = pl.BlockSpec(memory_space=pltpu.SMEM)
ANYWHERE = pl.BlockSpec(memory_space=pl.ANY)


def struct(shape, kind):
    return jax.ShapeDtypeStruct(shape, kind)


class Kernels:
    def __init__(self, zs, qs, hour_local, lat_local, lat_rows, lon_local):
        self.zs, self.qs = zs, qs
        self.al, self.lr, self.ol = lat_local, lat_rows, lon_local
        self.hl = hour_local
        self.hp = hour_local // HALVES
        self.hours, self.lats, self.lons = zs * hour_local, zs * lat_local, qs * lon_local
        self.cells = self.hp * lat_rows * self.lons
        self.token = None
        self.ease = 1

    def call(self, body, name, grid, out_shape, in_specs, out_specs, flops, moved, scratch=(), aliases={}):
        tokens = [] if self.token is None else [self.token]

        def run(*args):
            def whole(*refs):
                refs = list(refs)
                del refs[len(args) : len(args) + len(tokens)]
                place = len(args) + len(out_shape)
                token_ref = refs.pop(place)
                token_ref[...] = jnp.zeros_like(token_ref)
                body(*refs)

            out = pl.pallas_call(
                whole,
                name=name,
                grid=(grid,),
                out_shape=list(out_shape) + [struct((8, 128), F32)],
                in_specs=list(in_specs) + [ANYWHERE] * len(tokens),
                out_specs=list(out_specs) + [whole_spec((8, 128))],
                scratch_shapes=list(scratch),
                input_output_aliases=aliases,
                compiler_params=pltpu.CompilerParams(vmem_limit_bytes=VMEM),
                cost_estimate=pl.CostEstimate(flops=flops * self.ease, bytes_accessed=moved * self.ease, transcendentals=0),
            )(*args, *tokens)
            self.token = out[-1]
            return out[:-1]

        return run

    def after(self, x, *tokens):
        tokens = [self.token, *tokens]
        return pl.pallas_call(
            lambda *refs: None,
            name="after",
            out_shape=struct(x.shape, x.dtype),
            in_specs=[ANYWHERE] * (1 + len(tokens)),
            out_specs=ANYWHERE,
            input_output_aliases={0: 0},
            compiler_params=pltpu.CompilerParams(vmem_limit_bytes=VMEM),
            cost_estimate=pl.CostEstimate(flops=0, bytes_accessed=0, transcendentals=0),
        )(x, *tokens)

    def parts_specs(self, group):
        return [pl.BlockSpec((group, self.lr, self.ol), lambda i: (i, 0, 0))] * self.qs

    def parts_shape(self, kind, size=None):
        return [struct((size or self.hp, self.lr, self.ol), kind)] * self.qs

    def grid_spec(self, group, start=0):
        offset = start // group
        return pl.BlockSpec((group, self.lr, self.lons), lambda i: (i + offset, 0, 0))

    def hourly(self, noise, tables):
        zs, hp, al, ol, hours = self.zs, self.hp, self.al, self.ol, self.hours
        periods = noise.shape[3]

        def body(noise_ref, table_ref, *refs):
            outs, turned = refs[:HALVES], refs[HALVES]
            for start in range(0, GROUP, 4):
                part = noise_ref[:, start : start + 4].reshape(2, 4 * ol, periods)
                total = dot_rows(table_ref[0], part[0]) + dot_rows(table_ref[1], part[1])
                for k in range(4):
                    turned[pl.ds(start + k, hours, stride=GROUP), :] = total[:, k * ol : (k + 1) * ol]
            value = turned[...].reshape(zs, HALVES, hp, GROUP, ol).astype(BF16)
            for c in range(HALVES):
                outs[c][...] = value[:, c]

        return self.call(
            body, "hourly", al // GROUP, [struct((zs, hp, al, ol), BF16)] * HALVES,
            [pl.BlockSpec((2, GROUP, ol, periods), lambda i: (0, i, 0, 0)), whole_spec(tables.shape)],
            [pl.BlockSpec((zs, hp, GROUP, ol), lambda i: (0, 0, i, 0))] * HALVES,
            4 * hours * periods * al * ol, 2 * noise.size + 2 * hours * al * ol,
            [pltpu.VMEM((hours * GROUP, ol), F32)],
        )(noise, tables)

    def lat_up(self, start, size, g, lat, gain):
        zs, qs, lr, ol, lats = self.zs, self.qs, self.lr, self.ol, self.lats
        cells = size * lr * self.lons
        group = 8
        offset = start // group

        def body(gain_ref, g_ref, lat_ref, *outs):
            for h in range(0, group, 4):
                part = [g_ref[:, h + k].reshape(lats, ol) for k in range(4)]
                total = dot(lat_ref[...], jnp.concatenate(part, axis=1))
                code = encode(total * gain_ref[0])
                for k in range(4):
                    for d in range(qs):
                        outs[d][h + k] = code[d * lr : (d + 1) * lr, k * ol : (k + 1) * ol]

        return self.call(
            body, "lat_up", size // group, self.parts_shape(I16, size),
            [SCALARS, pl.BlockSpec((zs, group, self.al, ol), lambda i: (0, i + offset, 0, 0)), whole_spec(lat.shape)],
            self.parts_specs(group), 2 * cells * self.lats, 4 * cells,
        )(gain.reshape(1), g, lat)

    def residual(self, c, codes, back, lon_up, lon_down, observed, mask):
        qs, hp, lr, ol, lons = self.qs, self.hp, self.lr, self.ol, self.lons
        group = 8
        rows = group * lr

        def body(back_ref, *refs):
            arrived, (up_ref, down_ref, observed_ref, mask_ref) = refs[:qs], refs[qs : qs + 4]
            prior_ref, norm_ref, outs = refs[qs + 4], refs[qs + 5], refs[qs + 6 :]
            x = jnp.concatenate([decode(a[...].reshape(rows, ol)) for a in arrived], axis=1)
            prior = two_part_dot(x, up_ref[...]) * back_ref[0]
            prior_ref[...] = prior.reshape(group, lr, lons)
            seen = mask_ref[...].reshape(rows, lons).astype(F32)
            resid = seen * (observed_ref[...].reshape(rows, lons) - prior)

            @pl.when(pl.program_id(0) == 0)
            def _():
                norm_ref[...] = jnp.zeros_like(norm_ref)

            norm_ref[...] += fold(resid * resid)
            v = two_part_dot(resid, down_ref[...]).astype(BF16)
            for d in range(qs):
                outs[d][...] = v[:, d * ol : (d + 1) * ol].reshape(group, lr, ol)

        out = self.call(
            body, "residual", hp // group,
            [struct((hp, lr, lons), F32), struct((8, 128), F32)] + self.parts_shape(BF16),
            [SCALARS] + self.parts_specs(group) + [whole_spec(lon_up.shape)] * 2 + [self.grid_spec(group, c * hp)] * 2,
            [self.grid_spec(group), whole_spec((8, 128))] + self.parts_specs(group),
            8 * self.cells * lons, 16 * self.cells,
        )(back.reshape(1), *codes, lon_up, lon_down, observed, mask)
        return out[0], out[1], out[2:]

    def lat_down(self, c, v, lat_t, whole, earlier):
        zs, qs, hp, al, lr, ol, lats = self.zs, self.qs, self.hp, self.al, self.lr, self.ol, self.lats

        offset = c * (hp // GROUP) if whole else 0
        size = self.hl if whole else hp

        def body(*refs):
            sent, lat_ref, (out_ref, turned) = refs[:qs], refs[qs], refs[-2:]
            for start in range(0, GROUP, 4):
                part = [jnp.concatenate([s[start + k] for s in sent], axis=0) for k in range(4)]
                total = dot(lat_ref[...], jnp.concatenate(part, axis=1))
                for k in range(4):
                    turned[pl.ds(start + k, lats, stride=GROUP), :] = total[:, k * ol : (k + 1) * ol]
            out_ref[...] = turned[...].reshape(zs, al, GROUP, ol).astype(BF16)

        return self.call(
            body, "lat_down", hp // GROUP, [struct((zs, al, size, ol), BF16)],
            self.parts_specs(GROUP) + [whole_spec(lat_t.shape)] + [ANYWHERE] * len(earlier),
            [pl.BlockSpec((zs, al, GROUP, ol), lambda i: (0, 0, i + offset, 0))],
            2 * self.cells * lats, 4 * self.cells,
            [pltpu.VMEM((lats * GROUP, ol), F32)], {qs + 1: 0} if earlier else {},
        )(*v, lat_t, *earlier)

    def over_hours(self, xs, kern, pieces):
        zs, hl, al, ol, hours = self.zs, self.hl, self.al, self.ol, self.hours
        count = len(xs)

        def body(*refs):
            arrived, kern_ref, refs = refs[:count], refs[count], refs[count + 1 :]
            outs, (bend_ref, turned) = refs[: len(pieces)], refs[len(pieces) :]

            @pl.when(pl.program_id(0) == 0)
            def _():
                bend_ref[...] = jnp.zeros_like(bend_ref)

            for start in range(0, GROUP, 4):
                part = []
                for k in range(4):
                    rows = [x[z, start + k] for z in range(zs) for x in arrived]
                    part.append(jnp.concatenate(rows, axis=0))
                part = jnp.concatenate(part, axis=1)
                total = dot(kern_ref[0], part) + dot(kern_ref[1], part)
                bend_ref[...] += fold(total * part.astype(F32))
                for k in range(4):
                    turned[pl.ds(start + k, hours, stride=GROUP), :] = total[:, k * ol : (k + 1) * ol]
            value = turned[...].reshape(zs, hl, GROUP, ol).astype(BF16)
            for out_ref, (first, size) in zip(outs, pieces):
                out_ref[...] = value[:, first : first + size]

        out = self.call(
            body, "over_hours", al // GROUP, [struct((zs, size, al, ol), BF16) for _, size in pieces] + [struct((8, 128), F32)],
            [pl.BlockSpec((zs, GROUP, hl // count, ol), lambda i: (0, i, 0, 0))] * count + [whole_spec(kern.shape)],
            [pl.BlockSpec((zs, size, GROUP, ol), lambda i: (0, 0, i, 0)) for _, size in pieces]
            + [whole_spec((8, 128))],
            8 * self.cells * hours, 8 * self.cells,
            [pltpu.VMEM((hours * GROUP, ol), F32)],
        )(*xs, kern)
        return out[:-1], out[-1]

    def finish(self, s, first, size, codes, back, step, lon_up, prior, observed, mask, earlier):
        qs, hp, lr, ol, lons = self.qs, self.hp, self.lr, self.ol, self.lons
        cells = size * lr * lons
        group = 8
        rows = group * lr

        def body(scalar_ref, *refs):
            arrived, (up_ref, prior_ref, observed_ref, mask_ref) = refs[:qs], refs[qs : qs + 4]
            posterior_ref, next_ref = refs[-2:]
            x = jnp.concatenate([decode(a[...].reshape(rows, ol)) for a in arrived], axis=1)
            scaled = two_part_dot(x, up_ref[...]) * scalar_ref[0]
            prior = prior_ref[...].reshape(rows, lons)
            seen = mask_ref[...].reshape(rows, lons).astype(F32)
            resid = seen * (observed_ref[...].reshape(rows, lons) - prior)
            shape = (1, group, lr, lons)
            posterior_ref[...] = (prior + scaled).reshape(shape)
            next_ref[...] = (resid - seen * scaled - scalar_ref[1] * resid).reshape(shape)

        full = struct((2, self.hl, lr, lons), F32)
        offset = first // group
        out_spec = pl.BlockSpec((1, group, lr, lons), lambda i: (s, i + offset, 0, 0))
        count = 1 + qs + 4
        return self.call(
            body, "finish", size // group, [full, full],
            [SCALARS] + self.parts_specs(group) + [whole_spec(lon_up.shape), self.grid_spec(group, first % hp)]
            + [self.grid_spec(group, first)] * 2 + [ANYWHERE] * len(earlier),
            [out_spec, out_spec], 4 * cells * lons, 22 * cells,
            aliases={count + i: i for i in range(len(earlier))},
        )(jnp.stack([back * step, NOISE_VAR * step]), *codes, lon_up, prior, observed, mask, *earlier)

    def joined(self, earlier):
        return tuple(earlier)


class Plain(Kernels):
    def after(self, x, *tokens):
        return x

    def hourly(self, noise, tables):
        h = jnp.einsum("cyxk,cjk->jyx", noise, tables, preferred_element_type=F32).astype(BF16)
        h = h.reshape(self.zs, HALVES, self.hp, self.al, self.ol)
        return [h[:, c] for c in range(HALVES)]

    def lat_up(self, start, size, g, lat, gain):
        g = g[:, start : start + size]
        split = lat.reshape(self.qs, self.lr, self.zs, self.al)
        x = encode(jnp.einsum("qlzy,zhyx->qhlx", split, g, preferred_element_type=F32) * gain)
        return [x[d] for d in range(self.qs)]

    def up(self, codes, lon_up):
        x = jnp.concatenate([decode(c) for c in codes], axis=2)
        return jnp.einsum("hlx,xo->hlo", x, lon_up.astype(F32), precision=HIGH)

    def residual(self, c, codes, back, lon_up, lon_down, observed, mask):
        prior = self.up(codes, lon_up) * back
        here = slice(c * self.hp, (c + 1) * self.hp)
        resid = mask[here].astype(F32) * (observed[here] - prior)
        v = jnp.einsum("hlo,op->hlp", resid, lon_down.astype(F32), precision=HIGH).astype(BF16)
        return prior, jnp.sum(resid * resid), jnp.split(v, self.qs, axis=2)

    def lat_down(self, c, v, lat_t, whole, earlier):
        split = lat_t.reshape(self.zs, self.al, self.qs, self.lr)
        x = jnp.einsum("zyql,qhlx->zyhx", split, jnp.stack(v), preferred_element_type=F32)
        return (jnp.concatenate(list(earlier) + [x.astype(BF16)], axis=2),)

    def over_hours(self, xs, kern, pieces):
        x = jnp.concatenate(xs, axis=2)
        x = jnp.swapaxes(x, 0, 1).reshape(self.al, self.hours, self.ol).astype(F32)
        y = jnp.einsum("gk,ykx->gyx", kern.astype(F32).sum(0), x, precision=HIGH)
        bend = jnp.einsum("gyx,ygx->", y, x)
        y = y.astype(BF16).reshape(self.zs, self.hl, self.al, self.ol)
        return [y[:, first : first + size] for first, size in pieces], bend

    def finish(self, s, first, size, codes, back, step, lon_up, prior, observed, mask, earlier):
        scaled = self.up(codes, lon_up) * (back * step)
        here = slice(first, first + size)
        prior = prior[first % self.hp : first % self.hp + size]
        seen = mask[here].astype(F32)
        resid = seen * (observed[here] - prior)
        return tuple(earlier) + ((s, prior + scaled, resid - seen * scaled - NOISE_VAR * step * resid),)

    def joined(self, earlier):
        samples = [[e[1:] for e in earlier if e[0] == s] for s in range(2)]
        return tuple(jnp.stack([jnp.concatenate([e[i] for e in part]) for part in samples]) for i in range(2))


def swap_tm(x):
    return lax.all_to_all(x, "tm", split_axis=0, concat_axis=0, tiled=True)


def swap_lon(parts):
    count = len(parts)
    return [parts[0]] + [
        lax.ppermute(parts[d], "lon", [(i, i ^ d) for i in range(count)]) for d in range(1, count)
    ]


def add_over_tm(x, count):
    return sum([lax.ppermute(x, "tm", [(i, i ^ d) for i in range(count)]) for d in range(1, count)], x)


def add_over_lon(x, count):
    d = 1
    while d < count:
        x = x + lax.ppermute(x, "lon", [(i, i ^ d) for i in range(count)])
        d *= 2
    return x


def largest_norm(factor, axis):
    return jnp.sqrt(jnp.max(jnp.sum(jnp.square(factor.astype(F32)), axis=axis)))


def shards(noise, observed, mask, lat_factor, lon_factor, spectrum):
    _, lat_local, lon_local, periods = noise.shape
    hour_local, lat_rows, lon_count = observed.shape
    hours = periods // 2
    hour_part = hour_local // HALVES
    zs, qs = hours // hour_local, lon_count // lon_local
    lat_count = zs * lat_local
    fits = lon_local % 128 == 0 and lat_rows % 16 == 0
    fits = fits and lat_local % GROUP == 0 and hour_part % GROUP == 0
    stages = (Kernels if fits else Plain)(zs, qs, hour_local, lat_local, lat_rows, lon_local)
    order = lax.axis_index("lon") ^ jnp.arange(qs)

    powers = jnp.concatenate([spectrum, spectrum[1:-1][::-1]])
    amplitude = jnp.sqrt(powers / periods)
    clock = jnp.arange(hours)[:, None]
    phase = (clock * jnp.arange(periods) % periods).astype(F32) * (2.0 * jnp.pi / periods)
    cosine_tab, sine_tab = jnp.cos(phase), jnp.sin(phase)
    table_cos = (cosine_tab * amplitude).astype(BF16)
    table_sin = (sine_tab * amplitude).astype(BF16)
    tables = (jnp.stack([table_cos, table_sin]), jnp.stack([-table_sin, table_cos]))

    def hour_kernel():
        scaled = powers / periods
        kern = jnp.dot(cosine_tab * scaled, cosine_tab.T, precision=EXACT) + jnp.dot(
            sine_tab * scaled, sine_tab.T, precision=EXACT
        )
        top = lax.reduce_precision(kern, 8, 7)
        return jnp.stack([top.astype(BF16), (kern - top).astype(BF16)])

    lon = lax.all_gather(lon_factor, "lon", axis=0, tiled=True)
    units = [(s, c) for s in range(2) for c in range(HALVES)]
    lon_down = jnp.concatenate(
        [lax.dynamic_slice_in_dim(lon, order[d] * lon_local, lon_local, axis=1) for d in range(qs)], axis=1
    )
    lon_up = lon_down.T
    first, second, third, fourth = units
    wait = stages.after
    arrived, waves = {}, {}
    for s in range(2):
        for c, part in enumerate(stages.hourly(noise, tables[s])):
            waves[s, c] = part
    arrived[first] = swap_tm(waves[first])
    arrived[second] = swap_tm(wait(waves[second], lon_up, lon_down))
    kern = hour_kernel()
    lat = jnp.take(lat_factor.reshape(qs, lat_rows, lat_count), order, axis=0)
    lat = lat.reshape(lat_count, lat_count)
    lat_t = lat.T
    lat_row_norm = largest_norm(lat_factor, 1)
    lon_col_norm = largest_norm(lon_down, 0)
    lat_norm = jnp.sqrt(jnp.sum(jnp.square(lat_factor.astype(F32))))
    first_gain = CODE_MAX / jnp.maximum(lat_row_norm * (lat_count**0.5 * HOURLY_MAX), 1e-30)
    codes, priors, norms, sent, down = {}, {}, {}, {}, {}

    def up(u):
        codes[u] = swap_lon(stages.lat_up(0, hour_part, arrived[u], lat, first_gain))

    def middle(u):
        priors[u], norms[u], v = stages.residual(
            u[1], codes[u], 1.0 / first_gain, lon_up, lon_down, observed, mask
        )
        sent[u] = swap_lon(v)

    def lower(u):
        down[u] = stages.lat_down(u[1], sent[u], lat_t, u[0] == 0, down[first] if u == second else ())

    stages.ease = 1
    up(first)
    middle(first)
    stages.ease = 4
    arrived[third] = swap_tm(wait(waves[third]))
    up(second)
    lower(first)
    arrived[fourth] = swap_tm(wait(waves[fourth]))
    middle(second)
    up(third)
    lower(second)
    down[second] = swap_tm(wait(down[second][0]))
    up(fourth)
    middle(third)
    lower(third)
    middle(fourth)
    down[third] = swap_tm(wait(down[third][0]))
    early, bending = stages.over_hours([down[second]], kern, [(0, hour_part), (hour_part, hour_part)])
    sums = [sum(jnp.sum(norms[u]) for u in units if u[0] == s) for s in range(2)] + [jnp.sum(bending)]
    lower(fourth)
    down[fourth] = swap_tm(down[fourth][0])
    early = list(early)
    early[0] = swap_tm(early[0])

    quarter = hour_part // 2
    pieces = [(0, hour_part), (hour_part, quarter), (hour_part + quarter, hour_part - quarter)]
    late, bending = stages.over_hours([down[third], down[fourth]], kern, pieces)
    sums.append(jnp.sum(bending))
    sums = add_over_tm(jnp.broadcast_to(jnp.stack(sums)[:, None], (4, 128)), zs)
    late = list(late)
    early[1] = swap_tm(wait(early[1], sums))
    sums = add_over_lon(sums, qs)[:, 0]
    gains, steps = [], []
    for s in range(2):
        norm_sq, bending = sums[s], sums[2 + s]
        bound = SPECTRUM_MAX * lat_row_norm * lat_norm * lon_col_norm * jnp.sqrt(norm_sq)
        gains.append(CODE_MAX / jnp.maximum(bound, 1e-30))
        steps.append(norm_sq / (bending + NOISE_VAR * norm_sq))
    earlier = ()

    stages.ease = 2

    def back(s, start, size, g):
        return swap_lon(stages.lat_up(start, size, g, lat, gains[s]))

    def end(s, start, size, codes):
        prior = priors[s, start // hour_part]
        return stages.finish(
            s, start, size, codes, 1.0 / gains[s], steps[s], lon_up, prior, observed, mask, earlier
        )

    codes = back(0, 0, hour_part, early[0])
    earlier = end(0, 0, hour_part, codes)
    late[0] = swap_tm(wait(late[0]))
    codes = back(0, 0, hour_part, early[1])
    earlier = end(0, hour_part, hour_part, codes)
    late[1] = swap_tm(wait(late[1]))
    codes = back(1, 0, hour_part, late[0])
    earlier = end(1, *pieces[0], codes)
    late[2] = swap_tm(wait(late[2]))
    codes = back(1, 0, pieces[1][1], late[1])
    earlier = end(1, *pieces[1], codes)
    codes = back(1, 0, pieces[2][1], late[2])
    earlier = end(1, *pieces[2], codes)
    return stages.joined(earlier)


def solution(mesh):
    return jax.shard_map(
        shards,
        mesh=mesh,
        in_specs=(
            P(None, "tm", "lon", None),
            P("tm", "lon", None),
            P("tm", "lon", None),
            P(),
            P("lon", None),
            P(),
        ),
        out_specs=(P(None, "tm", "lon", None), P(None, "tm", "lon", None)),
        check_vma=False,
    )
```

```python
import functools
import jax
import jax.numpy as jnp
from jax import lax
from jax.experimental import pallas as pl
from jax.experimental.pallas import tpu as pltpu
from jax.sharding import PartitionSpec as P

F32, BF16, I16, I32 = jnp.float32, jnp.bfloat16, jnp.int16, jnp.int32
EXACT, HIGH = lax.Precision.HIGHEST, lax.Precision.HIGH
NOISE_VAR = 0.25
SPECTRUM_MAX = 4.0
HOURLY_MAX = 400.0
STEPS = 1024.0
LEAST = -18.0
CODE_MAX = 2.0**13.5
GROUP = 16
HALVES = 2
VMEM = 52 * 1024 * 1024


def encode(x):
    size = jnp.maximum(jnp.abs(x), 2.0**LEAST)
    code = (jnp.log(size) * (STEPS / 0.6931471805599453) + (0.5 - STEPS * LEAST)).astype(I32)
    return jnp.where(x < 0, -code, code).astype(I16)


def decode(code):
    wide = code.astype(I32)
    size = jnp.exp2(jnp.abs(wide).astype(F32) * (1.0 / STEPS) + LEAST)
    size = jnp.where(wide == 0, 0.0, size)
    return jnp.where(wide < 0, -size, size)


def dot(a, b):
    return jnp.dot(a, b, preferred_element_type=F32)


def dot_rows(a, b):
    return lax.dot_general(a, b, (((1,), (1,)), ((), ())), preferred_element_type=F32)


def two_part_dot(a, b):
    top = a.astype(BF16)
    rest = (a - top.astype(F32)).astype(BF16)
    both = dot(jnp.concatenate([top, rest], axis=0), b)
    return both[: a.shape[0]] + both[a.shape[0] :]


def fold(x):
    rows, cols = x.shape
    x = jnp.sum(x.reshape(rows // 8, 8, cols), axis=0)
    total = x[:, :128]
    for start in range(128, cols, 128):
        total = total + x[:, start : start + 128]
    return total


def whole_spec(shape):
    return pl.BlockSpec(shape, lambda i: (0,) * len(shape))


SCALARS = pl.BlockSpec(memory_space=pltpu.SMEM)
ANYWHERE = pl.BlockSpec(memory_space=pl.ANY)


def struct(shape, kind):
    return jax.ShapeDtypeStruct(shape, kind)


class Kernels:
    def __init__(self, zs, qs, hour_local, lat_local, lat_rows, lon_local):
        self.zs, self.qs = zs, qs
        self.al, self.lr, self.ol = lat_local, lat_rows, lon_local
        self.hl = hour_local
        self.hp = hour_local // HALVES
        self.hours, self.lats, self.lons = zs * hour_local, zs * lat_local, qs * lon_local
        self.cells = self.hp * lat_rows * self.lons
        self.token = None
        self.ease = 1

    def call(self, body, name, grid, out_shape, in_specs, out_specs, flops, moved, scratch=(), aliases={}):
        tokens = [] if self.token is None else [self.token]

        def run(*args):
            def whole(*refs):
                refs = list(refs)
                del refs[len(args) : len(args) + len(tokens)]
                place = len(args) + len(out_shape)
                token_ref = refs.pop(place)
                token_ref[...] = jnp.zeros_like(token_ref)
                body(*refs)

            out = pl.pallas_call(
                whole,
                name=name,
                grid=(grid,),
                out_shape=list(out_shape) + [struct((8, 128), F32)],
                in_specs=list(in_specs) + [ANYWHERE] * len(tokens),
                out_specs=list(out_specs) + [whole_spec((8, 128))],
                scratch_shapes=list(scratch),
                input_output_aliases=aliases,
                compiler_params=pltpu.CompilerParams(vmem_limit_bytes=VMEM),
                cost_estimate=pl.CostEstimate(flops=flops * self.ease, bytes_accessed=moved * self.ease, transcendentals=0),
            )(*args, *tokens)
            self.token = out[-1]
            return out[:-1]

        return run

    def after(self, x, *tokens):
        tokens = [self.token, *tokens]
        return pl.pallas_call(
            lambda *refs: None,
            name="after",
            out_shape=struct(x.shape, x.dtype),
            in_specs=[ANYWHERE] * (1 + len(tokens)),
            out_specs=ANYWHERE,
            input_output_aliases={0: 0},
            compiler_params=pltpu.CompilerParams(vmem_limit_bytes=VMEM),
            cost_estimate=pl.CostEstimate(flops=0, bytes_accessed=0, transcendentals=0),
        )(x, *tokens)

    def parts_specs(self, group):
        return [pl.BlockSpec((group, self.lr, self.ol), lambda i: (i, 0, 0))] * self.qs

    def parts_shape(self, kind, size=None):
        return [struct((size or self.hp, self.lr, self.ol), kind)] * self.qs

    def grid_spec(self, group, start=0):
        offset = start // group
        return pl.BlockSpec((group, self.lr, self.lons), lambda i: (i + offset, 0, 0))

    def hourly(self, noise, tables):
        zs, hp, al, ol, hours = self.zs, self.hp, self.al, self.ol, self.hours
        periods = noise.shape[3]

        def body(noise_ref, table_ref, *refs):
            outs, turned = refs[:HALVES], refs[HALVES]
            for start in range(0, GROUP, 4):
                part = noise_ref[:, start : start + 4].reshape(2, 4 * ol, periods)
                total = dot_rows(table_ref[0], part[0]) + dot_rows(table_ref[1], part[1])
                for k in range(4):
                    turned[pl.ds(start + k, hours, stride=GROUP), :] = total[:, k * ol : (k + 1) * ol]
            value = turned[...].reshape(zs, HALVES, hp, GROUP, ol).astype(BF16)
            for c in range(HALVES):
                outs[c][...] = value[:, c]

        return self.call(
            body, "hourly", al // GROUP, [struct((zs, hp, al, ol), BF16)] * HALVES,
            [pl.BlockSpec((2, GROUP, ol, periods), lambda i: (0, i, 0, 0)), whole_spec(tables.shape)],
            [pl.BlockSpec((zs, hp, GROUP, ol), lambda i: (0, 0, i, 0))] * HALVES,
            4 * hours * periods * al * ol, 2 * noise.size + 2 * hours * al * ol,
            [pltpu.VMEM((hours * GROUP, ol), F32)],
        )(noise, tables)

    def lat_up(self, start, size, g, lat, gain):
        zs, qs, lr, ol, lats = self.zs, self.qs, self.lr, self.ol, self.lats
        cells = size * lr * self.lons
        group = 8
        offset = start // group

        def body(gain_ref, g_ref, lat_ref, *outs):
            for h in range(0, group, 4):
                part = [g_ref[:, h + k].reshape(lats, ol) for k in range(4)]
                total = dot(lat_ref[...], jnp.concatenate(part, axis=1))
                code = encode(total * gain_ref[0])
                for k in range(4):
                    for d in range(qs):
                        outs[d][h + k] = code[d * lr : (d + 1) * lr, k * ol : (k + 1) * ol]

        return self.call(
            body, "lat_up", size // group, self.parts_shape(I16, size),
            [SCALARS, pl.BlockSpec((zs, group, self.al, ol), lambda i: (0, i + offset, 0, 0)), whole_spec(lat.shape)],
            self.parts_specs(group), 2 * cells * self.lats, 4 * cells,
        )(gain.reshape(1), g, lat)

    def residual(self, c, codes, back, lon_up, lon_down, observed, mask):
        qs, hp, lr, ol, lons = self.qs, self.hp, self.lr, self.ol, self.lons
        group = 8
        rows = group * lr

        def body(back_ref, *refs):
            arrived, (up_ref, down_ref, observed_ref, mask_ref) = refs[:qs], refs[qs : qs + 4]
            prior_ref, norm_ref, outs = refs[qs + 4], refs[qs + 5], refs[qs + 6 :]
            x = jnp.concatenate([decode(a[...].reshape(rows, ol)) for a in arrived], axis=1)
            prior = two_part_dot(x, up_ref[...]) * back_ref[0]
            prior_ref[...] = prior.reshape(group, lr, lons)
            seen = mask_ref[...].reshape(rows, lons).astype(F32)
            resid = seen * (observed_ref[...].reshape(rows, lons) - prior)

            @pl.when(pl.program_id(0) == 0)
            def _():
                norm_ref[...] = jnp.zeros_like(norm_ref)

            norm_ref[...] += fold(resid * resid)
            v = two_part_dot(resid, down_ref[...]).astype(BF16)
            for d in range(qs):
                outs[d][...] = v[:, d * ol : (d + 1) * ol].reshape(group, lr, ol)

        out = self.call(
            body, "residual", hp // group,
            [struct((hp, lr, lons), F32), struct((8, 128), F32)] + self.parts_shape(BF16),
            [SCALARS] + self.parts_specs(group) + [whole_spec(lon_up.shape)] * 2 + [self.grid_spec(group, c * hp)] * 2,
            [self.grid_spec(group), whole_spec((8, 128))] + self.parts_specs(group),
            8 * self.cells * lons, 16 * self.cells,
        )(back.reshape(1), *codes, lon_up, lon_down, observed, mask)
        return out[0], out[1], out[2:]

    def lat_down(self, c, v, lat_t, whole, earlier):
        zs, qs, hp, al, lr, ol, lats = self.zs, self.qs, self.hp, self.al, self.lr, self.ol, self.lats

        offset = c * (hp // GROUP) if whole else 0
        size = self.hl if whole else hp

        def body(*refs):
            sent, lat_ref, (out_ref, turned) = refs[:qs], refs[qs], refs[-2:]
            for start in range(0, GROUP, 4):
                part = [jnp.concatenate([s[start + k] for s in sent], axis=0) for k in range(4)]
                total = dot(lat_ref[...], jnp.concatenate(part, axis=1))
                for k in range(4):
                    turned[pl.ds(start + k, lats, stride=GROUP), :] = total[:, k * ol : (k + 1) * ol]
            out_ref[...] = turned[...].reshape(zs, al, GROUP, ol).astype(BF16)

        return self.call(
            body, "lat_down", hp // GROUP, [struct((zs, al, size, ol), BF16)],
            self.parts_specs(GROUP) + [whole_spec(lat_t.shape)] + [ANYWHERE] * len(earlier),
            [pl.BlockSpec((zs, al, GROUP, ol), lambda i: (0, 0, i + offset, 0))],
            2 * self.cells * lats, 4 * self.cells,
            [pltpu.VMEM((lats * GROUP, ol), F32)], {qs + 1: 0} if earlier else {},
        )(*v, lat_t, *earlier)

    def over_hours(self, xs, kern, pieces):
        zs, hl, al, ol, hours = self.zs, self.hl, self.al, self.ol, self.hours
        count = len(xs)

        def body(*refs):
            arrived, kern_ref, refs = refs[:count], refs[count], refs[count + 1 :]
            outs, (bend_ref, turned) = refs[: len(pieces)], refs[len(pieces) :]

            @pl.when(pl.program_id(0) == 0)
            def _():
                bend_ref[...] = jnp.zeros_like(bend_ref)

            for start in range(0, GROUP, 4):
                part = []
                for k in range(4):
                    rows = [x[z, start + k] for z in range(zs) for x in arrived]
                    part.append(jnp.concatenate(rows, axis=0))
                part = jnp.concatenate(part, axis=1)
                total = dot(kern_ref[0], part) + dot(kern_ref[1], part)
                bend_ref[...] += fold(total * part.astype(F32))
                for k in range(4):
                    turned[pl.ds(start + k, hours, stride=GROUP), :] = total[:, k * ol : (k + 1) * ol]
            value = turned[...].reshape(zs, hl, GROUP, ol).astype(BF16)
            for out_ref, (first, size) in zip(outs, pieces):
                out_ref[...] = value[:, first : first + size]

        out = self.call(
            body, "over_hours", al // GROUP, [struct((zs, size, al, ol), BF16) for _, size in pieces] + [struct((8, 128), F32)],
            [pl.BlockSpec((zs, GROUP, hl // count, ol), lambda i: (0, i, 0, 0))] * count + [whole_spec(kern.shape)],
            [pl.BlockSpec((zs, size, GROUP, ol), lambda i: (0, 0, i, 0)) for _, size in pieces]
            + [whole_spec((8, 128))],
            8 * self.cells * hours, 8 * self.cells,
            [pltpu.VMEM((hours * GROUP, ol), F32)],
        )(*xs, kern)
        return out[:-1], out[-1]

    def finish(self, s, first, size, codes, back, step, lon_up, prior, observed, mask, earlier):
        qs, hp, lr, ol, lons = self.qs, self.hp, self.lr, self.ol, self.lons
        cells = size * lr * lons
        group = 8
        rows = group * lr

        def body(scalar_ref, *refs):
            arrived, (up_ref, prior_ref, observed_ref, mask_ref) = refs[:qs], refs[qs : qs + 4]
            posterior_ref, next_ref = refs[-2:]
            x = jnp.concatenate([decode(a[...].reshape(rows, ol)) for a in arrived], axis=1)
            scaled = two_part_dot(x, up_ref[...]) * scalar_ref[0]
            prior = prior_ref[...].reshape(rows, lons)
            seen = mask_ref[...].reshape(rows, lons).astype(F32)
            resid = seen * (observed_ref[...].reshape(rows, lons) - prior)
            shape = (1, group, lr, lons)
            posterior_ref[...] = (prior + scaled).reshape(shape)
            next_ref[...] = (resid - seen * scaled - scalar_ref[1] * resid).reshape(shape)

        full = struct((2, self.hl, lr, lons), F32)
        offset = first // group
        out_spec = pl.BlockSpec((1, group, lr, lons), lambda i: (s, i + offset, 0, 0))
        count = 1 + qs + 4
        return self.call(
            body, "finish", size // group, [full, full],
            [SCALARS] + self.parts_specs(group) + [whole_spec(lon_up.shape), self.grid_spec(group, first % hp)]
            + [self.grid_spec(group, first)] * 2 + [ANYWHERE] * len(earlier),
            [out_spec, out_spec], 4 * cells * lons, 22 * cells,
            aliases={count + i: i for i in range(len(earlier))},
        )(jnp.stack([back * step, NOISE_VAR * step]), *codes, lon_up, prior, observed, mask, *earlier)

    def joined(self, earlier):
        return tuple(earlier)


class Plain(Kernels):
    def after(self, x, *tokens):
        return x

    def hourly(self, noise, tables):
        h = jnp.einsum("cyxk,cjk->jyx", noise, tables, preferred_element_type=F32).astype(BF16)
        h = h.reshape(self.zs, HALVES, self.hp, self.al, self.ol)
        return [h[:, c] for c in range(HALVES)]

    def lat_up(self, start, size, g, lat, gain):
        g = g[:, start : start + size]
        split = lat.reshape(self.qs, self.lr, self.zs, self.al)
        x = encode(jnp.einsum("qlzy,zhyx->qhlx", split, g, preferred_element_type=F32) * gain)
        return [x[d] for d in range(self.qs)]

    def up(self, codes, lon_up):
        x = jnp.concatenate([decode(c) for c in codes], axis=2)
        return jnp.einsum("hlx,xo->hlo", x, lon_up.astype(F32), precision=HIGH)

    def residual(self, c, codes, back, lon_up, lon_down, observed, mask):
        prior = self.up(codes, lon_up) * back
        here = slice(c * self.hp, (c + 1) * self.hp)
        resid = mask[here].astype(F32) * (observed[here] - prior)
        v = jnp.einsum("hlo,op->hlp", resid, lon_down.astype(F32), precision=HIGH).astype(BF16)
        return prior, jnp.sum(resid * resid), jnp.split(v, self.qs, axis=2)

    def lat_down(self, c, v, lat_t, whole, earlier):
        split = lat_t.reshape(self.zs, self.al, self.qs, self.lr)
        x = jnp.einsum("zyql,qhlx->zyhx", split, jnp.stack(v), preferred_element_type=F32)
        return (jnp.concatenate(list(earlier) + [x.astype(BF16)], axis=2),)

    def over_hours(self, xs, kern, pieces):
        x = jnp.concatenate(xs, axis=2)
        x = jnp.swapaxes(x, 0, 1).reshape(self.al, self.hours, self.ol).astype(F32)
        y = jnp.einsum("gk,ykx->gyx", kern.astype(F32).sum(0), x, precision=HIGH)
        bend = jnp.einsum("gyx,ygx->", y, x)
        y = y.astype(BF16).reshape(self.zs, self.hl, self.al, self.ol)
        return [y[:, first : first + size] for first, size in pieces], bend

    def finish(self, s, first, size, codes, back, step, lon_up, prior, observed, mask, earlier):
        scaled = self.up(codes, lon_up) * (back * step)
        here = slice(first, first + size)
        prior = prior[first % self.hp : first % self.hp + size]
        seen = mask[here].astype(F32)
        resid = seen * (observed[here] - prior)
        return tuple(earlier) + ((s, prior + scaled, resid - seen * scaled - NOISE_VAR * step * resid),)

    def joined(self, earlier):
        samples = [[e[1:] for e in earlier if e[0] == s] for s in range(2)]
        return tuple(jnp.stack([jnp.concatenate([e[i] for e in part]) for part in samples]) for i in range(2))


def swap_tm(x):
    return lax.all_to_all(x, "tm", split_axis=0, concat_axis=0, tiled=True)


def swap_lon(parts):
    count = len(parts)
    return [parts[0]] + [
        lax.ppermute(parts[d], "lon", [(i, i ^ d) for i in range(count)]) for d in range(1, count)
    ]


def add_over_tm(x, count):
    return sum([lax.ppermute(x, "tm", [(i, i ^ d) for i in range(count)]) for d in range(1, count)], x)


def add_over_lon(x, count):
    d = 1
    while d < count:
        x = x + lax.ppermute(x, "lon", [(i, i ^ d) for i in range(count)])
        d *= 2
    return x


def largest_norm(factor, axis):
    return jnp.sqrt(jnp.max(jnp.sum(jnp.square(factor.astype(F32)), axis=axis)))


def shards(noise, observed, mask, lat_factor, lon_factor, spectrum):
    _, lat_local, lon_local, periods = noise.shape
    hour_local, lat_rows, lon_count = observed.shape
    hours = periods // 2
    hour_part = hour_local // HALVES
    zs, qs = hours // hour_local, lon_count // lon_local
    lat_count = zs * lat_local
    fits = lon_local % 128 == 0 and lat_rows % 16 == 0
    fits = fits and lat_local % GROUP == 0 and hour_part % GROUP == 0
    stages = (Kernels if fits else Plain)(zs, qs, hour_local, lat_local, lat_rows, lon_local)
    order = lax.axis_index("lon") ^ jnp.arange(qs)

    powers = jnp.concatenate([spectrum, spectrum[1:-1][::-1]])
    amplitude = jnp.sqrt(powers / periods)
    clock = jnp.arange(hours)[:, None]
    phase = (clock * jnp.arange(periods) % periods).astype(F32) * (2.0 * jnp.pi / periods)
    cosine_tab, sine_tab = jnp.cos(phase), jnp.sin(phase)
    table_cos = (cosine_tab * amplitude).astype(BF16)
    table_sin = (sine_tab * amplitude).astype(BF16)
    tables = (jnp.stack([table_cos, table_sin]), jnp.stack([-table_sin, table_cos]))

    def hour_kernel():
        scaled = powers / periods
        kern = jnp.dot(cosine_tab * scaled, cosine_tab.T, precision=EXACT) + jnp.dot(
            sine_tab * scaled, sine_tab.T, precision=EXACT
        )
        top = lax.reduce_precision(kern, 8, 7)
        return jnp.stack([top.astype(BF16), (kern - top).astype(BF16)])

    lon = lax.all_gather(lon_factor, "lon", axis=0, tiled=True)
    units = [(s, c) for s in range(2) for c in range(HALVES)]
    lon_down = jnp.concatenate(
        [lax.dynamic_slice_in_dim(lon, order[d] * lon_local, lon_local, axis=1) for d in range(qs)], axis=1
    )
    lon_up = lon_down.T
    first, second, third, fourth = units
    wait = stages.after
    arrived, waves = {}, {}
    for s in range(2):
        for c, part in enumerate(stages.hourly(noise, tables[s])):
            waves[s, c] = part
    arrived[first] = swap_tm(waves[first])
    arrived[second] = swap_tm(wait(waves[second], lon_up, lon_down))
    kern = hour_kernel()
    lat = jnp.take(lat_factor.reshape(qs, lat_rows, lat_count), order, axis=0)
    lat = lat.reshape(lat_count, lat_count)
    lat_t = lat.T
    lat_row_norm = largest_norm(lat_factor, 1)
    lon_col_norm = largest_norm(lon_down, 0)
    lat_norm = jnp.sqrt(jnp.sum(jnp.square(lat_factor.astype(F32))))
    first_gain = CODE_MAX / jnp.maximum(lat_row_norm * (lat_count**0.5 * HOURLY_MAX), 1e-30)
    codes, priors, norms, sent, down = {}, {}, {}, {}, {}

    def up(u):
        codes[u] = swap_lon(stages.lat_up(0, hour_part, arrived[u], lat, first_gain))

    def middle(u):
        priors[u], norms[u], v = stages.residual(
            u[1], codes[u], 1.0 / first_gain, lon_up, lon_down, observed, mask
        )
        sent[u] = swap_lon(v)

    def lower(u):
        down[u] = stages.lat_down(u[1], sent[u], lat_t, u[0] == 0, down[first] if u == second else ())

    stages.ease = 1
    up(first)
    middle(first)
    stages.ease = 4
    arrived[third] = swap_tm(wait(waves[third]))
    up(second)
    lower(first)
    arrived[fourth] = swap_tm(wait(waves[fourth]))
    middle(second)
    up(third)
    lower(second)
    down[second] = swap_tm(wait(down[second][0]))
    up(fourth)
    middle(third)
    lower(third)
    middle(fourth)
    down[third] = swap_tm(wait(down[third][0]))
    early, bending = stages.over_hours([down[second]], kern, [(0, hour_part), (hour_part, hour_part)])
    sums = [sum(jnp.sum(norms[u]) for u in units if u[0] == s) for s in range(2)] + [jnp.sum(bending)]
    lower(fourth)
    down[fourth] = swap_tm(down[fourth][0])
    early = list(early)
    early[0] = swap_tm(early[0])

    quarter = hour_part // 2
    pieces = [(0, hour_part), (hour_part, quarter), (hour_part + quarter, hour_part - quarter)]
    late, bending = stages.over_hours([down[third], down[fourth]], kern, pieces)
    sums.append(jnp.sum(bending))
    sums = add_over_tm(jnp.broadcast_to(jnp.stack(sums)[:, None], (4, 128)), zs)
    late = list(late)
    early[1] = swap_tm(wait(early[1], sums))
    sums = add_over_lon(sums, qs)[:, 0]
    gains, steps = [], []
    for s in range(2):
        norm_sq, bending = sums[s], sums[2 + s]
        bound = SPECTRUM_MAX * lat_row_norm * lat_norm * lon_col_norm * jnp.sqrt(norm_sq)
        gains.append(CODE_MAX / jnp.maximum(bound, 1e-30))
        steps.append(norm_sq / (bending + NOISE_VAR * norm_sq))
    earlier = ()

    stages.ease = 2

    def back(s, start, size, g):
        return swap_lon(stages.lat_up(start, size, g, lat, gains[s]))

    def end(s, start, size, codes):
        prior = priors[s, start // hour_part]
        return stages.finish(
            s, start, size, codes, 1.0 / gains[s], steps[s], lon_up, prior, observed, mask, earlier
        )

    quarters = pieces[1:]
    first_codes = back(0, 0, hour_part, early[0])
    late[0] = swap_tm(wait(late[0], *first_codes[1:]))
    second_codes = back(0, 0, hour_part, early[1])
    earlier = end(0, 0, hour_part, first_codes)
    late[1] = swap_tm(wait(late[1], *second_codes[1:]))
    third_codes = back(1, 0, hour_part, late[0])
    earlier = end(0, hour_part, hour_part, second_codes)
    late[2] = swap_tm(wait(late[2], *third_codes[1:5]))
    fourth_codes = back(1, 0, quarters[0][1], late[1])
    earlier = end(1, *pieces[0], third_codes)
    fifth_codes = back(1, 0, quarters[1][1], late[2])
    earlier = end(1, *quarters[0], fourth_codes)
    earlier = end(1, *quarters[1], fifth_codes)
    return stages.joined(earlier)


def solution(mesh):
    return jax.shard_map(
        shards,
        mesh=mesh,
        in_specs=(
            P(None, "tm", "lon", None),
            P("tm", "lon", None),
            P("tm", "lon", None),
            P(),
            P("lon", None),
            P(),
        ),
        out_specs=(P(None, "tm", "lon", None), P(None, "tm", "lon", None)),
        check_vma=False,
    )
```

```python
import functools
import jax
import jax.numpy as jnp
from jax import lax
from jax.experimental import pallas as pl
from jax.experimental.pallas import tpu as pltpu
from jax.sharding import PartitionSpec as P

F32, BF16, I16, I32 = jnp.float32, jnp.bfloat16, jnp.int16, jnp.int32
EXACT, HIGH = lax.Precision.HIGHEST, lax.Precision.HIGH
NOISE_VAR = 0.25
SPECTRUM_MAX = 4.0
HOURLY_MAX = 400.0
STEPS = 1024.0
LEAST = -18.0
CODE_MAX = 2.0**13.5
GROUP = 16
HALVES = 2
VMEM = 52 * 1024 * 1024


def encode(x):
    size = jnp.maximum(jnp.abs(x), 2.0**LEAST)
    code = (jnp.log(size) * (STEPS / 0.6931471805599453) + (0.5 - STEPS * LEAST)).astype(I32)
    return jnp.where(x < 0, -code, code).astype(I16)


def decode(code):
    wide = code.astype(I32)
    size = jnp.exp2(jnp.abs(wide).astype(F32) * (1.0 / STEPS) + LEAST)
    size = jnp.where(wide == 0, 0.0, size)
    return jnp.where(wide < 0, -size, size)


def dot(a, b):
    return jnp.dot(a, b, preferred_element_type=F32)


def dot_rows(a, b):
    return lax.dot_general(a, b, (((1,), (1,)), ((), ())), preferred_element_type=F32)


def two_part_dot(a, b):
    top = a.astype(BF16)
    rest = (a - top.astype(F32)).astype(BF16)
    both = dot(jnp.concatenate([top, rest], axis=0), b)
    return both[: a.shape[0]] + both[a.shape[0] :]


def fold(x):
    rows, cols = x.shape
    x = jnp.sum(x.reshape(rows // 8, 8, cols), axis=0)
    total = x[:, :128]
    for start in range(128, cols, 128):
        total = total + x[:, start : start + 128]
    return total


def whole_spec(shape):
    return pl.BlockSpec(shape, lambda i: (0,) * len(shape))


SCALARS = pl.BlockSpec(memory_space=pltpu.SMEM)
ANYWHERE = pl.BlockSpec(memory_space=pl.ANY)


def struct(shape, kind):
    return jax.ShapeDtypeStruct(shape, kind)


class Kernels:
    def __init__(self, zs, qs, hour_local, lat_local, lat_rows, lon_local):
        self.zs, self.qs = zs, qs
        self.al, self.lr, self.ol = lat_local, lat_rows, lon_local
        self.hl = hour_local
        self.hp = hour_local // HALVES
        self.hours, self.lats, self.lons = zs * hour_local, zs * lat_local, qs * lon_local
        self.cells = self.hp * lat_rows * self.lons
        self.token = None
        self.ease = 1

    def call(self, body, name, grid, out_shape, in_specs, out_specs, flops, moved, scratch=(), aliases={}):
        tokens = [] if self.token is None else [self.token]

        def run(*args):
            def whole(*refs):
                refs = list(refs)
                del refs[len(args) : len(args) + len(tokens)]
                place = len(args) + len(out_shape)
                token_ref = refs.pop(place)
                token_ref[...] = jnp.zeros_like(token_ref)
                body(*refs)

            out = pl.pallas_call(
                whole,
                name=name,
                grid=(grid,),
                out_shape=list(out_shape) + [struct((8, 128), F32)],
                in_specs=list(in_specs) + [ANYWHERE] * len(tokens),
                out_specs=list(out_specs) + [whole_spec((8, 128))],
                scratch_shapes=list(scratch),
                input_output_aliases=aliases,
                compiler_params=pltpu.CompilerParams(vmem_limit_bytes=VMEM),
                cost_estimate=pl.CostEstimate(flops=flops * self.ease, bytes_accessed=moved * self.ease, transcendentals=0),
            )(*args, *tokens)
            self.token = out[-1]
            return out[:-1]

        return run

    def after(self, x, *tokens):
        tokens = [self.token, *tokens]
        return pl.pallas_call(
            lambda *refs: None,
            name="after",
            out_shape=struct(x.shape, x.dtype),
            in_specs=[ANYWHERE] * (1 + len(tokens)),
            out_specs=ANYWHERE,
            input_output_aliases={0: 0},
            compiler_params=pltpu.CompilerParams(vmem_limit_bytes=VMEM),
            cost_estimate=pl.CostEstimate(flops=0, bytes_accessed=0, transcendentals=0),
        )(x, *tokens)

    def parts_specs(self, group):
        return [pl.BlockSpec((group, self.lr, self.ol), lambda i: (i, 0, 0))] * self.qs

    def parts_shape(self, kind, size=None):
        return [struct((size or self.hp, self.lr, self.ol), kind)] * self.qs

    def grid_spec(self, group, start=0):
        offset = start // group
        return pl.BlockSpec((group, self.lr, self.lons), lambda i: (i + offset, 0, 0))

    def hourly(self, noise, tables):
        zs, hp, al, ol, hours = self.zs, self.hp, self.al, self.ol, self.hours
        periods = noise.shape[3]

        def body(noise_ref, table_ref, *refs):
            outs, turned = refs[:HALVES], refs[HALVES]
            for start in range(0, GROUP, 4):
                part = noise_ref[:, start : start + 4].reshape(2, 4 * ol, periods)
                total = dot_rows(table_ref[0], part[0]) + dot_rows(table_ref[1], part[1])
                for k in range(4):
                    turned[pl.ds(start + k, hours, stride=GROUP), :] = total[:, k * ol : (k + 1) * ol]
            value = turned[...].reshape(zs, HALVES, hp, GROUP, ol).astype(BF16)
            for c in range(HALVES):
                outs[c][...] = value[:, c]

        return self.call(
            body, "hourly", al // GROUP, [struct((zs, hp, al, ol), BF16)] * HALVES,
            [pl.BlockSpec((2, GROUP, ol, periods), lambda i: (0, i, 0, 0)), whole_spec(tables.shape)],
            [pl.BlockSpec((zs, hp, GROUP, ol), lambda i: (0, 0, i, 0))] * HALVES,
            4 * hours * periods * al * ol, 2 * noise.size + 2 * hours * al * ol,
            [pltpu.VMEM((hours * GROUP, ol), F32)],
        )(noise, tables)

    def lat_up(self, start, size, g, lat, gain):
        zs, qs, lr, ol, lats = self.zs, self.qs, self.lr, self.ol, self.lats
        cells = size * lr * self.lons
        group = 8
        offset = start // group

        def body(gain_ref, g_ref, lat_ref, *outs):
            for h in range(0, group, 4):
                part = [g_ref[:, h + k].reshape(lats, ol) for k in range(4)]
                total = dot(lat_ref[...], jnp.concatenate(part, axis=1))
                code = encode(total * gain_ref[0])
                for k in range(4):
                    for d in range(qs):
                        outs[d][h + k] = code[d * lr : (d + 1) * lr, k * ol : (k + 1) * ol]

        return self.call(
            body, "lat_up", size // group, self.parts_shape(I16, size),
            [SCALARS, pl.BlockSpec((zs, group, self.al, ol), lambda i: (0, i + offset, 0, 0)), whole_spec(lat.shape)],
            self.parts_specs(group), 2 * cells * self.lats, 4 * cells,
        )(gain.reshape(1), g, lat)

    def residual(self, c, codes, back, lon_up, lon_down, observed, mask):
        qs, hp, lr, ol, lons = self.qs, self.hp, self.lr, self.ol, self.lons
        group = 8
        rows = group * lr

        def body(back_ref, *refs):
            arrived, (up_ref, down_ref, observed_ref, mask_ref) = refs[:qs], refs[qs : qs + 4]
            prior_ref, norm_ref, outs = refs[qs + 4], refs[qs + 5], refs[qs + 6 :]
            x = jnp.concatenate([decode(a[...].reshape(rows, ol)) for a in arrived], axis=1)
            prior = two_part_dot(x, up_ref[...]) * back_ref[0]
            prior_ref[...] = prior.reshape(group, lr, lons)
            seen = mask_ref[...].reshape(rows, lons).astype(F32)
            resid = seen * (observed_ref[...].reshape(rows, lons) - prior)

            @pl.when(pl.program_id(0) == 0)
            def _():
                norm_ref[...] = jnp.zeros_like(norm_ref)

            norm_ref[...] += fold(resid * resid)
            v = two_part_dot(resid, down_ref[...]).astype(BF16)
            for d in range(qs):
                outs[d][...] = v[:, d * ol : (d + 1) * ol].reshape(group, lr, ol)

        out = self.call(
            body, "residual", hp // group,
            [struct((hp, lr, lons), F32), struct((8, 128), F32)] + self.parts_shape(BF16),
            [SCALARS] + self.parts_specs(group) + [whole_spec(lon_up.shape)] * 2 + [self.grid_spec(group, c * hp)] * 2,
            [self.grid_spec(group), whole_spec((8, 128))] + self.parts_specs(group),
            8 * self.cells * lons, 16 * self.cells,
        )(back.reshape(1), *codes, lon_up, lon_down, observed, mask)
        return out[0], out[1], out[2:]

    def lat_down(self, c, v, lat_t, whole, earlier):
        zs, qs, hp, al, lr, ol, lats = self.zs, self.qs, self.hp, self.al, self.lr, self.ol, self.lats

        offset = c * (hp // GROUP) if whole else 0
        size = self.hl if whole else hp

        def body(*refs):
            sent, lat_ref, (out_ref, turned) = refs[:qs], refs[qs], refs[-2:]
            for start in range(0, GROUP, 4):
                part = [jnp.concatenate([s[start + k] for s in sent], axis=0) for k in range(4)]
                total = dot(lat_ref[...], jnp.concatenate(part, axis=1))
                for k in range(4):
                    turned[pl.ds(start + k, lats, stride=GROUP), :] = total[:, k * ol : (k + 1) * ol]
            out_ref[...] = turned[...].reshape(zs, al, GROUP, ol).astype(BF16)

        return self.call(
            body, "lat_down", hp // GROUP, [struct((zs, al, size, ol), BF16)],
            self.parts_specs(GROUP) + [whole_spec(lat_t.shape)] + [ANYWHERE] * len(earlier),
            [pl.BlockSpec((zs, al, GROUP, ol), lambda i: (0, 0, i + offset, 0))],
            2 * self.cells * lats, 4 * self.cells,
            [pltpu.VMEM((lats * GROUP, ol), F32)], {qs + 1: 0} if earlier else {},
        )(*v, lat_t, *earlier)

    def over_hours(self, xs, kern, pieces):
        zs, hl, al, ol, hours = self.zs, self.hl, self.al, self.ol, self.hours
        count = len(xs)

        def body(*refs):
            arrived, kern_ref, refs = refs[:count], refs[count], refs[count + 1 :]
            outs, (bend_ref, turned) = refs[: len(pieces)], refs[len(pieces) :]

            @pl.when(pl.program_id(0) == 0)
            def _():
                bend_ref[...] = jnp.zeros_like(bend_ref)

            for start in range(0, GROUP, 4):
                part = []
                for k in range(4):
                    rows = [x[z, start + k] for z in range(zs) for x in arrived]
                    part.append(jnp.concatenate(rows, axis=0))
                part = jnp.concatenate(part, axis=1)
                total = dot(kern_ref[0], part) + dot(kern_ref[1], part)
                bend_ref[...] += fold(total * part.astype(F32))
                for k in range(4):
                    turned[pl.ds(start + k, hours, stride=GROUP), :] = total[:, k * ol : (k + 1) * ol]
            value = turned[...].reshape(zs, hl, GROUP, ol).astype(BF16)
            for out_ref, (first, size) in zip(outs, pieces):
                out_ref[...] = value[:, first : first + size]

        out = self.call(
            body, "over_hours", al // GROUP, [struct((zs, size, al, ol), BF16) for _, size in pieces] + [struct((8, 128), F32)],
            [pl.BlockSpec((zs, GROUP, hl // count, ol), lambda i: (0, i, 0, 0))] * count + [whole_spec(kern.shape)],
            [pl.BlockSpec((zs, size, GROUP, ol), lambda i: (0, 0, i, 0)) for _, size in pieces]
            + [whole_spec((8, 128))],
            8 * self.cells * hours, 8 * self.cells,
            [pltpu.VMEM((hours * GROUP, ol), F32)],
        )(*xs, kern)
        return out[:-1], out[-1]

    def finish(self, s, first, size, codes, back, step, lon_up, prior, observed, mask, earlier):
        qs, hp, lr, ol, lons = self.qs, self.hp, self.lr, self.ol, self.lons
        cells = size * lr * lons
        group = 8
        rows = group * lr

        def body(scalar_ref, *refs):
            arrived, (up_ref, prior_ref, observed_ref, mask_ref) = refs[:qs], refs[qs : qs + 4]
            posterior_ref, next_ref = refs[-2:]
            x = jnp.concatenate([decode(a[...].reshape(rows, ol)) for a in arrived], axis=1)
            scaled = two_part_dot(x, up_ref[...]) * scalar_ref[0]
            prior = prior_ref[...].reshape(rows, lons)
            seen = mask_ref[...].reshape(rows, lons).astype(F32)
            resid = seen * (observed_ref[...].reshape(rows, lons) - prior)
            shape = (1, group, lr, lons)
            posterior_ref[...] = (prior + scaled).reshape(shape)
            next_ref[...] = (resid - seen * scaled - scalar_ref[1] * resid).reshape(shape)

        full = struct((2, self.hl, lr, lons), F32)
        offset = first // group
        out_spec = pl.BlockSpec((1, group, lr, lons), lambda i: (s, i + offset, 0, 0))
        count = 1 + qs + 4
        return self.call(
            body, "finish", size // group, [full, full],
            [SCALARS] + self.parts_specs(group) + [whole_spec(lon_up.shape), self.grid_spec(group, first % hp)]
            + [self.grid_spec(group, first)] * 2 + [ANYWHERE] * len(earlier),
            [out_spec, out_spec], 4 * cells * lons, 22 * cells,
            aliases={count + i: i for i in range(len(earlier))},
        )(jnp.stack([back * step, NOISE_VAR * step]), *codes, lon_up, prior, observed, mask, *earlier)

    def joined(self, earlier):
        return tuple(earlier)


class Plain(Kernels):
    def after(self, x, *tokens):
        return x

    def hourly(self, noise, tables):
        h = jnp.einsum("cyxk,cjk->jyx", noise, tables, preferred_element_type=F32).astype(BF16)
        h = h.reshape(self.zs, HALVES, self.hp, self.al, self.ol)
        return [h[:, c] for c in range(HALVES)]

    def lat_up(self, start, size, g, lat, gain):
        g = g[:, start : start + size]
        split = lat.reshape(self.qs, self.lr, self.zs, self.al)
        x = encode(jnp.einsum("qlzy,zhyx->qhlx", split, g, preferred_element_type=F32) * gain)
        return [x[d] for d in range(self.qs)]

    def up(self, codes, lon_up):
        x = jnp.concatenate([decode(c) for c in codes], axis=2)
        return jnp.einsum("hlx,xo->hlo", x, lon_up.astype(F32), precision=HIGH)

    def residual(self, c, codes, back, lon_up, lon_down, observed, mask):
        prior = self.up(codes, lon_up) * back
        here = slice(c * self.hp, (c + 1) * self.hp)
        resid = mask[here].astype(F32) * (observed[here] - prior)
        v = jnp.einsum("hlo,op->hlp", resid, lon_down.astype(F32), precision=HIGH).astype(BF16)
        return prior, jnp.sum(resid * resid), jnp.split(v, self.qs, axis=2)

    def lat_down(self, c, v, lat_t, whole, earlier):
        split = lat_t.reshape(self.zs, self.al, self.qs, self.lr)
        x = jnp.einsum("zyql,qhlx->zyhx", split, jnp.stack(v), preferred_element_type=F32)
        return (jnp.concatenate(list(earlier) + [x.astype(BF16)], axis=2),)

    def over_hours(self, xs, kern, pieces):
        x = jnp.concatenate(xs, axis=2)
        x = jnp.swapaxes(x, 0, 1).reshape(self.al, self.hours, self.ol).astype(F32)
        y = jnp.einsum("gk,ykx->gyx", kern.astype(F32).sum(0), x, precision=HIGH)
        bend = jnp.einsum("gyx,ygx->", y, x)
        y = y.astype(BF16).reshape(self.zs, self.hl, self.al, self.ol)
        return [y[:, first : first + size] for first, size in pieces], bend

    def finish(self, s, first, size, codes, back, step, lon_up, prior, observed, mask, earlier):
        scaled = self.up(codes, lon_up) * (back * step)
        here = slice(first, first + size)
        prior = prior[first % self.hp : first % self.hp + size]
        seen = mask[here].astype(F32)
        resid = seen * (observed[here] - prior)
        return tuple(earlier) + ((s, prior + scaled, resid - seen * scaled - NOISE_VAR * step * resid),)

    def joined(self, earlier):
        samples = [[e[1:] for e in earlier if e[0] == s] for s in range(2)]
        return tuple(jnp.stack([jnp.concatenate([e[i] for e in part]) for part in samples]) for i in range(2))


def swap_tm(x):
    return lax.all_to_all(x, "tm", split_axis=0, concat_axis=0, tiled=True)


def swap_lon(parts):
    count = len(parts)
    return [parts[0]] + [
        lax.ppermute(parts[d], "lon", [(i, i ^ d) for i in range(count)]) for d in range(1, count)
    ]


def add_over_tm(x, count):
    return sum([lax.ppermute(x, "tm", [(i, i ^ d) for i in range(count)]) for d in range(1, count)], x)


def add_over_lon(x, count):
    d = 1
    while d < count:
        x = x + lax.ppermute(x, "lon", [(i, i ^ d) for i in range(count)])
        d *= 2
    return x


def largest_norm(factor, axis):
    return jnp.sqrt(jnp.max(jnp.sum(jnp.square(factor.astype(F32)), axis=axis)))


def shards(noise, observed, mask, lat_factor, lon_factor, spectrum):
    _, lat_local, lon_local, periods = noise.shape
    hour_local, lat_rows, lon_count = observed.shape
    hours = periods // 2
    hour_part = hour_local // HALVES
    zs, qs = hours // hour_local, lon_count // lon_local
    lat_count = zs * lat_local
    fits = lon_local % 128 == 0 and lat_rows % 16 == 0
    fits = fits and lat_local % GROUP == 0 and hour_part % GROUP == 0
    stages = (Kernels if fits else Plain)(zs, qs, hour_local, lat_local, lat_rows, lon_local)
    order = lax.axis_index("lon") ^ jnp.arange(qs)

    powers = jnp.concatenate([spectrum, spectrum[1:-1][::-1]])
    amplitude = jnp.sqrt(powers / periods)
    clock = jnp.arange(hours)[:, None]
    phase = (clock * jnp.arange(periods) % periods).astype(F32) * (2.0 * jnp.pi / periods)
    cosine_tab, sine_tab = jnp.cos(phase), jnp.sin(phase)
    table_cos = (cosine_tab * amplitude).astype(BF16)
    table_sin = (sine_tab * amplitude).astype(BF16)
    tables = (jnp.stack([table_cos, table_sin]), jnp.stack([-table_sin, table_cos]))

    def hour_kernel():
        scaled = powers / periods
        kern = jnp.dot(cosine_tab * scaled, cosine_tab.T, precision=EXACT) + jnp.dot(
            sine_tab * scaled, sine_tab.T, precision=EXACT
        )
        top = lax.reduce_precision(kern, 8, 7)
        return jnp.stack([top.astype(BF16), (kern - top).astype(BF16)])

    lon = lax.all_gather(lon_factor, "lon", axis=0, tiled=True)
    units = [(s, c) for s in range(2) for c in range(HALVES)]
    lon_down = jnp.concatenate(
        [lax.dynamic_slice_in_dim(lon, order[d] * lon_local, lon_local, axis=1) for d in range(qs)], axis=1
    )
    lon_up = lon_down.T
    first, second, third, fourth = units
    wait = stages.after
    arrived, waves = {}, {}
    for s in range(2):
        for c, part in enumerate(stages.hourly(noise, tables[s])):
            waves[s, c] = part
    arrived[first] = swap_tm(waves[first])
    arrived[second] = swap_tm(wait(waves[second], lon_up, lon_down))
    kern = hour_kernel()
    lat = jnp.take(lat_factor.reshape(qs, lat_rows, lat_count), order, axis=0)
    lat = lat.reshape(lat_count, lat_count)
    lat_t = lat.T
    lat_row_norm = largest_norm(lat_factor, 1)
    lon_col_norm = largest_norm(lon_down, 0)
    lat_norm = jnp.sqrt(jnp.sum(jnp.square(lat_factor.astype(F32))))
    first_gain = CODE_MAX / jnp.maximum(lat_row_norm * (lat_count**0.5 * HOURLY_MAX), 1e-30)
    codes, priors, norms, sent, down = {}, {}, {}, {}, {}

    def up(u):
        codes[u] = swap_lon(stages.lat_up(0, hour_part, arrived[u], lat, first_gain))

    def middle(u):
        priors[u], norms[u], v = stages.residual(
            u[1], codes[u], 1.0 / first_gain, lon_up, lon_down, observed, mask
        )
        sent[u] = swap_lon(v)

    def lower(u):
        down[u] = stages.lat_down(u[1], sent[u], lat_t, u[0] == 0, down[first] if u == second else ())

    stages.ease = 1
    up(first)
    middle(first)
    stages.ease = 4
    arrived[third] = swap_tm(wait(waves[third]))
    up(second)
    lower(first)
    arrived[fourth] = swap_tm(wait(waves[fourth]))
    middle(second)
    arrived[third] = wait(arrived[third], *sent[second][1:4])
    up(third)
    lower(second)
    down[second] = swap_tm(wait(down[second][0]))
    up(fourth)
    middle(third)
    lower(third)
    middle(fourth)
    down[third] = swap_tm(wait(down[third][0]))
    early, bending = stages.over_hours([down[second]], kern, [(0, hour_part), (hour_part, hour_part)])
    sums = [sum(jnp.sum(norms[u]) for u in units if u[0] == s) for s in range(2)] + [jnp.sum(bending)]
    lower(fourth)
    down[fourth] = swap_tm(down[fourth][0])
    early = list(early)
    early[0] = swap_tm(early[0])

    quarter = hour_part // 2
    pieces = [(0, hour_part), (hour_part, quarter), (hour_part + quarter, hour_part - quarter)]
    late, bending = stages.over_hours([down[third], down[fourth]], kern, pieces)
    sums.append(jnp.sum(bending))
    sums = add_over_tm(jnp.broadcast_to(jnp.stack(sums)[:, None], (4, 128)), zs)
    late = list(late)
    early[1] = swap_tm(wait(early[1], sums))
    sums = add_over_lon(sums, qs)[:, 0]
    gains, steps = [], []
    for s in range(2):
        norm_sq, bending = sums[s], sums[2 + s]
        bound = SPECTRUM_MAX * lat_row_norm * lat_norm * lon_col_norm * jnp.sqrt(norm_sq)
        gains.append(CODE_MAX / jnp.maximum(bound, 1e-30))
        steps.append(norm_sq / (bending + NOISE_VAR * norm_sq))
    earlier = ()

    stages.ease = 2

    def back(s, start, size, g):
        return swap_lon(stages.lat_up(start, size, g, lat, gains[s]))

    def end(s, start, size, codes):
        prior = priors[s, start // hour_part]
        return stages.finish(
            s, start, size, codes, 1.0 / gains[s], steps[s], lon_up, prior, observed, mask, earlier
        )

    quarters = pieces[1:]
    first_codes = back(0, 0, hour_part, early[0])
    late[0] = swap_tm(wait(late[0], *first_codes[1:]))
    second_codes = back(0, 0, hour_part, early[1])
    earlier = end(0, 0, hour_part, first_codes)
    late[1] = swap_tm(wait(late[1], *second_codes[1:]))
    third_codes = back(1, 0, hour_part, late[0])
    earlier = end(0, hour_part, hour_part, second_codes)
    late[2] = swap_tm(wait(late[2], *third_codes[1:6]))
    fourth_codes = back(1, 0, quarters[0][1], late[1])
    earlier = end(1, *pieces[0], third_codes)
    fifth_codes = back(1, 0, quarters[1][1], late[2])
    earlier = end(1, *quarters[0], fourth_codes)
    earlier = end(1, *quarters[1], fifth_codes)
    return stages.joined(earlier)


def solution(mesh):
    return jax.shard_map(
        shards,
        mesh=mesh,
        in_specs=(
            P(None, "tm", "lon", None),
            P("tm", "lon", None),
            P("tm", "lon", None),
            P(),
            P("lon", None),
            P(),
        ),
        out_specs=(P(None, "tm", "lon", None), P(None, "tm", "lon", None)),
        check_vma=False,
    )
```

```python
import functools
import jax
import jax.numpy as jnp
import numpy as np
from jax import lax
from jax.experimental import pallas as pl
from jax.experimental.pallas import tpu as pltpu
from jax.sharding import PartitionSpec as P

F32, BF16, I16, I32 = jnp.float32, jnp.bfloat16, jnp.int16, jnp.int32
EXACT, HIGH = lax.Precision.HIGHEST, lax.Precision.HIGH
NOISE_VAR = 0.25
SPECTRUM_MAX = 4.0
HOURLY_MAX = 400.0
STEPS = 1024.0
LEAST = -18.0
CODE_MAX = 2.0**13.5
GROUP = 16
HALVES = 2
VMEM = 52 * 1024 * 1024


def encode(x):
    size = jnp.maximum(jnp.abs(x), 2.0**LEAST)
    code = (jnp.log(size) * (STEPS / 0.6931471805599453) + (0.5 - STEPS * LEAST)).astype(I32)
    return jnp.where(x < 0, -code, code).astype(I16)


def decode(code):
    wide = code.astype(I32)
    size = jnp.exp2(jnp.abs(wide).astype(F32) * (1.0 / STEPS) + LEAST)
    size = jnp.where(wide == 0, 0.0, size)
    return jnp.where(wide < 0, -size, size)


def dot(a, b):
    return jnp.dot(a, b, preferred_element_type=F32)


def dot_rows(a, b):
    return lax.dot_general(a, b, (((1,), (1,)), ((), ())), preferred_element_type=F32)


def two_part_dot(a, b):
    top = a.astype(BF16)
    rest = (a - top.astype(F32)).astype(BF16)
    both = dot(jnp.concatenate([top, rest], axis=0), b)
    return both[: a.shape[0]] + both[a.shape[0] :]


def fold(x):
    rows, cols = x.shape
    x = jnp.sum(x.reshape(rows // 8, 8, cols), axis=0)
    total = x[:, :128]
    for start in range(128, cols, 128):
        total = total + x[:, start : start + 128]
    return total


def whole_spec(shape):
    return pl.BlockSpec(shape, lambda i: (0,) * len(shape))


SCALARS = pl.BlockSpec(memory_space=pltpu.SMEM)
ANYWHERE = pl.BlockSpec(memory_space=pl.ANY)


def struct(shape, kind):
    return jax.ShapeDtypeStruct(shape, kind)


class Kernels:
    def __init__(self, zs, qs, hour_local, lat_local, lat_rows, lon_local):
        self.zs, self.qs = zs, qs
        self.al, self.lr, self.ol = lat_local, lat_rows, lon_local
        self.hl = hour_local
        self.hp = hour_local // HALVES
        self.hours, self.lats, self.lons = zs * hour_local, zs * lat_local, qs * lon_local
        self.cells = self.hp * lat_rows * self.lons
        self.token = None
        self.ease = 1

    def call(self, body, name, grid, out_shape, in_specs, out_specs, flops, moved, scratch=(), aliases={}):
        tokens = [] if self.token is None else [self.token]

        def run(*args):
            def whole(*refs):
                refs = list(refs)
                del refs[len(args) : len(args) + len(tokens)]
                place = len(args) + len(out_shape)
                token_ref = refs.pop(place)
                token_ref[...] = jnp.zeros_like(token_ref)
                body(*refs)

            out = pl.pallas_call(
                whole,
                name=name,
                grid=(grid,),
                out_shape=list(out_shape) + [struct((8, 128), F32)],
                in_specs=list(in_specs) + [ANYWHERE] * len(tokens),
                out_specs=list(out_specs) + [whole_spec((8, 128))],
                scratch_shapes=list(scratch),
                input_output_aliases=aliases,
                compiler_params=pltpu.CompilerParams(vmem_limit_bytes=VMEM),
                cost_estimate=pl.CostEstimate(flops=flops * self.ease, bytes_accessed=moved * self.ease, transcendentals=0),
            )(*args, *tokens)
            self.token = out[-1]
            return out[:-1]

        return run

    def after(self, x, *tokens):
        tokens = [self.token, *tokens]
        return pl.pallas_call(
            lambda *refs: None,
            name="after",
            out_shape=struct(x.shape, x.dtype),
            in_specs=[ANYWHERE] * (1 + len(tokens)),
            out_specs=ANYWHERE,
            input_output_aliases={0: 0},
            compiler_params=pltpu.CompilerParams(vmem_limit_bytes=VMEM),
            cost_estimate=pl.CostEstimate(flops=0, bytes_accessed=0, transcendentals=0),
        )(x, *tokens)

    def parts_specs(self, group):
        return [pl.BlockSpec((group, self.lr, self.ol), lambda i: (i, 0, 0))] * self.qs

    def parts_shape(self, kind, size=None):
        return [struct((size or self.hp, self.lr, self.ol), kind)] * self.qs

    def grid_spec(self, group, start=0):
        offset = start // group
        return pl.BlockSpec((group, self.lr, self.lons), lambda i: (i + offset, 0, 0))

    def hourly(self, noise, tables):
        zs, hp, al, ol, hours = self.zs, self.hp, self.al, self.ol, self.hours
        periods = noise.shape[3]

        def body(noise_ref, table_ref, *refs):
            outs, turned = refs[:HALVES], refs[HALVES]
            for start in range(0, GROUP, 4):
                part = noise_ref[:, start : start + 4].reshape(2, 4 * ol, periods)
                total = dot_rows(table_ref[0], part[0]) + dot_rows(table_ref[1], part[1])
                for k in range(4):
                    turned[pl.ds(start + k, hours, stride=GROUP), :] = total[:, k * ol : (k + 1) * ol]
            value = turned[...].reshape(zs, HALVES, hp, GROUP, ol).astype(BF16)
            for c in range(HALVES):
                outs[c][...] = value[:, c]

        return self.call(
            body, "hourly", al // GROUP, [struct((zs, hp, al, ol), BF16)] * HALVES,
            [pl.BlockSpec((2, GROUP, ol, periods), lambda i: (0, i, 0, 0)), whole_spec(tables.shape)],
            [pl.BlockSpec((zs, hp, GROUP, ol), lambda i: (0, 0, i, 0))] * HALVES,
            4 * hours * periods * al * ol, 2 * noise.size + 2 * hours * al * ol,
            [pltpu.VMEM((hours * GROUP, ol), F32)],
        )(noise, tables)

    def lat_up(self, start, size, g, lat, gain):
        zs, qs, lr, ol, lats = self.zs, self.qs, self.lr, self.ol, self.lats
        cells = size * lr * self.lons
        group = 8
        offset = start // group

        def body(gain_ref, g_ref, lat_ref, *outs):
            for h in range(0, group, 4):
                part = [g_ref[:, h + k].reshape(lats, ol) for k in range(4)]
                total = dot(lat_ref[...], jnp.concatenate(part, axis=1))
                code = encode(total * gain_ref[0])
                for k in range(4):
                    for d in range(qs):
                        outs[d][h + k] = code[d * lr : (d + 1) * lr, k * ol : (k + 1) * ol]

        return self.call(
            body, "lat_up", size // group, self.parts_shape(I16, size),
            [SCALARS, pl.BlockSpec((zs, group, self.al, ol), lambda i: (0, i + offset, 0, 0)), whole_spec(lat.shape)],
            self.parts_specs(group), 2 * cells * self.lats, 4 * cells,
        )(gain.reshape(1), g, lat)

    def residual(self, c, codes, back, lon_up, lon_down, observed, mask):
        qs, hp, lr, ol, lons = self.qs, self.hp, self.lr, self.ol, self.lons
        group = 8
        rows = group * lr

        def body(back_ref, *refs):
            arrived, (up_ref, down_ref, observed_ref, mask_ref) = refs[:qs], refs[qs : qs + 4]
            prior_ref, norm_ref, outs = refs[qs + 4], refs[qs + 5], refs[qs + 6 :]
            x = jnp.concatenate([decode(a[...].reshape(rows, ol)) for a in arrived], axis=1)
            prior = two_part_dot(x, up_ref[...]) * back_ref[0]
            prior_ref[...] = prior.reshape(group, lr, lons)
            seen = mask_ref[...].reshape(rows, lons).astype(F32)
            resid = seen * (observed_ref[...].reshape(rows, lons) - prior)

            @pl.when(pl.program_id(0) == 0)
            def _():
                norm_ref[...] = jnp.zeros_like(norm_ref)

            norm_ref[...] += fold(resid * resid)
            v = two_part_dot(resid, down_ref[...]).astype(BF16)
            for d in range(qs):
                outs[d][...] = v[:, d * ol : (d + 1) * ol].reshape(group, lr, ol)

        out = self.call(
            body, "residual", hp // group,
            [struct((hp, lr, lons), F32), struct((8, 128), F32)] + self.parts_shape(BF16),
            [SCALARS] + self.parts_specs(group) + [whole_spec(lon_up.shape)] * 2 + [self.grid_spec(group, c * hp)] * 2,
            [self.grid_spec(group), whole_spec((8, 128))] + self.parts_specs(group),
            8 * self.cells * lons, 16 * self.cells,
        )(back.reshape(1), *codes, lon_up, lon_down, observed, mask)
        return out[0], out[1], out[2:]

    def lat_down(self, c, v, lat_t, whole, earlier):
        zs, qs, hp, al, lr, ol, lats = self.zs, self.qs, self.hp, self.al, self.lr, self.ol, self.lats

        offset = c * (hp // GROUP) if whole else 0
        size = self.hl if whole else hp

        def body(*refs):
            sent, lat_ref, (out_ref, turned) = refs[:qs], refs[qs], refs[-2:]
            for start in range(0, GROUP, 4):
                part = [jnp.concatenate([s[start + k] for s in sent], axis=0) for k in range(4)]
                total = dot(lat_ref[...], jnp.concatenate(part, axis=1))
                for k in range(4):
                    turned[pl.ds(start + k, lats, stride=GROUP), :] = total[:, k * ol : (k + 1) * ol]
            out_ref[...] = turned[...].reshape(zs, al, GROUP, ol).astype(BF16)

        return self.call(
            body, "lat_down", hp // GROUP, [struct((zs, al, size, ol), BF16)],
            self.parts_specs(GROUP) + [whole_spec(lat_t.shape)] + [ANYWHERE] * len(earlier),
            [pl.BlockSpec((zs, al, GROUP, ol), lambda i: (0, 0, i + offset, 0))],
            2 * self.cells * lats, 4 * self.cells,
            [pltpu.VMEM((lats * GROUP, ol), F32)], {qs + 1: 0} if earlier else {},
        )(*v, lat_t, *earlier)

    def over_hours(self, xs, kern, pieces):
        zs, hl, al, ol, hours = self.zs, self.hl, self.al, self.ol, self.hours
        count = len(xs)

        def body(*refs):
            arrived, kern_ref, refs = refs[:count], refs[count], refs[count + 1 :]
            outs, (bend_ref, turned) = refs[: len(pieces)], refs[len(pieces) :]

            @pl.when(pl.program_id(0) == 0)
            def _():
                bend_ref[...] = jnp.zeros_like(bend_ref)

            for start in range(0, GROUP, 4):
                part = []
                for k in range(4):
                    rows = [x[z, start + k] for z in range(zs) for x in arrived]
                    part.append(jnp.concatenate(rows, axis=0))
                part = jnp.concatenate(part, axis=1)
                total = dot(kern_ref[0], part) + dot(kern_ref[1], part)
                bend_ref[...] += fold(total * part.astype(F32))
                for k in range(4):
                    turned[pl.ds(start + k, hours, stride=GROUP), :] = total[:, k * ol : (k + 1) * ol]
            value = turned[...].reshape(zs, hl, GROUP, ol).astype(BF16)
            for out_ref, (first, size) in zip(outs, pieces):
                out_ref[...] = value[:, first : first + size]

        out = self.call(
            body, "over_hours", al // GROUP, [struct((zs, size, al, ol), BF16) for _, size in pieces] + [struct((8, 128), F32)],
            [pl.BlockSpec((zs, GROUP, hl // count, ol), lambda i: (0, i, 0, 0))] * count + [whole_spec(kern.shape)],
            [pl.BlockSpec((zs, size, GROUP, ol), lambda i: (0, 0, i, 0)) for _, size in pieces]
            + [whole_spec((8, 128))],
            8 * self.cells * hours, 8 * self.cells,
            [pltpu.VMEM((hours * GROUP, ol), F32)],
        )(*xs, kern)
        return out[:-1], out[-1]

    def finish(self, s, first, size, codes, back, step, lon_up, prior, observed, mask, earlier):
        qs, hp, lr, ol, lons = self.qs, self.hp, self.lr, self.ol, self.lons
        cells = size * lr * lons
        group = 8
        rows = group * lr

        def body(scalar_ref, *refs):
            arrived, (up_ref, prior_ref, observed_ref, mask_ref) = refs[:qs], refs[qs : qs + 4]
            posterior_ref, next_ref = refs[-2:]
            x = jnp.concatenate([decode(a[...].reshape(rows, ol)) for a in arrived], axis=1)
            scaled = two_part_dot(x, up_ref[...]) * scalar_ref[0]
            prior = prior_ref[...].reshape(rows, lons)
            seen = mask_ref[...].reshape(rows, lons).astype(F32)
            resid = seen * (observed_ref[...].reshape(rows, lons) - prior)
            shape = (1, group, lr, lons)
            posterior_ref[...] = (prior + scaled).reshape(shape)
            next_ref[...] = (resid - seen * scaled - scalar_ref[1] * resid).reshape(shape)

        full = struct((2, self.hl, lr, lons), F32)
        offset = first // group
        out_spec = pl.BlockSpec((1, group, lr, lons), lambda i: (s, i + offset, 0, 0))
        count = 1 + qs + 4
        return self.call(
            body, "finish", size // group, [full, full],
            [SCALARS] + self.parts_specs(group) + [whole_spec(lon_up.shape), self.grid_spec(group, first % hp)]
            + [self.grid_spec(group, first)] * 2 + [ANYWHERE] * len(earlier),
            [out_spec, out_spec], 4 * cells * lons, 22 * cells,
            aliases={count + i: i for i in range(len(earlier))},
        )(jnp.stack([back * step, NOISE_VAR * step]), *codes, lon_up, prior, observed, mask, *earlier)

    def joined(self, earlier):
        return tuple(earlier)


class Plain(Kernels):
    def after(self, x, *tokens):
        return x

    def hourly(self, noise, tables):
        h = jnp.einsum("cyxk,cjk->jyx", noise, tables, preferred_element_type=F32).astype(BF16)
        h = h.reshape(self.zs, HALVES, self.hp, self.al, self.ol)
        return [h[:, c] for c in range(HALVES)]

    def lat_up(self, start, size, g, lat, gain):
        g = g[:, start : start + size]
        split = lat.reshape(self.qs, self.lr, self.zs, self.al)
        x = encode(jnp.einsum("qlzy,zhyx->qhlx", split, g, preferred_element_type=F32) * gain)
        return [x[d] for d in range(self.qs)]

    def up(self, codes, lon_up):
        x = jnp.concatenate([decode(c) for c in codes], axis=2)
        return jnp.einsum("hlx,xo->hlo", x, lon_up.astype(F32), precision=HIGH)

    def residual(self, c, codes, back, lon_up, lon_down, observed, mask):
        prior = self.up(codes, lon_up) * back
        here = slice(c * self.hp, (c + 1) * self.hp)
        resid = mask[here].astype(F32) * (observed[here] - prior)
        v = jnp.einsum("hlo,op->hlp", resid, lon_down.astype(F32), precision=HIGH).astype(BF16)
        return prior, jnp.sum(resid * resid), jnp.split(v, self.qs, axis=2)

    def lat_down(self, c, v, lat_t, whole, earlier):
        split = lat_t.reshape(self.zs, self.al, self.qs, self.lr)
        x = jnp.einsum("zyql,qhlx->zyhx", split, jnp.stack(v), preferred_element_type=F32)
        return (jnp.concatenate(list(earlier) + [x.astype(BF16)], axis=2),)

    def over_hours(self, xs, kern, pieces):
        x = jnp.concatenate(xs, axis=2)
        x = jnp.swapaxes(x, 0, 1).reshape(self.al, self.hours, self.ol).astype(F32)
        y = jnp.einsum("gk,ykx->gyx", kern.astype(F32).sum(0), x, precision=HIGH)
        bend = jnp.einsum("gyx,ygx->", y, x)
        y = y.astype(BF16).reshape(self.zs, self.hl, self.al, self.ol)
        return [y[:, first : first + size] for first, size in pieces], bend

    def finish(self, s, first, size, codes, back, step, lon_up, prior, observed, mask, earlier):
        scaled = self.up(codes, lon_up) * (back * step)
        here = slice(first, first + size)
        prior = prior[first % self.hp : first % self.hp + size]
        seen = mask[here].astype(F32)
        resid = seen * (observed[here] - prior)
        return tuple(earlier) + ((s, prior + scaled, resid - seen * scaled - NOISE_VAR * step * resid),)

    def joined(self, earlier):
        samples = [[e[1:] for e in earlier if e[0] == s] for s in range(2)]
        return tuple(jnp.stack([jnp.concatenate([e[i] for e in part]) for part in samples]) for i in range(2))


def swap_tm(x):
    return lax.all_to_all(x, "tm", split_axis=0, concat_axis=0, tiled=True)


def swap_lon(parts):
    count = len(parts)
    return [parts[0]] + [
        lax.ppermute(parts[d], "lon", [(i, i ^ d) for i in range(count)]) for d in range(1, count)
    ]


def add_over_tm(x, count):
    return sum([lax.ppermute(x, "tm", [(i, i ^ d) for i in range(count)]) for d in range(1, count)], x)


def add_over_lon(x, count):
    d = 1
    while d < count:
        x = x + lax.ppermute(x, "lon", [(i, i ^ d) for i in range(count)])
        d *= 2
    return x


def largest_norm(factor, axis):
    return jnp.sqrt(jnp.max(jnp.sum(jnp.square(factor.astype(F32)), axis=axis)))


def shards(noise, observed, mask, lat_factor, lon_factor, spectrum):
    _, lat_local, lon_local, periods = noise.shape
    hour_local, lat_rows, lon_count = observed.shape
    hours = periods // 2
    hour_part = hour_local // HALVES
    zs, qs = hours // hour_local, lon_count // lon_local
    lat_count = zs * lat_local
    fits = lon_local % 128 == 0 and lat_rows % 16 == 0
    fits = fits and lat_local % GROUP == 0 and hour_part % GROUP == 0
    stages = (Kernels if fits else Plain)(zs, qs, hour_local, lat_local, lat_rows, lon_local)
    order = lax.axis_index("lon") ^ jnp.arange(qs)

    powers = jnp.concatenate([spectrum, spectrum[1:-1][::-1]])
    amplitude = jnp.sqrt(powers / periods)
    turns = np.arange(hours)[:, None] * np.arange(periods) % periods * (2.0 * np.pi / periods)
    cosine_tab, sine_tab = jnp.asarray(np.cos(turns), F32), jnp.asarray(np.sin(turns), F32)
    table_cos = (cosine_tab * amplitude).astype(BF16)
    table_sin = (sine_tab * amplitude).astype(BF16)
    tables = (jnp.stack([table_cos, table_sin]), jnp.stack([-table_sin, table_cos]))

    def hour_kernel():
        scaled = powers / periods
        kern = jnp.dot(cosine_tab * scaled, cosine_tab.T, precision=EXACT) + jnp.dot(
            sine_tab * scaled, sine_tab.T, precision=EXACT
        )
        top = lax.reduce_precision(kern, 8, 7)
        return jnp.stack([top.astype(BF16), (kern - top).astype(BF16)])

    lon = lax.all_gather(lon_factor, "lon", axis=0, tiled=True)
    units = [(s, c) for s in range(2) for c in range(HALVES)]
    lon_down = jnp.concatenate(
        [lax.dynamic_slice_in_dim(lon, order[d] * lon_local, lon_local, axis=1) for d in range(qs)], axis=1
    )
    lon_up = lon_down.T
    first, second, third, fourth = units
    wait = stages.after
    arrived, waves = {}, {}
    for s in range(2):
        for c, part in enumerate(stages.hourly(noise, tables[s])):
            waves[s, c] = part
    arrived[first] = swap_tm(waves[first])
    arrived[second] = swap_tm(wait(waves[second], lon_up, lon_down))
    kern = hour_kernel()
    lat = jnp.take(lat_factor.reshape(qs, lat_rows, lat_count), order, axis=0)
    lat = lat.reshape(lat_count, lat_count)
    lat_t = lat.T
    lat_row_norm = largest_norm(lat_factor, 1)
    lon_col_norm = largest_norm(lon_down, 0)
    lat_norm = jnp.sqrt(jnp.sum(jnp.square(lat_factor.astype(F32))))
    first_gain = CODE_MAX / jnp.maximum(lat_row_norm * (lat_count**0.5 * HOURLY_MAX), 1e-30)
    codes, priors, norms, sent, down = {}, {}, {}, {}, {}

    def up(u):
        codes[u] = swap_lon(stages.lat_up(0, hour_part, arrived[u], lat, first_gain))

    def middle(u):
        priors[u], norms[u], v = stages.residual(
            u[1], codes[u], 1.0 / first_gain, lon_up, lon_down, observed, mask
        )
        sent[u] = swap_lon(v)

    def lower(u):
        down[u] = stages.lat_down(u[1], sent[u], lat_t, u[0] == 0, down[first] if u == second else ())

    stages.ease = 1
    up(first)
    middle(first)
    stages.ease = 4
    arrived[third] = swap_tm(wait(waves[third]))
    up(second)
    lower(first)
    arrived[fourth] = swap_tm(wait(waves[fourth]))
    middle(second)
    arrived[third] = wait(arrived[third], *sent[second][1:4])
    up(third)
    lower(second)
    down[second] = swap_tm(wait(down[second][0]))
    up(fourth)
    middle(third)
    lower(third)
    middle(fourth)
    down[third] = swap_tm(wait(down[third][0]))
    early, bending = stages.over_hours([down[second]], kern, [(0, hour_part), (hour_part, hour_part)])
    sums = [sum(jnp.sum(norms[u]) for u in units if u[0] == s) for s in range(2)] + [jnp.sum(bending)]
    lower(fourth)
    down[fourth] = swap_tm(down[fourth][0])
    early = list(early)
    early[0] = swap_tm(early[0])

    quarter = hour_part // 2
    pieces = [(0, hour_part), (hour_part, quarter), (hour_part + quarter, hour_part - quarter)]
    late, bending = stages.over_hours([down[third], down[fourth]], kern, pieces)
    sums.append(jnp.sum(bending))
    sums = add_over_tm(jnp.broadcast_to(jnp.stack(sums)[:, None], (4, 128)), zs)
    late = list(late)
    early[1] = swap_tm(wait(early[1], sums))
    sums = add_over_lon(sums, qs)[:, 0]
    gains, steps = [], []
    for s in range(2):
        norm_sq, bending = sums[s], sums[2 + s]
        bound = SPECTRUM_MAX * lat_row_norm * lat_norm * lon_col_norm * jnp.sqrt(norm_sq)
        gains.append(CODE_MAX / jnp.maximum(bound, 1e-30))
        steps.append(norm_sq / (bending + NOISE_VAR * norm_sq))
    earlier = ()

    stages.ease = 2

    def back(s, start, size, g):
        return swap_lon(stages.lat_up(start, size, g, lat, gains[s]))

    def end(s, start, size, codes):
        prior = priors[s, start // hour_part]
        return stages.finish(
            s, start, size, codes, 1.0 / gains[s], steps[s], lon_up, prior, observed, mask, earlier
        )

    quarters = pieces[1:]
    first_codes = back(0, 0, hour_part, early[0])
    late[0] = swap_tm(wait(late[0], *first_codes[1:]))
    second_codes = back(0, 0, hour_part, early[1])
    earlier = end(0, 0, hour_part, first_codes)
    late[1] = swap_tm(wait(late[1], *second_codes[1:]))
    third_codes = back(1, 0, hour_part, late[0])
    earlier = end(0, hour_part, hour_part, second_codes)
    late[2] = swap_tm(wait(late[2], *third_codes[1:6]))
    fourth_codes = back(1, 0, quarters[0][1], late[1])
    third_codes[0] = wait(third_codes[0], *fourth_codes[1:3])
    earlier = end(1, *pieces[0], third_codes)
    fifth_codes = back(1, 0, quarters[1][1], late[2])
    earlier = end(1, *quarters[0], fourth_codes)
    earlier = end(1, *quarters[1], fifth_codes)
    return stages.joined(earlier)


def solution(mesh):
    return jax.shard_map(
        shards,
        mesh=mesh,
        in_specs=(
            P(None, "tm", "lon", None),
            P("tm", "lon", None),
            P("tm", "lon", None),
            P(),
            P("lon", None),
            P(),
        ),
        out_specs=(P(None, "tm", "lon", None), P(None, "tm", "lon", None)),
        check_vma=False,
    )
```
